512 devices in a mesh: blk: 64 (over z, y), pslab: 8 (over x, core).
Axes of the slice: x: 4, y: 4, z: 16, core: 2. Of those that a mesh axis runs over, the one named last changes fastest.
Arguments:
- positions: float32 [64, 8, 64, 512], P('blk', 'pslab'), may hold values from 0 to 32768
- masses: bfloat16 [64, 8, 64, 512], P('blk', 'pslab'), may hold values from -6 to 6
- send_counts: int32 [64, 8, 64], P('blk', 'pslab'), may hold values from 0 to 512, as said below
- legendre: bfloat16 [16384, 64, 128], P(('pslab', 'blk')), may hold values from -0.75 to 0.75
- cycle_order: int32 [64], replicated, may hold values from 0 to 63, each once
- m_order: int32 [16384], replicated, may hold values from 0 to 16383, each once
Outputs:
- alm: float32 [16384, 2, 128], P(('pslab', 'blk'))
The draws below stay inside these ranges and needn't reach their ends.
Inputs may be any that keep to these rules, and one draw needn't show every extreme that they name: `send_counts`: live slots from one device to one owner are at most 512; in every draw one owner gets 512 from every device. `cycle_order`: a permutation of the cycles. `m_order`: a permutation of the orders.
All inputs are finite; a program needn't handle non-finite values.
Results may differ from the reference program's by a relative error of at most 0.004.
Values may be sent and summed in bfloat16 or wider, within the bound.
No kernel may reach another device: no remote copies, remote signals or barrier semaphores. Data moves between devices by JAX's collectives and lax.ppermute only.
A program may use at most 64 MiB of HBM per device.

```python
import math
import jax
import jax.numpy as jnp
from jax import lax

CYCLE_LEN = 32768
M = 16384
LMAX = 16384
LW = 128
CAP = 512
CYCLE_DEV = 1
CYCLES = 64
N_BLK = 64
N_PSLAB = 8


def draw_send_counts(key, part):
    key = jax.random.fold_in(key, 17)
    top_key, count_key, full_key = jax.random.split(key, 3)
    ceilings = jax.random.randint(top_key, (N_BLK,), CAP // 4, CAP + 1)
    lowest = ceilings // 2
    counts = jax.random.randint(count_key, (N_BLK, N_PSLAB, N_BLK), lowest[None, None, :], ceilings[None, None, :] + 1)
    busiest = jax.random.randint(full_key, (), 0, N_BLK)
    owners = jnp.arange(N_BLK)[None, None, :]
    return jnp.where(owners == busiest, CAP, counts).astype(jnp.int32)


def steps_of(stream_key, dims, cuts, smallest, largest):
    def one(dim, shards_of):
        steps = jax.random.uniform(jax.random.fold_in(jax.random.fold_in(stream_key, 6), dim), (shards_of,), jnp.float32, smallest / len(cuts), largest / len(cuts))
        return jnp.repeat(jnp.exp(steps), dims[dim] // shards_of).reshape((-1,) + (1,) * (len(dims) - dim - 1))

    factor_of = one(*cuts[0])
    for cut in cuts[1:]:
        factor_of = factor_of * one(*cut)
    return factor_of


def centred(stream_key, extent, deviation, bound, cuts=(), held_as=jnp.bfloat16):
    drawn = deviation * jax.random.normal(stream_key, extent, jnp.float32)
    if cuts:
        drawn = drawn * steps_of(stream_key, extent, cuts, -0.22, 0.18)
    return jnp.clip(drawn, -bound, bound).astype(held_as)


def setup_inputs(seed: int = 0) -> dict:
    arg_keys = jax.random.split(jax.random.key(seed), 7)
    positions = jnp.clip(32768.0 * jax.random.uniform(arg_keys[0], (N_BLK, N_PSLAB, N_BLK, CAP), jnp.float32) ** steps_of(arg_keys[0], (N_BLK, N_PSLAB, N_BLK, CAP), ((0, 64), (1, 8)), -0.2, 0.2), 0.0, 32768.0)
    masses = centred(arg_keys[1], (N_BLK, N_PSLAB, N_BLK, CAP), 1.0, 6.0, ((0, 64), (1, 8)))
    send_counts = draw_send_counts(jax.random.fold_in(arg_keys[6], 71), 0)
    legendre = centred(arg_keys[3], (M, CYCLES, LW), CYCLES ** -0.5, 0.75, ((0, 512),))
    cycle_order = jax.random.permutation(arg_keys[4], CYCLES).astype(jnp.int32)
    m_order = jax.random.permutation(arg_keys[5], M).astype(jnp.int32)
    return dict(positions=positions, masses=masses, send_counts=send_counts, legendre=legendre, cycle_order=cycle_order, m_order=m_order)


def rounded(values):
    return lax.optimization_barrier(values.astype(jnp.bfloat16)).astype(jnp.float32)


def reference(positions, masses, send_counts, legendre, cycle_order, m_order):
    total_pix = CYCLE_DEV * CYCLE_LEN
    slot_ids = jnp.arange(CAP, dtype=jnp.int32)
    live_rows = slot_ids[None, None, None, :] < send_counts[..., None]
    weights = jnp.where(live_rows, masses.astype(jnp.float32), jnp.float32(0.0))
    floored = jnp.floor(positions)
    fraction = positions - floored
    first_pix = floored.astype(jnp.int32) % total_pix
    within = first_pix % CYCLE_LEN
    second_pix = first_pix - within + (within + 1) % CYCLE_LEN
    owners = jnp.arange(N_BLK, dtype=jnp.int32)[None, None, :, None] * total_pix
    near_share = rounded(1.0 - fraction)
    far_share = rounded(fraction)
    cycle_maps = jnp.zeros((N_BLK * total_pix,), jnp.float32)
    cycle_maps = cycle_maps.at[(owners + first_pix).reshape(-1)].add((weights * near_share).reshape(-1))
    cycle_maps = cycle_maps.at[(owners + second_pix).reshape(-1)].add((weights * far_share).reshape(-1))
    cycle_maps = cycle_maps.reshape(N_BLK * CYCLE_DEV, CYCLE_LEN)
    spectrum = jnp.fft.rfft(cycle_maps, axis=1)[:, :M] * (CYCLE_LEN ** -0.5)
    stacked = jnp.stack([jnp.real(spectrum), jnp.imag(spectrum)], axis=1).astype(jnp.float32)
    ordered = jnp.take(stacked, m_order, axis=2).astype(jnp.bfloat16)
    by_cycle = jnp.zeros_like(ordered).at[cycle_order].set(ordered)
    cycles_total = N_BLK * CYCLE_DEV
    block_m = math.gcd(M, 512)
    tables = legendre.reshape(M // block_m, block_m, cycles_total, LW)
    columns = jnp.transpose(by_cycle, (2, 1, 0)).reshape(M // block_m, block_m, 2, cycles_total)

    def contract(operands):
        return jnp.einsum('igk,icg->ick', operands[0].astype(jnp.float32), operands[1].astype(jnp.float32))

    products = lax.map(contract, (tables, columns)).reshape(M, 2, LW)
    degrees = LMAX - LW + 1 + jnp.arange(LW, dtype=jnp.int32)
    return jnp.where(degrees[None, None, :] >= m_order[:, None, None], products, jnp.float32(0.0))
```

```python
import math

import jax
import jax.numpy as jnp
import numpy as np
from jax import lax
from jax.experimental import pallas as pl
from jax.experimental.pallas import tpu as pltpu
from jax.sharding import PartitionSpec as P

CYCLE_LEN = 32768
M = 16384
LMAX = 16384
LW = 128

LANES = 128
ROWS = CYCLE_LEN // LANES
UPPER = M // ROWS

F32 = jnp.float32
BF16 = jnp.bfloat16

NT = (((1,), (1,)), ((), ()))
NN = (((1,), (0,)), ((), ()))


def halves(table):
    high = table.astype(jnp.bfloat16)
    low = (table - high.astype(np.float64)).astype(jnp.bfloat16)
    return high, low


def split(values):
    high = values.astype(BF16)
    low = (values - high.astype(F32)).astype(BF16)
    return high, low


def tables():
    two_pi = 2.0 * math.pi
    rows = np.arange(ROWS)
    lanes = np.arange(LANES)
    upper = np.arange(UPPER)
    angle_one = (rows[:, None] * rows[None, :] % ROWS) * (two_pi / ROWS)
    one = np.concatenate([np.cos(angle_one), -np.sin(angle_one)], axis=0)
    twist = (rows[:, None] * lanes[None, :] % CYCLE_LEN) * (two_pi / CYCLE_LEN)
    angle_two = (upper[:, None] * lanes[None, :] % LANES) * (two_pi / LANES)
    cos_two, sin_two = np.cos(angle_two), np.sin(angle_two)
    two = np.concatenate(
        [
            np.concatenate([cos_two, sin_two], axis=1),
            np.concatenate([-sin_two, cos_two], axis=1),
        ],
        axis=0,
    ) * (CYCLE_LEN ** -0.5)
    return (
        *halves(one),
        np.cos(twist).astype(np.float32),
        np.sin(twist).astype(np.float32),
        *halves(two),
    )


def spread_row(values, row, count):
    tile = jnp.broadcast_to(values[row : row + 1, :], (16, LANES)).astype(BF16)
    return jnp.concatenate([tile] * (count // 16), axis=0)


def row_ids(count):
    return lax.broadcasted_iota(jnp.int32, (count, LANES), 0).astype(F32).astype(BF16)


def pack_kernel(positions_ref, masses_ref, counts_ref, out_ref):
    owners = out_ref.shape[0] // 8
    capacity = positions_ref.shape[1]
    slots = lax.broadcasted_iota(jnp.int32, (owners, LANES), 1)
    counts = counts_ref[...]
    for j in range(capacity // LANES):
        cols = slice(j * LANES, (j + 1) * LANES)
        out_ref[pl.ds(j, owners, stride=8), :] = positions_ref[:, cols]
        live = slots + j * LANES < counts
        out_ref[pl.ds(4 + j, owners, stride=8), :] = jnp.where(
            live, masses_ref[:, cols].astype(F32), 0.0
        )


def spectrum_kernel(
    got_ref, order_ref, one_h_ref, one_l_ref, cos_ref, sin_ref, two_h_ref, two_l_ref, out_ref, acc_ref
):
    sources = got_ref.shape[0]
    group = 4
    zero = jnp.zeros((), BF16)
    acc_ref[...] = jnp.zeros_like(acc_ref)

    def deposit(step, carry):
        ids = row_ids(ROWS)
        highs, lows = [], []
        for s in range(group):
            tile = got_ref[step * group + s]
            places, mass = tile[0:4], tile[4:8]
            floored = jnp.floor(places)
            fraction = places - floored
            pixel = floored.astype(jnp.int32) & (CYCLE_LEN - 1)
            high = (pixel >> 7).astype(F32)
            low = (pixel & (LANES - 1)).astype(F32)
            near = 1.0 - fraction
            for r in range(4):
                highs.append(
                    jnp.where(spread_row(high, r, ROWS) == ids, spread_row(mass, r, ROWS), zero)
                )
                hit = spread_row(low, r, LANES) == ids[:LANES]
                lows.append(
                    jnp.concatenate(
                        [
                            jnp.where(hit, spread_row(near, r, LANES), zero),
                            jnp.where(hit, spread_row(fraction, r, LANES), zero),
                        ],
                        axis=0,
                    )
                )
        acc_ref[...] += lax.dot_general(
            jnp.concatenate(highs, axis=1),
            jnp.concatenate(lows, axis=1),
            NT,
            preferred_element_type=F32,
        )
        return carry

    lax.fori_loop(0, sources // group, deposit, 0)

    near_map = acc_ref[:, :LANES]
    far_map = pltpu.roll(acc_ref[:, LANES:], 1, 1)
    far_next = pltpu.roll(far_map, 1, 0)
    lane = lax.broadcasted_iota(jnp.int32, (ROWS, LANES), 1)
    cycle = near_map + jnp.where(lane == 0, far_next, far_map)

    def dot(a, b, dims):
        return lax.dot_general(a, b, dims, preferred_element_type=F32)

    cycle_h, cycle_l = split(cycle)
    first = (
        dot(one_h_ref[...], cycle_l, NN)
        + dot(one_l_ref[...], cycle_h, NN)
        + dot(one_h_ref[...], cycle_h, NN)
    )
    real, imag = first[:ROWS], first[ROWS:]
    cos, sin = cos_ref[...], sin_ref[...]
    twisted = jnp.concatenate([real * cos + imag * sin, imag * cos - real * sin], axis=1)
    twisted_h, twisted_l = split(twisted)
    spectrum = (
        dot(two_h_ref[...], twisted_l, NT)
        + dot(two_l_ref[...], twisted_h, NT)
        + dot(two_h_ref[...], twisted_h, NT)
    )
    spectrum_halves = jnp.concatenate(split(spectrum), axis=0)
    slabs = out_ref.shape[0]
    steps_slab = order_ref.shape[0] // slabs // 8

    def pick(step, carry):
        ids = row_ids(ROWS)
        upper_ids = lax.broadcasted_iota(jnp.int32, (UPPER, LANES), 0)
        one = jnp.ones((), BF16)
        orders = order_ref[pl.ds(pl.multiple_of(step * 8, 8), 8), :]
        lower = (orders & (ROWS - 1)).astype(F32)
        upper = orders >> 8
        hits = [jnp.where(spread_row(lower, r, ROWS) == ids, one, zero) for r in range(8)]
        both = dot(spectrum_halves, jnp.concatenate(hits, axis=1), NN)
        picked = both[:LANES] + both[LANES:]
        reals, imags = [], []
        for r in range(8):
            cols = slice(r * LANES, (r + 1) * LANES)
            mine = jnp.broadcast_to(upper[r : r + 1, :], (UPPER, LANES)) == upper_ids
            reals.append(jnp.sum(jnp.where(mine, picked[:UPPER, cols], 0.0), axis=0, keepdims=True))
            imags.append(jnp.sum(jnp.where(mine, picked[UPPER:, cols], 0.0), axis=0, keepdims=True))
        slab = step // steps_slab
        first_row = pl.multiple_of(lax.rem(step, steps_slab) * 8, 8)
        out_ref[slab, pl.ds(first_row, 8), :] = jnp.concatenate(reals, axis=0)
        out_ref[slab, pl.ds(first_row + 16, 8), :] = jnp.concatenate(imags, axis=0)
        return carry

    lax.fori_loop(0, order_ref.shape[0] // 8, pick, 0)


def slab_sum_kernel(parts_ref, out_ref):
    total = parts_ref[0]
    for p in range(1, parts_ref.shape[0]):
        total = total + parts_ref[p]
    real, imag = total[:16], total[16:]
    lane = lax.broadcasted_iota(jnp.int32, (16, LANES), 1)
    for q in range(4):
        real_q = pltpu.roll(real, (LANES - 32 * q) % LANES, 1) if q else real
        imag_q = pltpu.roll(imag, (LANES - 32 * q + 32) % LANES, 1) if q != 1 else imag
        row = jnp.where(lane < 32, real_q, jnp.where(lane < 64, imag_q, 0.0))
        out_ref[pl.ds(q, 16, stride=4), :] = row


def product_kernel(got_ref, cycle_ref, order_ref, legendre_ref, out_ref):
    modes, cycles, width = legendre_ref.shape
    rows = 2 * modes
    turned = jnp.transpose(got_ref[...])[:rows].astype(BF16)
    place = lax.broadcasted_iota(jnp.int32, (cycles, cycles), 0) == jnp.broadcast_to(
        cycle_ref[...], (cycles, cycles)
    )
    sky = lax.dot_general(
        turned, jnp.where(place, 1.0, 0.0).astype(BF16), NT, preferred_element_type=F32
    )
    sky = jnp.concatenate([sky, sky], axis=1)
    lane = lax.broadcasted_iota(jnp.int32, (rows, 2 * cycles), 1)
    mode = lax.broadcasted_iota(jnp.int32, (rows, 2 * cycles), 0) & (modes - 1)
    owner = jnp.where(lane < cycles, 0, 1)
    blocks = [
        jnp.where(mode == owner + 2 * t, sky, 0.0).astype(BF16) for t in range(modes // 2)
    ]
    table = legendre_ref[...].reshape(modes * cycles, width)
    product = lax.dot_general(
        jnp.concatenate(blocks, axis=1), table, NN, preferred_element_type=F32
    )
    row_mode = lax.broadcasted_iota(jnp.int32, (rows, modes), 0) & (modes - 1)
    column = lax.broadcasted_iota(jnp.int32, (rows, modes), 1)
    order = jnp.sum(
        jnp.where(row_mode == column, jnp.broadcast_to(order_ref[...], (rows, modes)), 0).astype(F32),
        axis=1,
        keepdims=True,
    )
    degree = (LMAX - LW + 1 + lax.broadcasted_iota(jnp.int32, (rows, width), 1)).astype(F32)
    product = jnp.where(degree >= order, product, 0.0)
    out_ref[pl.ds(0, modes, stride=2), :] = product[:modes]
    out_ref[pl.ds(1, modes, stride=2), :] = product[modes:]


def kernel_call(kernel, out_shape, scratch=(), limit=32):
    return pl.pallas_call(
        kernel,
        out_shape=jax.ShapeDtypeStruct(out_shape, F32),
        scratch_shapes=list(scratch),
        compiler_params=pltpu.CompilerParams(vmem_limit_bytes=limit * 1024 * 1024),
    )


def local(positions, masses, send_counts, legendre, cycle_order, m_order):
    blk_count = lax.axis_size("blk")
    slab_count = lax.axis_size("pslab")
    capacity = positions.shape[-1]
    mode_count = legendre.shape[0]
    packed = kernel_call(pack_kernel, (blk_count * 8, LANES), limit=4)(
        positions.reshape(blk_count, capacity),
        masses.reshape(blk_count, capacity),
        send_counts.reshape(blk_count, 1),
    ).reshape(blk_count, 8, LANES)
    got = lax.all_to_all(packed, "blk", split_axis=0, concat_axis=0, tiled=True)
    parts = kernel_call(
        spectrum_kernel,
        (slab_count, 2 * M // slab_count // LANES, LANES),
        scratch=[pltpu.VMEM((ROWS, 2 * LANES), F32)],
    )(got, m_order.reshape(M // LANES, LANES), *tables())
    got_parts = lax.all_to_all(parts, "pslab", split_axis=0, concat_axis=0, tiled=True)
    own = kernel_call(slab_sum_kernel, (blk_count, LANES), limit=4)(got_parts)
    spread = lax.all_to_all(
        own.reshape(blk_count, 1, LANES), "blk", split_axis=0, concat_axis=0, tiled=True
    )
    slot_base = (lax.axis_index("pslab") * blk_count + lax.axis_index("blk")) * mode_count
    orders = lax.dynamic_slice_in_dim(m_order, slot_base, mode_count)
    alm = kernel_call(product_kernel, (2 * mode_count, LW), limit=8)(
        spread.reshape(blk_count, LANES),
        cycle_order.reshape(1, blk_count),
        orders.reshape(1, mode_count),
        legendre,
    )
    return alm.reshape(mode_count, 2, LW)


def solution(mesh):
    placed = (
        P("blk", "pslab", None, None),
        P("blk", "pslab", None, None),
        P("blk", "pslab", None),
        P(("pslab", "blk"), None, None),
        P(),
        P(),
    )
    return jax.shard_map(
        local,
        mesh=mesh,
        in_specs=placed,
        out_specs=P(("pslab", "blk"), None, None),
        check_vma=False,
    )
```

```python
import math

import jax
import jax.numpy as jnp
import numpy as np
from jax import lax
from jax.experimental import pallas as pl
from jax.experimental.pallas import tpu as pltpu
from jax.sharding import PartitionSpec as P

CYCLE_LEN = 32768
M = 16384
LMAX = 16384
LW = 128

LANES = 128
ROWS = CYCLE_LEN // LANES
UPPER = M // ROWS

F32 = jnp.float32
BF16 = jnp.bfloat16

NT = (((1,), (1,)), ((), ()))
NN = (((1,), (0,)), ((), ()))


def halves(table):
    high = table.astype(jnp.bfloat16)
    low = (table - high.astype(np.float64)).astype(jnp.bfloat16)
    return high, low


def split(values):
    high = values.astype(BF16)
    low = (values - high.astype(F32)).astype(BF16)
    return high, low


def tables():
    two_pi = 2.0 * math.pi
    rows = np.arange(ROWS)
    lanes = np.arange(LANES)
    upper = np.arange(UPPER)
    angle_one = (rows[:, None] * rows[None, :] % ROWS) * (two_pi / ROWS)
    one = np.concatenate([np.cos(angle_one), -np.sin(angle_one)], axis=0)
    twist = (rows[:, None] * lanes[None, :] % CYCLE_LEN) * (two_pi / CYCLE_LEN)
    angle_two = (upper[:, None] * lanes[None, :] % LANES) * (two_pi / LANES)
    cos_two, sin_two = np.cos(angle_two), np.sin(angle_two)
    two = np.concatenate(
        [
            np.concatenate([cos_two, sin_two], axis=1),
            np.concatenate([-sin_two, cos_two], axis=1),
        ],
        axis=0,
    ) * (CYCLE_LEN ** -0.5)
    return (
        *halves(one),
        np.cos(twist).astype(np.float32),
        np.sin(twist).astype(np.float32),
        *halves(two),
    )


def spread_row(values, row, count):
    tile = jnp.broadcast_to(values[row : row + 1, :], (16, LANES)).astype(BF16)
    return jnp.concatenate([tile] * (count // 16), axis=0)


def row_ids(count):
    return lax.broadcasted_iota(jnp.int32, (count, LANES), 0).astype(F32).astype(BF16)


def pack_kernel(positions_hbm, masses_hbm, counts_hbm, out_ref, positions_ref, masses_ref, counts_ref, sems):
    owners = out_ref.shape[0] // 8
    capacity = positions_ref.shape[1]
    copies = [
        pltpu.make_async_copy(positions_hbm, positions_ref, sems.at[0]),
        pltpu.make_async_copy(masses_hbm, masses_ref, sems.at[1]),
        pltpu.make_async_copy(counts_hbm, counts_ref, sems.at[2]),
    ]
    for copy in copies:
        copy.start()
    for copy in copies:
        copy.wait()
    slots = lax.broadcasted_iota(jnp.int32, (owners, LANES), 1)
    row = lax.broadcasted_iota(jnp.int32, (owners, owners), 0)
    column = lax.broadcasted_iota(jnp.int32, (owners, owners), 1)
    turned = jnp.where(row == column, jnp.broadcast_to(counts_ref[...], (owners, owners)), 0)
    counts = jnp.sum(turned.astype(F32), axis=1, keepdims=True).astype(jnp.int32)
    for j in range(capacity // LANES):
        cols = slice(j * LANES, (j + 1) * LANES)
        out_ref[pl.ds(j, owners, stride=8), :] = positions_ref[:, cols]
        live = slots + j * LANES < counts
        out_ref[pl.ds(4 + j, owners, stride=8), :] = jnp.where(
            live, masses_ref[:, cols].astype(F32), 0.0
        )


def spectrum_kernel(
    got_ref, order_ref, one_h_ref, one_l_ref, cos_ref, sin_ref, two_h_ref, two_l_ref, out_ref, acc_ref
):
    sources = got_ref.shape[0]
    group = 4
    zero = jnp.zeros((), BF16)
    acc_ref[...] = jnp.zeros_like(acc_ref)

    def deposit(step, carry):
        ids = row_ids(ROWS)
        highs, lows = [], []
        for s in range(group):
            tile = got_ref[step * group + s]
            places, mass = tile[0:4], tile[4:8]
            floored = jnp.floor(places)
            fraction = places - floored
            pixel = floored.astype(jnp.int32) & (CYCLE_LEN - 1)
            high = (pixel >> 7).astype(F32)
            low = (pixel & (LANES - 1)).astype(F32)
            near = 1.0 - fraction
            for r in range(4):
                highs.append(
                    jnp.where(spread_row(high, r, ROWS) == ids, spread_row(mass, r, ROWS), zero)
                )
                hit = spread_row(low, r, LANES) == ids[:LANES]
                lows.append(
                    jnp.concatenate(
                        [
                            jnp.where(hit, spread_row(near, r, LANES), zero),
                            jnp.where(hit, spread_row(fraction, r, LANES), zero),
                        ],
                        axis=0,
                    )
                )
        acc_ref[...] += lax.dot_general(
            jnp.concatenate(highs, axis=1),
            jnp.concatenate(lows, axis=1),
            NT,
            preferred_element_type=F32,
        )
        return carry

    lax.fori_loop(0, sources // group, deposit, 0)

    near_map = acc_ref[:, :LANES]
    far_map = pltpu.roll(acc_ref[:, LANES:], 1, 1)
    far_next = pltpu.roll(far_map, 1, 0)
    lane = lax.broadcasted_iota(jnp.int32, (ROWS, LANES), 1)
    cycle = near_map + jnp.where(lane == 0, far_next, far_map)

    def dot(a, b, dims):
        return lax.dot_general(a, b, dims, preferred_element_type=F32)

    cycle_h, cycle_l = split(cycle)
    first = (
        dot(one_h_ref[...], cycle_l, NN)
        + dot(one_l_ref[...], cycle_h, NN)
        + dot(one_h_ref[...], cycle_h, NN)
    )
    real, imag = first[:ROWS], first[ROWS:]
    cos, sin = cos_ref[...], sin_ref[...]
    twisted = jnp.concatenate([real * cos + imag * sin, imag * cos - real * sin], axis=1)
    twisted_h, twisted_l = split(twisted)
    spectrum = (
        dot(two_h_ref[...], twisted_l, NT)
        + dot(two_l_ref[...], twisted_h, NT)
        + dot(two_h_ref[...], twisted_h, NT)
    )
    spectrum_halves = jnp.concatenate(split(spectrum), axis=0)
    def pick(step, carry):
        ids = row_ids(ROWS)
        upper_ids = lax.broadcasted_iota(jnp.int32, (UPPER, LANES), 0)
        one = jnp.ones((), BF16)
        orders = order_ref[pl.ds(pl.multiple_of(step * 8, 8), 8), :]
        lower = (orders & (ROWS - 1)).astype(F32)
        upper = orders >> 8
        hits = [jnp.where(spread_row(lower, r, ROWS) == ids, one, zero) for r in range(8)]
        both = dot(spectrum_halves, jnp.concatenate(hits, axis=1), NN)
        picked = both[:LANES] + both[LANES:]
        reals, imags = [], []
        for r in range(8):
            cols = slice(r * LANES, (r + 1) * LANES)
            mine = jnp.broadcast_to(upper[r : r + 1, :], (UPPER, LANES)) == upper_ids
            reals.append(jnp.sum(jnp.where(mine, picked[:UPPER, cols], 0.0), axis=0, keepdims=True))
            imags.append(jnp.sum(jnp.where(mine, picked[UPPER:, cols], 0.0), axis=0, keepdims=True))
        for r in range(8):
            part = lax.rem(step, 2) * 4 + r // 2
            row = (r % 2) * 8 + step // 2
            out_ref[part, pl.ds(row, 1), :] = reals[r]
            out_ref[part, pl.ds(row + 16, 1), :] = imags[r]
        return carry

    lax.fori_loop(0, order_ref.shape[0] // 8, pick, 0)


def slab_sum_kernel(parts_ref, out_ref):
    total = parts_ref[0]
    for p in range(1, parts_ref.shape[0]):
        total = total + parts_ref[p]
    real, imag = total[:16], total[16:]
    lane = lax.broadcasted_iota(jnp.int32, (16, LANES), 1)
    for q in range(4):
        real_q = pltpu.roll(real, (LANES - 32 * q) % LANES, 1) if q else real
        imag_q = pltpu.roll(imag, (LANES - 32 * q + 32) % LANES, 1) if q != 1 else imag
        row = jnp.where(lane < 32, real_q, jnp.where(lane < 64, imag_q, 0.0))
        out_ref[pl.ds(8 * q, 8), :] = row[:8]
        out_ref[pl.ds(32 + 8 * q, 8), :] = row[8:]


def product_kernel(got_ref, side_ref, legendre_ref, out_ref):
    modes, cycles, width = legendre_ref.shape
    rows = 2 * modes
    turned = jnp.transpose(got_ref[...])[:rows].astype(BF16)
    place = lax.broadcasted_iota(jnp.int32, (cycles, cycles), 0) == jnp.broadcast_to(
        side_ref[:, :cycles], (cycles, cycles)
    )
    sky = lax.dot_general(
        turned, jnp.where(place, 1.0, 0.0).astype(BF16), NT, preferred_element_type=F32
    )
    sky = jnp.concatenate([sky, sky], axis=1)
    lane = lax.broadcasted_iota(jnp.int32, (rows, 2 * cycles), 1)
    mode = lax.broadcasted_iota(jnp.int32, (rows, 2 * cycles), 0) & (modes - 1)
    owner = jnp.where(lane < cycles, 0, 1)
    blocks = [
        jnp.where(mode == owner + 2 * t, sky, 0.0).astype(BF16) for t in range(modes // 2)
    ]
    table = legendre_ref[...].reshape(modes * cycles, width)
    product = lax.dot_general(
        jnp.concatenate(blocks, axis=1), table, NN, preferred_element_type=F32
    )
    row_mode = lax.broadcasted_iota(jnp.int32, (rows, LANES), 0) & (modes - 1)
    column = lax.broadcasted_iota(jnp.int32, (rows, LANES), 1) - cycles
    order = jnp.sum(
        jnp.where(row_mode == column, jnp.broadcast_to(side_ref[...], (rows, LANES)), 0).astype(F32),
        axis=1,
        keepdims=True,
    )
    degree = (LMAX - LW + 1 + lax.broadcasted_iota(jnp.int32, (rows, width), 1)).astype(F32)
    product = jnp.where(degree >= order, product, 0.0)
    out_ref[pl.ds(0, modes, stride=2), :] = product[:modes]
    out_ref[pl.ds(1, modes, stride=2), :] = product[modes:]


def kernel_call(kernel, out_shape, scratch=(), limit=32, **options):
    return pl.pallas_call(
        kernel,
        out_shape=jax.ShapeDtypeStruct(out_shape, F32),
        scratch_shapes=list(scratch),
        compiler_params=pltpu.CompilerParams(vmem_limit_bytes=limit * 1024 * 1024),
        **options,
    )


def pack_call(blk_count, capacity):
    return kernel_call(
        pack_kernel,
        (blk_count * 8, LANES),
        scratch=[
            pltpu.VMEM((blk_count, capacity), F32),
            pltpu.VMEM((blk_count, capacity), BF16),
            pltpu.VMEM((1, blk_count), jnp.int32),
            pltpu.SemaphoreType.DMA((3,)),
        ],
        limit=60,
        in_specs=[pl.BlockSpec(memory_space=pl.ANY)] * 3,
    )


def local(positions, masses, send_counts, legendre, cycle_order, m_order):
    near_axes = ("z_lo", "y", "pslab")
    blk_count = lax.axis_size(("z_hi", "z_lo", "y"))
    slab_count = lax.axis_size("z_hi")
    capacity = positions.shape[-1]
    mode_count = legendre.shape[0]
    packed = pack_call(blk_count, capacity)(
        positions.reshape(blk_count, capacity),
        masses.reshape(blk_count, capacity),
        send_counts.reshape(1, blk_count),
    ).reshape(blk_count, 8, LANES)
    got = lax.all_to_all(packed, near_axes, split_axis=0, concat_axis=0, tiled=True)
    parts = kernel_call(
        spectrum_kernel,
        (slab_count, 2 * M // slab_count // LANES, LANES),
        scratch=[pltpu.VMEM((ROWS, 2 * LANES), F32)],
    )(got, m_order.reshape(M // LANES, LANES), *tables())
    got_parts = lax.all_to_all(parts, "z_hi", split_axis=0, concat_axis=0, tiled=True)
    own = kernel_call(slab_sum_kernel, (blk_count, LANES), limit=4)(got_parts)
    spread = lax.all_to_all(
        own.reshape(blk_count, 1, LANES), near_axes, split_axis=0, concat_axis=0, tiled=True
    )
    slot_base = lax.axis_index(("pslab", "z_hi", "z_lo", "y")) * mode_count
    orders = lax.dynamic_slice_in_dim(m_order, slot_base, mode_count)
    side = jnp.concatenate([cycle_order, orders, jnp.zeros((LANES - blk_count - mode_count,), jnp.int32)])
    alm = kernel_call(product_kernel, (2 * mode_count, LW), limit=8)(
        spread.reshape(blk_count, LANES), side.reshape(1, LANES), legendre
    )
    return alm.reshape(mode_count, 2, LW)


def solution(mesh):
    cut = jax.sharding.Mesh(mesh.devices.reshape(8, 2, 4, 8), ("z_hi", "z_lo", "y", "pslab"))
    blk = ("z_hi", "z_lo", "y")
    placed = (
        P(blk, "pslab", None, None),
        P(blk, "pslab", None, None),
        P(blk, "pslab", None),
        P(("pslab",) + blk, None, None),
        P(),
        P(),
    )
    return jax.shard_map(
        local,
        mesh=cut,
        in_specs=placed,
        out_specs=P(("pslab",) + blk, None, None),
        check_vma=False,
    )
```

```python
import math

import jax
import jax.numpy as jnp
import numpy as np
from jax import lax
from jax.experimental import pallas as pl
from jax.experimental.pallas import tpu as pltpu
from jax.sharding import PartitionSpec as P

CYCLE_LEN = 32768
M = 16384
LMAX = 16384
LW = 128

LANES = 128
ROWS = CYCLE_LEN // LANES
UPPER = M // ROWS

F32 = jnp.float32
BF16 = jnp.bfloat16

NT = (((1,), (1,)), ((), ()))
NN = (((1,), (0,)), ((), ()))


def halves(table):
    high = table.astype(jnp.bfloat16)
    low = (table - high.astype(np.float64)).astype(jnp.bfloat16)
    return high, low


def split(values):
    high = values.astype(BF16)
    low = (values - high.astype(F32)).astype(BF16)
    return high, low


def tables():
    two_pi = 2.0 * math.pi
    rows = np.arange(ROWS)
    lanes = np.arange(LANES)
    upper = np.arange(UPPER)
    angle_one = (rows[:, None] * rows[None, :] % ROWS) * (two_pi / ROWS)
    one = np.concatenate([np.cos(angle_one), -np.sin(angle_one)], axis=0)
    twist = (rows[:, None] * lanes[None, :] % CYCLE_LEN) * (two_pi / CYCLE_LEN)
    angle_two = (upper[:, None] * lanes[None, :] % LANES) * (two_pi / LANES)
    cos_two, sin_two = np.cos(angle_two), np.sin(angle_two)
    two = np.concatenate(
        [
            np.concatenate([cos_two, sin_two], axis=1),
            np.concatenate([-sin_two, cos_two], axis=1),
        ],
        axis=0,
    ) * (CYCLE_LEN ** -0.5)
    return (
        *halves(one),
        np.cos(twist).astype(np.float32),
        np.sin(twist).astype(np.float32),
        *halves(two),
    )


def spread_row(values, row, count):
    tile = jnp.broadcast_to(values[row : row + 1, :], (16, LANES)).astype(BF16)
    return jnp.concatenate([tile] * (count // 16), axis=0)


def row_ids(count):
    return lax.broadcasted_iota(jnp.int32, (count, LANES), 0).astype(F32).astype(BF16)


def pack_kernel(positions_hbm, masses_hbm, counts_hbm, out_ref, positions_ref, masses_ref, counts_ref, sems):
    owners = out_ref.shape[0] // 8
    capacity = positions_ref.shape[1]
    copies = [
        pltpu.make_async_copy(positions_hbm, positions_ref, sems.at[0]),
        pltpu.make_async_copy(masses_hbm, masses_ref, sems.at[1]),
        pltpu.make_async_copy(counts_hbm, counts_ref, sems.at[2]),
    ]
    for copy in copies:
        copy.start()
    for copy in copies:
        copy.wait()
    slots = lax.broadcasted_iota(jnp.int32, (owners, LANES), 1)
    row = lax.broadcasted_iota(jnp.int32, (owners, owners), 0)
    column = lax.broadcasted_iota(jnp.int32, (owners, owners), 1)
    turned = jnp.where(row == column, jnp.broadcast_to(counts_ref[...], (owners, owners)), 0)
    counts = jnp.sum(turned.astype(F32), axis=1, keepdims=True).astype(jnp.int32)
    for j in range(capacity // LANES):
        cols = slice(j * LANES, (j + 1) * LANES)
        out_ref[pl.ds(j, owners, stride=8), :] = positions_ref[:, cols]
        live = slots + j * LANES < counts
        out_ref[pl.ds(4 + j, owners, stride=8), :] = jnp.where(
            live, masses_ref[:, cols].astype(F32), 0.0
        )


def deposit_kernel(got_ref, acc_ref):
    sources = got_ref.shape[0]
    group = 4
    zero = jnp.zeros((), BF16)
    acc_ref[...] = jnp.zeros_like(acc_ref)

    def deposit(step, carry):
        ids = row_ids(ROWS)
        highs, lows = [], []
        for s in range(group):
            tile = got_ref[step * group + s]
            places, mass = tile[0:4], tile[4:8]
            floored = jnp.floor(places)
            fraction = places - floored
            pixel = floored.astype(jnp.int32) & (CYCLE_LEN - 1)
            high = (pixel >> 7).astype(F32)
            low = (pixel & (LANES - 1)).astype(F32)
            near = 1.0 - fraction
            for r in range(4):
                highs.append(
                    jnp.where(spread_row(high, r, ROWS) == ids, spread_row(mass, r, ROWS), zero)
                )
                hit = spread_row(low, r, LANES) == ids[:LANES]
                lows.append(
                    jnp.concatenate(
                        [
                            jnp.where(hit, spread_row(near, r, LANES), zero),
                            jnp.where(hit, spread_row(fraction, r, LANES), zero),
                        ],
                        axis=0,
                    )
                )
        acc_ref[...] += lax.dot_general(
            jnp.concatenate(highs, axis=1),
            jnp.concatenate(lows, axis=1),
            NT,
            preferred_element_type=F32,
        )
        return carry

    lax.fori_loop(0, sources // group, deposit, 0)


def spectrum_kernel(
    acc_ref, order_ref, one_h_ref, one_l_ref, cos_ref, sin_ref, two_h_ref, two_l_ref, *out_refs, z_hi=None
):
    near_map = acc_ref[:, :LANES]
    far_map = pltpu.roll(acc_ref[:, LANES:], 1, 1)
    far_next = pltpu.roll(far_map, 1, 0)
    lane = lax.broadcasted_iota(jnp.int32, (ROWS, LANES), 1)
    cycle = near_map + jnp.where(lane == 0, far_next, far_map)

    def dot(a, b, dims):
        return lax.dot_general(a, b, dims, preferred_element_type=F32)

    cycle_h, cycle_l = split(cycle)
    first = (
        dot(one_h_ref[...], cycle_l, NN)
        + dot(one_l_ref[...], cycle_h, NN)
        + dot(one_h_ref[...], cycle_h, NN)
    )
    real, imag = first[:ROWS], first[ROWS:]
    cos, sin = cos_ref[...], sin_ref[...]
    twisted = jnp.concatenate([real * cos + imag * sin, imag * cos - real * sin], axis=1)
    twisted_h, twisted_l = split(twisted)
    spectrum = (
        dot(two_h_ref[...], twisted_l, NT)
        + dot(two_l_ref[...], twisted_h, NT)
        + dot(two_h_ref[...], twisted_h, NT)
    )
    spectrum_halves = jnp.concatenate(split(spectrum), axis=0)
    zero, one = jnp.zeros((), BF16), jnp.ones((), BF16)
    ids = row_ids(ROWS)
    upper_ids = lax.broadcasted_iota(jnp.int32, (UPPER, LANES), 0)
    if z_hi is None:
        z_hi = lax.axis_index("z_hi")
    for k, out_ref in enumerate(out_refs):
        first_row = 2 * lax.rem(z_hi + k, len(out_refs))
        orders = jnp.concatenate(
            [order_ref[pl.ds(first_row + z_lo, 8, stride=16), :] for z_lo in range(2)], axis=0
        )
        lower = (orders & (ROWS - 1)).astype(F32)
        upper = orders >> 8
        hits = [jnp.where(spread_row(lower, r, ROWS) == ids, one, zero) for r in range(16)]
        both = dot(spectrum_halves, jnp.concatenate(hits, axis=1), NN)
        picked = both[:LANES] + both[LANES:]
        reals, imags = [], []
        for r in range(16):
            cols = slice(r * LANES, (r + 1) * LANES)
            mine = jnp.broadcast_to(upper[r : r + 1, :], (UPPER, LANES)) == upper_ids
            reals.append(jnp.sum(jnp.where(mine, picked[:UPPER, cols], 0.0), axis=0, keepdims=True))
            imags.append(jnp.sum(jnp.where(mine, picked[UPPER:, cols], 0.0), axis=0, keepdims=True))
        out_ref[...] = jnp.concatenate(reals + imags, axis=0).astype(BF16)


def slab_sum_kernel(*refs):
    *parts, out_ref = refs
    total = parts[0][...].astype(F32)
    for part in parts[1:]:
        total = total + part[...].astype(F32)
    real, imag = total[:16], total[16:]
    lane = lax.broadcasted_iota(jnp.int32, (16, LANES), 1)
    for q in range(4):
        real_q = pltpu.roll(real, (LANES - 32 * q) % LANES, 1) if q else real
        imag_q = pltpu.roll(imag, (LANES - 32 * q + 32) % LANES, 1) if q != 1 else imag
        row = jnp.where(lane < 32, real_q, jnp.where(lane < 64, imag_q, 0.0))
        out_ref[pl.ds(8 * q, 8), :] = row[:8]
        out_ref[pl.ds(32 + 8 * q, 8), :] = row[8:]


def product_kernel(got_ref, side_ref, legendre_ref, out_ref):
    modes, cycles, width = legendre_ref.shape
    rows = 2 * modes
    turned = jnp.transpose(got_ref[...])[:rows].astype(BF16)
    place = lax.broadcasted_iota(jnp.int32, (cycles, cycles), 0) == jnp.broadcast_to(
        side_ref[:, :cycles], (cycles, cycles)
    )
    sky = lax.dot_general(
        turned, jnp.where(place, 1.0, 0.0).astype(BF16), NT, preferred_element_type=F32
    )
    sky = jnp.concatenate([sky, sky], axis=1)
    lane = lax.broadcasted_iota(jnp.int32, (rows, 2 * cycles), 1)
    mode = lax.broadcasted_iota(jnp.int32, (rows, 2 * cycles), 0) & (modes - 1)
    owner = jnp.where(lane < cycles, 0, 1)
    blocks = [
        jnp.where(mode == owner + 2 * t, sky, 0.0).astype(BF16) for t in range(modes // 2)
    ]
    table = legendre_ref[...].reshape(modes * cycles, width)
    product = lax.dot_general(
        jnp.concatenate(blocks, axis=1), table, NN, preferred_element_type=F32
    )
    row_mode = lax.broadcasted_iota(jnp.int32, (rows, LANES), 0) & (modes - 1)
    column = lax.broadcasted_iota(jnp.int32, (rows, LANES), 1) - cycles
    order = jnp.sum(
        jnp.where(row_mode == column, jnp.broadcast_to(side_ref[...], (rows, LANES)), 0).astype(F32),
        axis=1,
        keepdims=True,
    )
    degree = (LMAX - LW + 1 + lax.broadcasted_iota(jnp.int32, (rows, width), 1)).astype(F32)
    product = jnp.where(degree >= order, product, 0.0)
    out_ref[pl.ds(0, modes, stride=2), :] = product[:modes]
    out_ref[pl.ds(1, modes, stride=2), :] = product[modes:]


def kernel_call(kernel, out_shape, scratch=(), limit=32, **options):
    return pl.pallas_call(
        kernel,
        out_shape=out_shape if isinstance(out_shape, list) else jax.ShapeDtypeStruct(out_shape, F32),
        scratch_shapes=list(scratch),
        compiler_params=pltpu.CompilerParams(vmem_limit_bytes=limit * 1024 * 1024),
        **options,
    )


def pack_call(blk_count, capacity):
    return kernel_call(
        pack_kernel,
        (blk_count * 8, LANES),
        scratch=[
            pltpu.VMEM((blk_count, capacity), F32),
            pltpu.VMEM((blk_count, capacity), BF16),
            pltpu.VMEM((1, blk_count), jnp.int32),
            pltpu.SemaphoreType.DMA((3,)),
        ],
        limit=60,
        in_specs=[pl.BlockSpec(memory_space=pl.ANY)] * 3,
    )


def local(positions, masses, send_counts, legendre, cycle_order, m_order):
    near_axes = ("z_lo", "y", "pslab")
    blk_count = lax.axis_size(("z_hi", "z_lo", "y"))
    slab_count = lax.axis_size("z_hi")
    capacity = positions.shape[-1]
    mode_count = legendre.shape[0]
    packed = pack_call(blk_count, capacity)(
        positions.reshape(blk_count, capacity),
        masses.reshape(blk_count, capacity),
        send_counts.reshape(1, blk_count),
    ).reshape(blk_count, 8, LANES)
    got = lax.all_to_all(packed, near_axes, split_axis=0, concat_axis=0, tiled=True)
    maps = kernel_call(deposit_kernel, (ROWS, 2 * LANES))(got)
    part = jax.ShapeDtypeStruct((2 * M // slab_count // LANES, LANES), BF16)
    parts = kernel_call(spectrum_kernel, [part] * slab_count)(
        maps, m_order.reshape(M // LANES, LANES), *tables()
    )
    got_parts = [
        lax.ppermute(parts[k], "z_hi", [(i, (i + k) % slab_count) for i in range(slab_count)])
        for k in range(1, slab_count)
    ]
    own = kernel_call(slab_sum_kernel, (blk_count, LANES), limit=4)(parts[0], *got_parts)
    spread = lax.all_to_all(
        own.reshape(blk_count, 1, LANES), near_axes, split_axis=0, concat_axis=0, tiled=True
    )
    slot_base = lax.axis_index(("pslab", "z_hi", "z_lo", "y")) * mode_count
    orders = lax.dynamic_slice_in_dim(m_order, slot_base, mode_count)
    side = jnp.concatenate([cycle_order, orders, jnp.zeros((LANES - blk_count - mode_count,), jnp.int32)])
    alm = kernel_call(product_kernel, (2 * mode_count, LW), limit=8)(
        spread.reshape(blk_count, LANES), side.reshape(1, LANES), legendre
    )
    return alm.reshape(mode_count, 2, LW)


def solution(mesh):
    cut = jax.sharding.Mesh(mesh.devices.reshape(8, 2, 4, 8), ("z_hi", "z_lo", "y", "pslab"))
    blk = ("z_hi", "z_lo", "y")
    placed = (
        P(blk, "pslab", None, None),
        P(blk, "pslab", None, None),
        P(blk, "pslab", None),
        P(("pslab",) + blk, None, None),
        P(),
        P(),
    )
    return jax.shard_map(
        local,
        mesh=cut,
        in_specs=placed,
        out_specs=P(("pslab",) + blk, None, None),
        check_vma=False,
    )
```

```python
import math

import jax
import jax.numpy as jnp
import numpy as np
from jax import lax
from jax.experimental import pallas as pl
from jax.experimental.pallas import tpu as pltpu
from jax.sharding import PartitionSpec as P

CYCLE_LEN = 32768
M = 16384
LMAX = 16384
LW = 128

LANES = 128
ROWS = CYCLE_LEN // LANES
UPPER = M // ROWS
SPILL = LANES + 16

F32 = jnp.float32
BF16 = jnp.bfloat16

NT = (((1,), (1,)), ((), ()))
NN = (((1,), (0,)), ((), ()))


def halves(table):
    high = table.astype(jnp.bfloat16)
    low = (table - high.astype(np.float64)).astype(jnp.bfloat16)
    return high, low


def split(values):
    high = values.astype(BF16)
    low = (values - high.astype(F32)).astype(BF16)
    return high, low


def tables():
    two_pi = 2.0 * math.pi
    rows = np.arange(ROWS)
    lanes = np.arange(LANES)
    upper = np.arange(UPPER)
    angle_one = (rows[:, None] * rows[None, :] % ROWS) * (two_pi / ROWS)
    one = np.concatenate([np.cos(angle_one), -np.sin(angle_one)], axis=0)
    twist = (rows[:, None] * lanes[None, :] % CYCLE_LEN) * (two_pi / CYCLE_LEN)
    angle_two = (upper[:, None] * lanes[None, :] % LANES) * (two_pi / LANES)
    cos_two, sin_two = np.cos(angle_two), np.sin(angle_two)
    two = np.concatenate(
        [
            np.concatenate([cos_two, sin_two], axis=1),
            np.concatenate([-sin_two, cos_two], axis=1),
        ],
        axis=0,
    ) * (CYCLE_LEN ** -0.5)
    return (
        *halves(one),
        np.cos(twist).astype(np.float32),
        np.sin(twist).astype(np.float32),
        *halves(two),
    )


def spread_row(values, row, count):
    tile = jnp.broadcast_to(values[row : row + 1, :], (16, LANES)).astype(BF16)
    return jnp.concatenate([tile] * (count // 16), axis=0)


def row_ids(count):
    return lax.broadcasted_iota(jnp.int32, (count, LANES), 0).astype(F32).astype(BF16)


def pack_kernel(positions_hbm, masses_hbm, counts_hbm, out_ref, positions_ref, masses_ref, counts_ref, sems):
    owners = out_ref.shape[0] // 8
    capacity = positions_ref.shape[1]
    copies = [
        pltpu.make_async_copy(positions_hbm, positions_ref, sems.at[0]),
        pltpu.make_async_copy(masses_hbm, masses_ref, sems.at[1]),
        pltpu.make_async_copy(counts_hbm, counts_ref, sems.at[2]),
    ]
    for copy in copies:
        copy.start()
    for copy in copies:
        copy.wait()
    slots = lax.broadcasted_iota(jnp.int32, (owners, LANES), 1)
    row = lax.broadcasted_iota(jnp.int32, (owners, owners), 0)
    column = lax.broadcasted_iota(jnp.int32, (owners, owners), 1)
    turned = jnp.where(row == column, jnp.broadcast_to(counts_ref[...], (owners, owners)), 0)
    counts = jnp.sum(turned.astype(F32), axis=1, keepdims=True).astype(jnp.int32)
    for j in range(capacity // LANES):
        cols = slice(j * LANES, (j + 1) * LANES)
        out_ref[pl.ds(j, owners, stride=8), :] = positions_ref[:, cols]
        live = slots + j * LANES < counts
        out_ref[pl.ds(4 + j, owners, stride=8), :] = jnp.where(
            live, masses_ref[:, cols].astype(F32), 0.0
        )


def deposit_kernel(got_ref, acc_ref):
    sources = got_ref.shape[0]
    group = 16
    zero = jnp.zeros((), BF16)
    acc_ref[...] = jnp.zeros_like(acc_ref)

    def deposit(step, carry):
        row_id = row_ids(ROWS)
        lane_id = row_ids(SPILL)
        highs, lows = [], []
        for s in range(group):
            tile = got_ref[step * group + s]
            places, mass = tile[0:4], tile[4:8]
            floored = jnp.floor(places)
            fraction = places - floored
            pixel = floored.astype(jnp.int32) & (CYCLE_LEN - 1)
            high = (pixel >> 7).astype(F32)
            low = (pixel & (LANES - 1)).astype(F32)
            near = 1.0 - fraction
            after = low + 1.0
            for r in range(4):
                highs.append(
                    jnp.where(spread_row(high, r, ROWS) == row_id, spread_row(mass, r, ROWS), zero)
                )
                far_part = jnp.where(
                    spread_row(after, r, SPILL) == lane_id, spread_row(fraction, r, SPILL), zero
                )
                near_part = jnp.where(
                    spread_row(low, r, LANES) == lane_id[:LANES],
                    spread_row(near, r, LANES),
                    far_part[:LANES],
                )
                lows.append(jnp.concatenate([near_part, far_part[LANES:]], axis=0))
        acc_ref[...] += lax.dot_general(
            jnp.concatenate(lows, axis=1),
            jnp.concatenate(highs, axis=1),
            NT,
            preferred_element_type=F32,
        )
        return carry

    lax.fori_loop(0, sources // group, deposit, 0)


def spectrum_kernel(
    acc_ref,
    order_ref,
    place_ref,
    one_h_ref,
    one_l_ref,
    cos_ref,
    sin_ref,
    two_h_ref,
    two_l_ref,
    out_ref,
    side_ref,
    block=None,
):
    if block is None:
        block = lax.axis_index(("pslab", "z_hi", "z_lo", "y"))
    own = jnp.broadcast_to(order_ref[pl.ds(block // 4, 1), :], side_ref.shape)
    own = pltpu.roll(own, lax.rem(LANES + UPPER - lax.rem(block, 4) * 32, LANES), 1)
    places = jnp.concatenate([place_ref[...], place_ref[...]], axis=1)
    side_lane = lax.broadcasted_iota(jnp.int32, side_ref.shape, 1)
    side_ref[...] = jnp.where(side_lane < place_ref.shape[1], places, own)

    spilled = pltpu.roll(acc_ref[LANES : LANES + 8, :], 1, 1)[:1]
    lane = lax.broadcasted_iota(jnp.int32, (LANES, ROWS), 0)
    cycle = acc_ref[:LANES, :] + jnp.where(lane == 0, spilled, 0.0)

    def dot(a, b, dims):
        return lax.dot_general(a, b, dims, preferred_element_type=F32)

    cycle_h, cycle_l = split(cycle)
    first = (
        dot(one_h_ref[...], cycle_l, NT)
        + dot(one_l_ref[...], cycle_h, NT)
        + dot(one_h_ref[...], cycle_h, NT)
    )
    real, imag = first[:ROWS], first[ROWS:]
    cos, sin = cos_ref[...], sin_ref[...]
    twisted = jnp.concatenate([real * cos + imag * sin, imag * cos - real * sin], axis=1)
    twisted_h, twisted_l = split(twisted)
    spectrum = (
        dot(two_h_ref[...], twisted_l, NT)
        + dot(two_l_ref[...], twisted_h, NT)
        + dot(two_h_ref[...], twisted_h, NT)
    )
    spectrum_halves = jnp.concatenate(split(spectrum), axis=0)
    zero, one = jnp.zeros((), BF16), jnp.ones((), BF16)
    ids = row_ids(ROWS)
    upper_ids = lax.broadcasted_iota(jnp.int32, (UPPER, LANES), 0)
    for k in range(out_ref.shape[0]):
        orders = jnp.concatenate(
            [order_ref[pl.ds(2 * k + z_lo, 8, stride=16), :] for z_lo in range(2)], axis=0
        )
        lower = (orders & (ROWS - 1)).astype(F32)
        upper = orders >> 8
        hits = [jnp.where(spread_row(lower, r, ROWS) == ids, one, zero) for r in range(16)]
        both = dot(spectrum_halves, jnp.concatenate(hits, axis=1), NN)
        picked = both[:LANES] + both[LANES:]
        reals, imags = [], []
        for r in range(16):
            cols = slice(r * LANES, (r + 1) * LANES)
            mine = jnp.broadcast_to(upper[r : r + 1, :], (UPPER, LANES)) == upper_ids
            reals.append(jnp.sum(jnp.where(mine, picked[:UPPER, cols], 0.0), axis=0, keepdims=True))
            imags.append(jnp.sum(jnp.where(mine, picked[UPPER:, cols], 0.0), axis=0, keepdims=True))
        out_ref[k] = jnp.concatenate(reals + imags, axis=0).astype(BF16)


def slab_sum_kernel(parts_ref, out_ref):
    total = parts_ref[0].astype(F32)
    for p in range(1, parts_ref.shape[0]):
        total = total + parts_ref[p].astype(F32)
    real, imag = total[:16], total[16:]
    lane = lax.broadcasted_iota(jnp.int32, (16, LANES), 1)
    for q in range(4):
        real_q = pltpu.roll(real, (LANES - 32 * q) % LANES, 1) if q else real
        imag_q = pltpu.roll(imag, (LANES - 32 * q + 32) % LANES, 1) if q != 1 else imag
        row = jnp.where(lane < 32, real_q, jnp.where(lane < 64, imag_q, 0.0))
        out_ref[pl.ds(8 * q, 8), :] = row[:8]
        out_ref[pl.ds(32 + 8 * q, 8), :] = row[8:]


def turn_kernel(in_ref, out_ref):
    for a in range(8):
        out_ref[pl.ds(8 * a, 8), :] = in_ref[pl.ds(a, 8, stride=8), :]


def product_kernel(got_ref, side_ref, legendre_ref, out_ref):
    modes, cycles, width = legendre_ref.shape
    rows = 2 * modes
    by_cycle = jnp.concatenate([got_ref[pl.ds(a, 8, stride=8), :] for a in range(8)], axis=0)
    turned = jnp.transpose(by_cycle)[:rows].astype(BF16)
    place = lax.broadcasted_iota(jnp.int32, (cycles, cycles), 0) == jnp.broadcast_to(
        side_ref[:1, :cycles], (cycles, cycles)
    )
    sky = lax.dot_general(
        turned, jnp.where(place, 1.0, 0.0).astype(BF16), NT, preferred_element_type=F32
    )
    sky = jnp.concatenate([sky, sky], axis=1)
    lane = lax.broadcasted_iota(jnp.int32, (rows, 2 * cycles), 1)
    mode = lax.broadcasted_iota(jnp.int32, (rows, 2 * cycles), 0) & (modes - 1)
    owner = jnp.where(lane < cycles, 0, 1)
    blocks = [
        jnp.where(mode == owner + 2 * t, sky, 0.0).astype(BF16) for t in range(modes // 2)
    ]
    table = legendre_ref[...].reshape(modes * cycles, width)
    product = lax.dot_general(
        jnp.concatenate(blocks, axis=1), table, NN, preferred_element_type=F32
    )
    row_mode = lax.broadcasted_iota(jnp.int32, (rows, LANES), 0) & (modes - 1)
    column = lax.broadcasted_iota(jnp.int32, (rows, LANES), 1) - cycles
    order = jnp.sum(
        jnp.where(row_mode == column, jnp.broadcast_to(side_ref[:1, :], (rows, LANES)), 0).astype(F32),
        axis=1,
        keepdims=True,
    )
    degree = (LMAX - LW + 1 + lax.broadcasted_iota(jnp.int32, (rows, width), 1)).astype(F32)
    product = jnp.where(degree >= order, product, 0.0)
    out_ref[pl.ds(0, modes, stride=2), :] = product[:modes]
    out_ref[pl.ds(1, modes, stride=2), :] = product[modes:]


def kernel_call(kernel, out_shape, dtype=F32, scratch=(), limit=32, **options):
    return pl.pallas_call(
        kernel,
        out_shape=jax.ShapeDtypeStruct(out_shape, dtype) if dtype else out_shape,
        scratch_shapes=list(scratch),
        compiler_params=pltpu.CompilerParams(vmem_limit_bytes=limit * 1024 * 1024),
        **options,
    )


def pack_call(blk_count, capacity):
    return kernel_call(
        pack_kernel,
        (blk_count * 8, LANES),
        scratch=[
            pltpu.VMEM((blk_count, capacity), F32),
            pltpu.VMEM((blk_count, capacity), BF16),
            pltpu.VMEM((1, blk_count), jnp.int32),
            pltpu.SemaphoreType.DMA((3,)),
        ],
        limit=60,
        in_specs=[pl.BlockSpec(memory_space=pl.ANY)] * 3,
    )


def local(positions, masses, send_counts, legendre, cycle_order, m_order):
    near_axes = ("z_lo", "y", "pslab")
    blk_count = lax.axis_size(("z_hi", "z_lo", "y"))
    slab_count = lax.axis_size("z_hi")
    capacity = positions.shape[-1]
    mode_count = legendre.shape[0]
    packed = pack_call(blk_count, capacity)(
        positions.reshape(blk_count, capacity),
        masses.reshape(blk_count, capacity),
        send_counts.reshape(1, blk_count),
    ).reshape(blk_count, 8, LANES)
    got = lax.all_to_all(packed, near_axes, split_axis=0, concat_axis=0, tiled=True)
    cycle = kernel_call(deposit_kernel, (SPILL, ROWS))(got)
    outs = [
        jax.ShapeDtypeStruct((slab_count, 2 * M // slab_count // LANES, LANES), BF16),
        jax.ShapeDtypeStruct((8, LANES), jnp.int32),
    ]
    parts, side = kernel_call(spectrum_kernel, outs, None)(
        cycle, m_order.reshape(M // LANES, LANES), cycle_order.reshape(1, blk_count), *tables()
    )
    got_parts = lax.all_to_all(parts, "z_hi", split_axis=0, concat_axis=0, tiled=True)
    own = kernel_call(slab_sum_kernel, (blk_count, LANES), limit=4)(got_parts)
    by_row = lax.all_to_all(
        own.reshape(8, 8, LANES), ("z_lo", "y"), split_axis=0, concat_axis=0, tiled=True
    )
    turned = kernel_call(turn_kernel, (blk_count, LANES), limit=4)(by_row.reshape(blk_count, LANES))
    spread = lax.all_to_all(
        turned.reshape(8, 8, LANES), "pslab", split_axis=0, concat_axis=0, tiled=True
    )
    alm = kernel_call(product_kernel, (2 * mode_count, LW), limit=8)(
        spread.reshape(blk_count, LANES), side, legendre
    )
    return alm.reshape(mode_count, 2, LW)


def solution(mesh):
    cut = jax.sharding.Mesh(mesh.devices.reshape(8, 2, 4, 8), ("z_hi", "z_lo", "y", "pslab"))
    blk = ("z_hi", "z_lo", "y")
    placed = (
        P(blk, "pslab", None, None),
        P(blk, "pslab", None, None),
        P(blk, "pslab", None),
        P(("pslab",) + blk, None, None),
        P(),
        P(),
    )
    return jax.shard_map(
        local,
        mesh=cut,
        in_specs=placed,
        out_specs=P(("pslab",) + blk, None, None),
        check_vma=False,
    )
```

```python
import math

import jax
import jax.numpy as jnp
import numpy as np
from jax import lax
from jax.experimental import pallas as pl
from jax.experimental.pallas import tpu as pltpu
from jax.sharding import PartitionSpec as P

CYCLE_LEN = 32768
M = 16384
LMAX = 16384
LW = 128

LANES = 128
ROWS = CYCLE_LEN // LANES
UPPER = M // ROWS
SPILL = LANES + 16

F32 = jnp.float32
BF16 = jnp.bfloat16

NT = (((1,), (1,)), ((), ()))
NN = (((1,), (0,)), ((), ()))


def halves(table):
    high = table.astype(jnp.bfloat16)
    low = (table - high.astype(np.float64)).astype(jnp.bfloat16)
    return high, low


def split(values):
    high = values.astype(BF16)
    low = (values - high.astype(F32)).astype(BF16)
    return high, low


def tables():
    two_pi = 2.0 * math.pi
    rows = np.arange(ROWS)
    lanes = np.arange(LANES)
    upper = np.arange(UPPER)
    angle_one = (rows[:, None] * rows[None, :] % ROWS) * (two_pi / ROWS)
    one = np.concatenate([np.cos(angle_one), -np.sin(angle_one)], axis=0)
    twist = (rows[:, None] * lanes[None, :] % CYCLE_LEN) * (two_pi / CYCLE_LEN)
    angle_two = (upper[:, None] * lanes[None, :] % LANES) * (two_pi / LANES)
    cos_two, sin_two = np.cos(angle_two), np.sin(angle_two)
    two = np.concatenate(
        [
            np.concatenate([cos_two, sin_two], axis=1),
            np.concatenate([-sin_two, cos_two], axis=1),
        ],
        axis=0,
    ) * (CYCLE_LEN ** -0.5)
    return (
        *halves(one),
        np.cos(twist).astype(np.float32),
        np.sin(twist).astype(np.float32),
        *halves(two),
    )


def spread_row(values, row, count):
    tile = jnp.broadcast_to(values[row : row + 1, :], (16, LANES)).astype(BF16)
    return jnp.concatenate([tile] * (count // 16), axis=0)


def row_ids(count):
    return lax.broadcasted_iota(jnp.int32, (count, LANES), 0).astype(F32).astype(BF16)


def pack_kernel(
    positions_hbm,
    masses_hbm,
    counts_hbm,
    places_hbm,
    orders_hbm,
    out_ref,
    side_ref,
    positions_ref,
    masses_ref,
    counts_ref,
    places_ref,
    orders_ref,
    sems,
    block=None,
):
    if block is None:
        block = lax.axis_index(("pslab", "z_hi", "z_lo", "y"))
    owners = out_ref.shape[0] // 8
    capacity = positions_ref.shape[1]
    order_rows = pl.ds(pl.multiple_of(block // 32 * 8, 8), 8)
    copies = [
        pltpu.make_async_copy(positions_hbm, positions_ref, sems.at[0]),
        pltpu.make_async_copy(masses_hbm, masses_ref, sems.at[1]),
        pltpu.make_async_copy(counts_hbm, counts_ref, sems.at[2]),
        pltpu.make_async_copy(places_hbm, places_ref, sems.at[3]),
        pltpu.make_async_copy(orders_hbm.at[order_rows, :], orders_ref, sems.at[4]),
    ]
    for copy in copies:
        copy.start()
    for copy in copies:
        copy.wait()
    own = jnp.broadcast_to(orders_ref[pl.ds(lax.rem(block // 4, 8), 1), :], side_ref.shape)
    own = pltpu.roll(own, lax.rem(LANES + owners - lax.rem(block, 4) * 32, LANES), 1)
    places = jnp.concatenate([places_ref[...], places_ref[...]], axis=1)
    side_lane = lax.broadcasted_iota(jnp.int32, side_ref.shape, 1)
    side_ref[...] = jnp.where(side_lane < owners, places, own)
    slots = lax.broadcasted_iota(jnp.int32, (owners, LANES), 1)
    row = lax.broadcasted_iota(jnp.int32, (owners, owners), 0)
    column = lax.broadcasted_iota(jnp.int32, (owners, owners), 1)
    turned = jnp.where(row == column, jnp.broadcast_to(counts_ref[...], (owners, owners)), 0)
    counts = jnp.sum(turned.astype(F32), axis=1, keepdims=True).astype(jnp.int32)
    for j in range(capacity // LANES):
        cols = slice(j * LANES, (j + 1) * LANES)
        out_ref[pl.ds(j, owners, stride=8), :] = positions_ref[:, cols]
        live = slots + j * LANES < counts
        out_ref[pl.ds(4 + j, owners, stride=8), :] = jnp.where(
            live, masses_ref[:, cols].astype(F32), 0.0
        )


def deposit_kernel(got_ref, acc_ref):
    sources = got_ref.shape[0]
    group = 16
    zero = jnp.zeros((), BF16)
    acc_ref[...] = jnp.zeros_like(acc_ref)

    def deposit(step, carry):
        row_id = row_ids(ROWS)
        lane_id = row_ids(SPILL)
        highs, lows = [], []
        for s in range(group):
            tile = got_ref[step * group + s]
            places, mass = tile[0:4], tile[4:8]
            floored = jnp.floor(places)
            fraction = places - floored
            pixel = floored.astype(jnp.int32) & (CYCLE_LEN - 1)
            high = (pixel >> 7).astype(F32)
            low = (pixel & (LANES - 1)).astype(F32)
            near = 1.0 - fraction
            after = low + 1.0
            for r in range(4):
                highs.append(
                    jnp.where(spread_row(high, r, ROWS) == row_id, spread_row(mass, r, ROWS), zero)
                )
                far_part = jnp.where(
                    spread_row(after, r, SPILL) == lane_id, spread_row(fraction, r, SPILL), zero
                )
                near_part = jnp.where(
                    spread_row(low, r, LANES) == lane_id[:LANES],
                    spread_row(near, r, LANES),
                    far_part[:LANES],
                )
                lows.append(jnp.concatenate([near_part, far_part[LANES:]], axis=0))
        acc_ref[...] += lax.dot_general(
            jnp.concatenate(highs, axis=1),
            jnp.concatenate(lows, axis=1),
            NT,
            preferred_element_type=F32,
        )
        return carry

    lax.fori_loop(0, sources // group, deposit, 0)


def spectrum_kernel(
    acc_ref, order_ref, one_h_ref, one_l_ref, cos_ref, sin_ref, two_h_ref, two_l_ref, out_ref
):
    spilled = pltpu.roll(acc_ref[:, LANES:], 1, 0)[:, :1]
    lane = lax.broadcasted_iota(jnp.int32, (ROWS, LANES), 1)
    cycle = acc_ref[:, :LANES] + jnp.where(lane == 0, spilled, 0.0)

    def dot(a, b, dims):
        return lax.dot_general(a, b, dims, preferred_element_type=F32)

    cycle_h, cycle_l = split(cycle)
    first = (
        dot(one_h_ref[...], cycle_l, NN)
        + dot(one_l_ref[...], cycle_h, NN)
        + dot(one_h_ref[...], cycle_h, NN)
    )
    real, imag = first[:ROWS], first[ROWS:]
    cos, sin = cos_ref[...], sin_ref[...]
    twisted = jnp.concatenate([real * cos + imag * sin, imag * cos - real * sin], axis=1)
    twisted_h, twisted_l = split(twisted)
    spectrum = (
        dot(two_h_ref[...], twisted_l, NT)
        + dot(two_l_ref[...], twisted_h, NT)
        + dot(two_h_ref[...], twisted_h, NT)
    )
    spectrum = spectrum.astype(BF16)
    zero, one = jnp.zeros((), BF16), jnp.ones((), BF16)
    ids = row_ids(ROWS)
    upper_ids = lax.broadcasted_iota(jnp.int32, (UPPER, LANES), 0)
    planes = out_ref.shape[0]
    for k in range(planes):
        orders = order_ref[pl.ds(k, 8, stride=planes), :]
        lower = (orders & (ROWS - 1)).astype(F32)
        upper = orders >> 8
        hits = [jnp.where(spread_row(lower, r, ROWS) == ids, one, zero) for r in range(8)]
        picked = dot(spectrum, jnp.concatenate(hits, axis=1), NN)
        reals, imags = [], []
        for r in range(8):
            cols = slice(r * LANES, (r + 1) * LANES)
            mine = jnp.broadcast_to(upper[r : r + 1, :], (UPPER, LANES)) == upper_ids
            reals.append(jnp.sum(jnp.where(mine, picked[:UPPER, cols], 0.0), axis=0, keepdims=True))
            imags.append(jnp.sum(jnp.where(mine, picked[UPPER:, cols], 0.0), axis=0, keepdims=True))
        out_ref[k] = jnp.concatenate(reals + imags, axis=0).astype(BF16)


def slab_sum_kernel(parts_ref, out_ref):
    z_count = parts_ref.shape[0]
    quarters = []
    for z_lo in range(2):
        total = parts_ref[z_lo].astype(F32)
        for z in range(z_lo + 2, z_count, 2):
            total = total + parts_ref[z].astype(F32)
        quarters += [total[:8], total[8:]]
    quarter = lax.broadcasted_iota(jnp.int32, (8, LANES), 1) // 32
    for y in range(4):
        row = jnp.zeros((8, LANES), F32)
        for n, values in enumerate(quarters):
            shift = (n - y) % 4 * 32
            row = jnp.where(quarter == n, pltpu.roll(values, shift, 1) if shift else values, row)
        out_ref[pl.ds(8 * y, 8), :] = row


def product_kernel(got_ref, side_ref, legendre_ref, out_ref):
    modes, cycles, width = legendre_ref.shape
    rows = 2 * modes
    turned = jnp.transpose(got_ref[...])
    turned = jnp.concatenate([turned[:rows], turned[rows:]], axis=1).astype(BF16)
    place = lax.broadcasted_iota(jnp.int32, (cycles, cycles), 0) == jnp.broadcast_to(
        side_ref[:1, :cycles], (cycles, cycles)
    )
    sky = lax.dot_general(
        turned, jnp.where(place, 1.0, 0.0).astype(BF16), NT, preferred_element_type=F32
    )
    sky = jnp.concatenate([sky, sky], axis=1)
    lane = lax.broadcasted_iota(jnp.int32, (rows, 2 * cycles), 1)
    mode = lax.broadcasted_iota(jnp.int32, (rows, 2 * cycles), 0) & (modes - 1)
    owner = jnp.where(lane < cycles, 0, 1)
    blocks = [
        jnp.where(mode == owner + 2 * t, sky, 0.0).astype(BF16) for t in range(modes // 2)
    ]
    table = legendre_ref[...].reshape(modes * cycles, width)
    product = lax.dot_general(
        jnp.concatenate(blocks, axis=1), table, NN, preferred_element_type=F32
    )
    row_mode = lax.broadcasted_iota(jnp.int32, (rows, LANES), 0) & (modes - 1)
    column = lax.broadcasted_iota(jnp.int32, (rows, LANES), 1) - cycles
    order = jnp.sum(
        jnp.where(row_mode == column, jnp.broadcast_to(side_ref[:1, :], (rows, LANES)), 0).astype(F32),
        axis=1,
        keepdims=True,
    )
    degree = (LMAX - LW + 1 + lax.broadcasted_iota(jnp.int32, (rows, width), 1)).astype(F32)
    product = jnp.where(degree >= order, product, 0.0)
    out_ref[pl.ds(0, modes, stride=2), :] = product[:modes]
    out_ref[pl.ds(1, modes, stride=2), :] = product[modes:]


def kernel_call(kernel, out_shape, dtype=F32, scratch=(), limit=32, **options):
    return pl.pallas_call(
        kernel,
        out_shape=jax.ShapeDtypeStruct(out_shape, dtype) if dtype else out_shape,
        scratch_shapes=list(scratch),
        compiler_params=pltpu.CompilerParams(vmem_limit_bytes=limit * 1024 * 1024),
        **options,
    )


def pack_call(owners, capacity, kernel=pack_kernel):
    outs = [
        jax.ShapeDtypeStruct((owners * 8, LANES), F32),
        jax.ShapeDtypeStruct((8, LANES), jnp.int32),
    ]
    return kernel_call(
        kernel,
        outs,
        None,
        scratch=[
            pltpu.VMEM((owners, capacity), F32),
            pltpu.VMEM((owners, capacity), BF16),
            pltpu.VMEM((1, owners), jnp.int32),
            pltpu.VMEM((1, owners), jnp.int32),
            pltpu.VMEM((8, LANES), jnp.int32),
            pltpu.SemaphoreType.DMA((5,)),
        ],
        limit=60,
        in_specs=[pl.BlockSpec(memory_space=pl.ANY)] * 5,
    )


def local(positions, masses, send_counts, legendre, cycle_order, m_order):
    cube = ("z_lo", "y", "pslab")
    plane = ("y", "pslab")
    cycles = cycle_order.shape[0]
    planes = 16
    capacity = positions.shape[-1]
    mode_count = legendre.shape[0]
    order_rows = m_order.reshape(M // LANES, LANES)
    packed, side = pack_call(cycles, capacity)(
        positions.reshape(cycles, capacity),
        masses.reshape(cycles, capacity),
        send_counts.reshape(1, cycles),
        cycle_order.reshape(1, cycles),
        order_rows,
    )
    got = lax.all_to_all(
        packed.reshape(cycles, 8, LANES), cube, split_axis=0, concat_axis=0, tiled=True
    )
    cycle = kernel_call(deposit_kernel, (ROWS, SPILL))(got)
    parts = kernel_call(spectrum_kernel, (planes, 2 * M // planes // LANES, LANES), BF16)(
        cycle, order_rows, *tables()
    )
    got_parts = lax.all_to_all(parts, ("z_hi", "z_lo"), split_axis=0, concat_axis=0, tiled=True)
    own = kernel_call(slab_sum_kernel, (cycles // 2, LANES), limit=4)(got_parts)
    spread = lax.all_to_all(
        own.reshape(cycles // 2, 1, LANES), plane, split_axis=0, concat_axis=0, tiled=True
    )
    alm = kernel_call(product_kernel, (2 * mode_count, LW), limit=8)(
        spread.reshape(cycles // 2, LANES), side, legendre
    )
    return alm.reshape(mode_count, 2, LW)


def solution(mesh):
    cut = jax.sharding.Mesh(mesh.devices.reshape(8, 2, 4, 8), ("z_hi", "z_lo", "y", "pslab"))
    blk = ("z_hi", "z_lo", "y")
    placed = (
        P(blk, "pslab", None, None),
        P(blk, "pslab", None, None),
        P(blk, "pslab", None),
        P(("pslab",) + blk, None, None),
        P(),
        P(),
    )
    return jax.shard_map(
        local,
        mesh=cut,
        in_specs=placed,
        out_specs=P(("pslab",) + blk, None, None),
        check_vma=False,
    )
```

```python
import math

import jax
import jax.numpy as jnp
import numpy as np
from jax import lax
from jax.experimental import pallas as pl
from jax.experimental.pallas import tpu as pltpu
from jax.sharding import PartitionSpec as P

CYCLE_LEN = 32768
M = 16384
LMAX = 16384
LW = 128

LANES = 128
ROWS = CYCLE_LEN // LANES
UPPER = M // ROWS
TILES = 8
SUB = LANES // TILES
COLUMNS = (TILES + 1) * SUB

F32 = jnp.float32
BF16 = jnp.bfloat16

NT = (((1,), (1,)), ((), ()))
NN = (((1,), (0,)), ((), ()))


def halves(table):
    high = table.astype(jnp.bfloat16)
    low = (table - high.astype(np.float64)).astype(jnp.bfloat16)
    return high, low


def split(values):
    high = values.astype(BF16)
    low = (values - high.astype(F32)).astype(BF16)
    return high, low


def tables():
    two_pi = 2.0 * math.pi
    rows = np.arange(ROWS)
    lanes = np.arange(LANES)
    lanes = TILES * (lanes % SUB) + lanes // SUB
    upper = np.arange(UPPER)
    angle_one = (rows[:, None] * rows[None, :] % ROWS) * (two_pi / ROWS)
    one = np.concatenate([np.cos(angle_one), -np.sin(angle_one)], axis=0)
    twist = (rows[:, None] * lanes[None, :] % CYCLE_LEN) * (two_pi / CYCLE_LEN)
    angle_two = (upper[:, None] * lanes[None, :] % LANES) * (two_pi / LANES)
    cos_two, sin_two = np.cos(angle_two), np.sin(angle_two)
    two = np.concatenate(
        [
            np.concatenate([cos_two, sin_two], axis=1),
            np.concatenate([-sin_two, cos_two], axis=1),
        ],
        axis=0,
    ) * (CYCLE_LEN ** -0.5)
    return (
        *halves(one),
        np.cos(twist).astype(np.float32),
        np.sin(twist).astype(np.float32),
        *halves(two),
    )


def spread_row(values, row, count):
    tile = jnp.broadcast_to(values[row : row + 1, :], (16, LANES)).astype(BF16)
    return jnp.concatenate([tile] * (count // 16), axis=0)


def row_ids(count):
    return lax.broadcasted_iota(jnp.int32, (count, LANES), 0).astype(F32).astype(BF16)


def pack_kernel(
    positions_hbm,
    masses_hbm,
    counts_hbm,
    places_hbm,
    orders_hbm,
    out_ref,
    side_ref,
    positions_ref,
    masses_ref,
    counts_ref,
    places_ref,
    orders_ref,
    sems,
    block=None,
):
    if block is None:
        block = lax.axis_index(("pslab", "z_hi", "z_lo", "y"))
    owners = out_ref.shape[0] // 8
    capacity = positions_ref.shape[1]
    order_rows = pl.ds(pl.multiple_of(block // 32 * 8, 8), 8)
    copies = [
        pltpu.make_async_copy(positions_hbm, positions_ref, sems.at[0]),
        pltpu.make_async_copy(masses_hbm, masses_ref, sems.at[1]),
        pltpu.make_async_copy(counts_hbm, counts_ref, sems.at[2]),
        pltpu.make_async_copy(places_hbm, places_ref, sems.at[3]),
        pltpu.make_async_copy(orders_hbm.at[order_rows, :], orders_ref, sems.at[4]),
    ]
    for copy in copies:
        copy.start()
    for copy in copies:
        copy.wait()
    own = jnp.broadcast_to(orders_ref[pl.ds(lax.rem(block // 4, 8), 1), :], side_ref.shape)
    own = pltpu.roll(own, lax.rem(LANES + owners - lax.rem(block, 4) * 32, LANES), 1)
    places = jnp.concatenate([places_ref[...], places_ref[...]], axis=1)
    side_lane = lax.broadcasted_iota(jnp.int32, side_ref.shape, 1)
    side_ref[...] = jnp.where(side_lane < owners, places, own)
    slots = lax.broadcasted_iota(jnp.int32, (owners, LANES), 1)
    row = lax.broadcasted_iota(jnp.int32, (owners, owners), 0)
    column = lax.broadcasted_iota(jnp.int32, (owners, owners), 1)
    turned = jnp.where(row == column, jnp.broadcast_to(counts_ref[...], (owners, owners)), 0)
    counts = jnp.sum(turned.astype(F32), axis=1, keepdims=True).astype(jnp.int32)
    for j in range(capacity // LANES):
        cols = slice(j * LANES, (j + 1) * LANES)
        out_ref[pl.ds(j, owners, stride=8), :] = positions_ref[:, cols]
        live = slots + j * LANES < counts
        out_ref[pl.ds(4 + j, owners, stride=8), :] = jnp.where(
            live, masses_ref[:, cols].astype(F32), 0.0
        )


def deposit_kernel(got_ref, acc_ref, group=64):
    sources = got_ref.shape[0]
    zero = jnp.zeros((), BF16)

    def deposit(first):
        row_id = row_ids(ROWS)
        sub_id = lax.broadcasted_iota(jnp.int32, (SUB, LANES), 0)
        lane_ids = [(TILES * sub_id + t).astype(F32).astype(BF16) for t in range(TILES)]
        highs, lows = [], []
        for s in range(group):
            tile = got_ref[first + s]
            places, mass = tile[0:4], tile[4:8]
            floored = jnp.floor(places)
            fraction = places - floored
            pixel = floored.astype(jnp.int32) & (CYCLE_LEN - 1)
            high = (pixel >> 7).astype(F32)
            low = (pixel & (LANES - 1)).astype(F32)
            near = 1.0 - fraction
            for r in range(4):
                highs.append(
                    jnp.where(spread_row(high, r, ROWS) == row_id, spread_row(mass, r, ROWS), zero)
                )
                low_r, near_r, far_r = (spread_row(v, r, SUB) for v in (low, near, fraction))
                hits = [low_r == lane_id for lane_id in lane_ids]
                tiles = [jnp.where(hits[0], near_r, zero)]
                for t in range(1, TILES):
                    tiles.append(jnp.where(hits[t], near_r, jnp.where(hits[t - 1], far_r, zero)))
                tiles.append(jnp.where(hits[-1], far_r, zero))
                lows.append(jnp.concatenate(tiles, axis=0))
        return lax.dot_general(
            jnp.concatenate(highs, axis=1),
            jnp.concatenate(lows, axis=1),
            NT,
            preferred_element_type=F32,
        )

    acc_ref[:, LANES:] = jnp.zeros((ROWS, LANES), F32)
    if group == sources:
        acc_ref[:, :COLUMNS] = deposit(0)
    else:
        acc_ref[:, :LANES] = jnp.zeros((ROWS, LANES), F32)

        def step(n, carry):
            acc_ref[:, :COLUMNS] += deposit(n * group)
            return carry

        lax.fori_loop(0, sources // group, step, 0)


def hits_kernel(order_ref, out_ref):
    zero, one = jnp.zeros((), BF16), jnp.ones((), BF16)
    planes = order_ref.shape[0] // 8

    def step(k, carry):
        ids = row_ids(ROWS)
        lower = (order_ref[pl.ds(k, 8, stride=planes), :] & (ROWS - 1)).astype(F32)
        hits = [jnp.where(spread_row(lower, r, ROWS) == ids, one, zero) for r in range(8)]
        out_ref[k] = jnp.concatenate(hits, axis=1)
        return carry

    lax.fori_loop(0, planes, step, 0)


def spectrum_kernel(
    acc_ref, order_ref, hits_ref, one_h_ref, one_l_ref, cos_ref, sin_ref, two_h_ref, two_l_ref, out_ref
):
    beyond = acc_ref[:, LANES:]
    column = lax.broadcasted_iota(jnp.int32, (ROWS, LANES), 1)
    next_row = pltpu.roll(pltpu.roll(beyond, LANES - SUB + 1, 1), 1, 0)
    cycle = acc_ref[:, :LANES] + jnp.where(
        column == 0, next_row, jnp.where(column < SUB, pltpu.roll(beyond, 1, 1), 0.0)
    )

    def dot(a, b, dims):
        return lax.dot_general(a, b, dims, preferred_element_type=F32)

    cycle_h, cycle_l = split(cycle)
    first = (
        dot(one_h_ref[...], cycle_l, NN)
        + dot(one_l_ref[...], cycle_h, NN)
        + dot(one_h_ref[...], cycle_h, NN)
    )
    real, imag = first[:ROWS], first[ROWS:]
    cos, sin = cos_ref[...], sin_ref[...]
    twisted = jnp.concatenate([real * cos + imag * sin, imag * cos - real * sin], axis=1)
    twisted_h, twisted_l = split(twisted)
    spectrum = (
        dot(two_h_ref[...], twisted_l, NT)
        + dot(two_l_ref[...], twisted_h, NT)
        + dot(two_h_ref[...], twisted_h, NT)
    )
    spectrum = spectrum.astype(BF16)
    upper_ids = lax.broadcasted_iota(jnp.int32, (UPPER, LANES), 0)
    planes = out_ref.shape[0]
    for k in range(planes):
        upper = order_ref[pl.ds(k, 8, stride=planes), :] >> 8
        picked = dot(spectrum, hits_ref[k], NN)
        reals, imags = [], []
        for r in range(8):
            cols = slice(r * LANES, (r + 1) * LANES)
            mine = jnp.broadcast_to(upper[r : r + 1, :], (UPPER, LANES)) == upper_ids
            reals.append(jnp.sum(jnp.where(mine, picked[:UPPER, cols], 0.0), axis=0, keepdims=True))
            imags.append(jnp.sum(jnp.where(mine, picked[UPPER:, cols], 0.0), axis=0, keepdims=True))
        out_ref[k] = jnp.concatenate(reals + imags, axis=0).astype(BF16)


def slab_sum_kernel(parts_ref, out_ref):
    z_count = parts_ref.shape[0]
    quarters = []
    for z_lo in range(2):
        total = parts_ref[z_lo].astype(F32)
        for z in range(z_lo + 2, z_count, 2):
            total = total + parts_ref[z].astype(F32)
        quarters += [total[:8], total[8:]]
    quarter = lax.broadcasted_iota(jnp.int32, (8, LANES), 1) // 32
    for y in range(4):
        row = jnp.zeros((8, LANES), F32)
        for n, values in enumerate(quarters):
            shift = (n - y) % 4 * 32
            row = jnp.where(quarter == n, pltpu.roll(values, shift, 1) if shift else values, row)
        out_ref[pl.ds(8 * y, 8), :] = row


def product_kernel(got_ref, side_ref, legendre_ref, out_ref):
    modes, cycles, width = legendre_ref.shape
    rows = 2 * modes
    turned = jnp.transpose(got_ref[...])
    turned = jnp.concatenate([turned[:rows], turned[rows:]], axis=1).astype(BF16)
    place = lax.broadcasted_iota(jnp.int32, (cycles, cycles), 0) == jnp.broadcast_to(
        side_ref[:1, :cycles], (cycles, cycles)
    )
    sky = lax.dot_general(
        turned, jnp.where(place, 1.0, 0.0).astype(BF16), NT, preferred_element_type=F32
    )
    sky = jnp.concatenate([sky, sky], axis=1)
    lane = lax.broadcasted_iota(jnp.int32, (rows, 2 * cycles), 1)
    mode = lax.broadcasted_iota(jnp.int32, (rows, 2 * cycles), 0) & (modes - 1)
    owner = jnp.where(lane < cycles, 0, 1)
    blocks = [
        jnp.where(mode == owner + 2 * t, sky, 0.0).astype(BF16) for t in range(modes // 2)
    ]
    table = legendre_ref[...].reshape(modes * cycles, width)
    product = lax.dot_general(
        jnp.concatenate(blocks, axis=1), table, NN, preferred_element_type=F32
    )
    row_mode = lax.broadcasted_iota(jnp.int32, (rows, LANES), 0) & (modes - 1)
    column = lax.broadcasted_iota(jnp.int32, (rows, LANES), 1) - cycles
    order = jnp.sum(
        jnp.where(row_mode == column, jnp.broadcast_to(side_ref[:1, :], (rows, LANES)), 0).astype(F32),
        axis=1,
        keepdims=True,
    )
    degree = (LMAX - LW + 1 + lax.broadcasted_iota(jnp.int32, (rows, width), 1)).astype(F32)
    product = jnp.where(degree >= order, product, 0.0)
    out_ref[pl.ds(0, modes, stride=2), :] = product[:modes]
    out_ref[pl.ds(1, modes, stride=2), :] = product[modes:]


def kernel_call(kernel, out_shape, dtype=F32, scratch=(), limit=32, **options):
    return pl.pallas_call(
        kernel,
        out_shape=jax.ShapeDtypeStruct(out_shape, dtype) if dtype else out_shape,
        scratch_shapes=list(scratch),
        compiler_params=pltpu.CompilerParams(vmem_limit_bytes=limit * 1024 * 1024),
        **options,
    )


def pack_call(owners, capacity, kernel=pack_kernel):
    outs = [
        jax.ShapeDtypeStruct((owners * 8, LANES), F32),
        jax.ShapeDtypeStruct((8, LANES), jnp.int32),
    ]
    return kernel_call(
        kernel,
        outs,
        None,
        scratch=[
            pltpu.VMEM((owners, capacity), F32),
            pltpu.VMEM((owners, capacity), BF16),
            pltpu.VMEM((1, owners), jnp.int32),
            pltpu.VMEM((1, owners), jnp.int32),
            pltpu.VMEM((8, LANES), jnp.int32),
            pltpu.SemaphoreType.DMA((5,)),
        ],
        limit=60,
        in_specs=[pl.BlockSpec(memory_space=pl.ANY)] * 5,
    )


def local(positions, masses, send_counts, legendre, cycle_order, m_order):
    cube = ("z_lo", "y", "pslab")
    plane = ("y", "pslab")
    cycles = cycle_order.shape[0]
    planes = 16
    capacity = positions.shape[-1]
    mode_count = legendre.shape[0]
    order_rows = m_order.reshape(M // LANES, LANES)
    packed, side = pack_call(cycles, capacity)(
        positions.reshape(cycles, capacity),
        masses.reshape(cycles, capacity),
        send_counts.reshape(1, cycles),
        cycle_order.reshape(1, cycles),
        order_rows,
    )
    got = lax.all_to_all(
        packed.reshape(cycles, 8, LANES), cube, split_axis=0, concat_axis=0, tiled=True
    )
    hits = kernel_call(
        hits_kernel,
        (planes, ROWS, M // planes),
        BF16,
        limit=16,
        cost_estimate=pl.CostEstimate(flops=0, transcendentals=0, bytes_accessed=2 * ROWS * M),
    )(order_rows)
    cycle = kernel_call(deposit_kernel, (ROWS, 2 * LANES))(got)
    parts = kernel_call(spectrum_kernel, (planes, 2 * M // planes // LANES, LANES), BF16)(
        cycle, order_rows, hits, *tables()
    )
    got_parts = lax.all_to_all(parts, ("z_hi", "z_lo"), split_axis=0, concat_axis=0, tiled=True)
    own = kernel_call(slab_sum_kernel, (cycles // 2, LANES), limit=4)(got_parts)
    spread = lax.all_to_all(
        own.reshape(cycles // 2, 1, LANES), plane, split_axis=0, concat_axis=0, tiled=True
    )
    alm = kernel_call(product_kernel, (2 * mode_count, LW), limit=8)(
        spread.reshape(cycles // 2, LANES), side, legendre
    )
    return alm.reshape(mode_count, 2, LW)


def solution(mesh):
    cut = jax.sharding.Mesh(mesh.devices.reshape(8, 2, 4, 8), ("z_hi", "z_lo", "y", "pslab"))
    blk = ("z_hi", "z_lo", "y")
    placed = (
        P(blk, "pslab", None, None),
        P(blk, "pslab", None, None),
        P(blk, "pslab", None),
        P(("pslab",) + blk, None, None),
        P(),
        P(),
    )
    return jax.shard_map(
        local,
        mesh=cut,
        in_specs=placed,
        out_specs=P(("pslab",) + blk, None, None),
        check_vma=False,
    )
```

```python
import math

import jax
import jax.numpy as jnp
import numpy as np
from jax import lax
from jax.experimental import pallas as pl
from jax.experimental.pallas import tpu as pltpu
from jax.sharding import PartitionSpec as P

CYCLE_LEN = 32768
M = 16384
LMAX = 16384
LW = 128

LANES = 128
ROWS = CYCLE_LEN // LANES
UPPER = M // ROWS
TILES = 8
SUB = LANES // TILES
COLUMNS = (TILES + 1) * SUB

F32 = jnp.float32
BF16 = jnp.bfloat16

NT = (((1,), (1,)), ((), ()))
NN = (((1,), (0,)), ((), ()))


def halves(table):
    high = table.astype(jnp.bfloat16)
    low = (table - high.astype(np.float64)).astype(jnp.bfloat16)
    return high, low


def split(values):
    high = values.astype(BF16)
    low = (values - high.astype(F32)).astype(BF16)
    return high, low


def tables():
    two_pi = 2.0 * math.pi
    rows = np.arange(ROWS)
    lanes = np.arange(LANES)
    lanes = TILES * (lanes % SUB) + lanes // SUB
    upper = np.arange(UPPER)
    angle_one = (rows[:, None] * rows[None, :] % ROWS) * (two_pi / ROWS)
    one = np.concatenate([np.cos(angle_one), -np.sin(angle_one)], axis=0)
    twist = (rows[:, None] * lanes[None, :] % CYCLE_LEN) * (two_pi / CYCLE_LEN)
    angle_two = (upper[:, None] * lanes[None, :] % LANES) * (two_pi / LANES)
    cos_two, sin_two = np.cos(angle_two), np.sin(angle_two)
    two = np.concatenate(
        [
            np.concatenate([cos_two, sin_two], axis=1),
            np.concatenate([-sin_two, cos_two], axis=1),
        ],
        axis=0,
    ) * (CYCLE_LEN ** -0.5)
    return (
        *halves(one),
        np.cos(twist).astype(np.float32),
        np.sin(twist).astype(np.float32),
        *halves(two),
    )


def spread_row(values, row, count):
    tile = jnp.broadcast_to(values[row : row + 1, :], (16, LANES)).astype(BF16)
    return jnp.concatenate([tile] * (count // 16), axis=0)


def row_ids(count):
    return lax.broadcasted_iota(jnp.int32, (count, LANES), 0).astype(F32).astype(BF16)


def pack_kernel(
    positions_hbm,
    masses_hbm,
    counts_hbm,
    places_hbm,
    orders_hbm,
    out_ref,
    side_ref,
    positions_ref,
    masses_ref,
    counts_ref,
    places_ref,
    orders_ref,
    sems,
    block=None,
):
    if block is None:
        block = lax.axis_index(("pslab", "z_hi", "z_lo", "y"))
    owners = out_ref.shape[0] // 8
    capacity = positions_ref.shape[1]
    order_rows = pl.ds(pl.multiple_of(block // 32 * 8, 8), 8)
    copies = [
        pltpu.make_async_copy(positions_hbm, positions_ref, sems.at[0]),
        pltpu.make_async_copy(masses_hbm, masses_ref, sems.at[1]),
        pltpu.make_async_copy(counts_hbm, counts_ref, sems.at[2]),
        pltpu.make_async_copy(places_hbm, places_ref, sems.at[3]),
        pltpu.make_async_copy(orders_hbm.at[order_rows, :], orders_ref, sems.at[4]),
    ]
    for copy in copies:
        copy.start()
    for copy in copies:
        copy.wait()
    own = jnp.broadcast_to(orders_ref[pl.ds(lax.rem(block // 4, 8), 1), :], side_ref.shape)
    own = pltpu.roll(own, lax.rem(LANES + owners - lax.rem(block, 4) * 32, LANES), 1)
    places = jnp.concatenate([places_ref[...], places_ref[...]], axis=1)
    side_lane = lax.broadcasted_iota(jnp.int32, side_ref.shape, 1)
    side_ref[...] = jnp.where(side_lane < owners, places, own)
    slots = lax.broadcasted_iota(jnp.int32, (owners, LANES), 1)
    row = lax.broadcasted_iota(jnp.int32, (owners, owners), 0)
    column = lax.broadcasted_iota(jnp.int32, (owners, owners), 1)
    turned = jnp.where(row == column, jnp.broadcast_to(counts_ref[...], (owners, owners)), 0)
    counts = jnp.sum(turned.astype(F32), axis=1, keepdims=True).astype(jnp.int32)
    for j in range(capacity // LANES):
        cols = slice(j * LANES, (j + 1) * LANES)
        out_ref[pl.ds(j, owners, stride=8), :] = positions_ref[:, cols]
        live = slots + j * LANES < counts
        out_ref[pl.ds(4 + j, owners, stride=8), :] = jnp.where(
            live, masses_ref[:, cols].astype(F32), 0.0
        )


def deposit_kernel(got_ref, acc_ref, group=64):
    sources = got_ref.shape[0]
    zero = jnp.zeros((), BF16)

    def deposit(first):
        row_id = row_ids(ROWS)
        sub_id = lax.broadcasted_iota(jnp.int32, (SUB, LANES), 0)
        lane_ids = [(TILES * sub_id + t).astype(F32).astype(BF16) for t in range(TILES)]
        highs, lows = [], []
        for s in range(group):
            tile = got_ref[first + s]
            places, mass = tile[0:4], tile[4:8]
            floored = jnp.floor(places)
            fraction = places - floored
            pixel = floored.astype(jnp.int32) & (CYCLE_LEN - 1)
            high = (pixel >> 7).astype(F32)
            low = (pixel & (LANES - 1)).astype(F32)
            near = 1.0 - fraction
            for r in range(4):
                highs.append(
                    jnp.where(spread_row(high, r, ROWS) == row_id, spread_row(mass, r, ROWS), zero)
                )
                low_r, near_r, far_r = (spread_row(v, r, SUB) for v in (low, near, fraction))
                hits = [low_r == lane_id for lane_id in lane_ids]
                tiles = [jnp.where(hits[0], near_r, zero)]
                for t in range(1, TILES):
                    tiles.append(jnp.where(hits[t], near_r, jnp.where(hits[t - 1], far_r, zero)))
                tiles.append(jnp.where(hits[-1], far_r, zero))
                lows.append(jnp.concatenate(tiles, axis=0))
        return lax.dot_general(
            jnp.concatenate(highs, axis=1),
            jnp.concatenate(lows, axis=1),
            NT,
            preferred_element_type=F32,
        )

    acc_ref[:, LANES:] = jnp.zeros((ROWS, LANES), F32)
    if group == sources:
        acc_ref[:, :COLUMNS] = deposit(0)
    else:
        acc_ref[:, :LANES] = jnp.zeros((ROWS, LANES), F32)

        def step(n, carry):
            acc_ref[:, :COLUMNS] += deposit(n * group)
            return carry

        lax.fori_loop(0, sources // group, step, 0)


def hits_kernel(order_ref, out_ref):
    zero, one = jnp.zeros((), BF16), jnp.ones((), BF16)
    planes = order_ref.shape[0] // 8

    def step(k, carry):
        ids = row_ids(ROWS)
        lower = (order_ref[pl.ds(k, 8, stride=planes), :] & (ROWS - 1)).astype(F32)
        hits = [jnp.where(spread_row(lower, r, ROWS) == ids, one, zero) for r in range(8)]
        out_ref[k] = jnp.concatenate(hits, axis=1)
        return carry

    lax.fori_loop(0, planes, step, 0)


def spectrum_kernel(
    acc_ref, order_ref, hits_ref, one_h_ref, one_l_ref, cos_ref, sin_ref, two_h_ref, two_l_ref, out_ref
):
    beyond = acc_ref[:, LANES:]
    column = lax.broadcasted_iota(jnp.int32, (ROWS, LANES), 1)
    next_row = pltpu.roll(pltpu.roll(beyond, LANES - SUB + 1, 1), 1, 0)
    cycle = acc_ref[:, :LANES] + jnp.where(
        column == 0, next_row, jnp.where(column < SUB, pltpu.roll(beyond, 1, 1), 0.0)
    )

    def dot(a, b, dims):
        return lax.dot_general(a, b, dims, preferred_element_type=F32)

    cycle_h, cycle_l = split(cycle)
    first = (
        dot(one_h_ref[...], cycle_l, NN)
        + dot(one_l_ref[...], cycle_h, NN)
        + dot(one_h_ref[...], cycle_h, NN)
    )
    real, imag = first[:ROWS], first[ROWS:]
    cos, sin = cos_ref[...], sin_ref[...]
    twisted = jnp.concatenate([real * cos + imag * sin, imag * cos - real * sin], axis=1)
    twisted_h, twisted_l = split(twisted)
    spectrum = (
        dot(two_h_ref[...], twisted_l, NT)
        + dot(two_l_ref[...], twisted_h, NT)
        + dot(two_h_ref[...], twisted_h, NT)
    )
    spectrum = spectrum.astype(BF16)
    summing = jnp.where(
        lax.broadcasted_iota(jnp.int32, (16, LANES), 1) // 8
        == lax.broadcasted_iota(jnp.int32, (16, LANES), 0),
        1.0,
        0.0,
    ).astype(BF16)
    sublane = lax.broadcasted_iota(jnp.int32, (8, LANES), 0)
    planes = out_ref.shape[0]
    for k in range(planes):
        uppers = order_ref[pl.ds(k, 8, stride=planes), :] >> 8
        picked = dot(spectrum, hits_ref[k], NN)
        reals, imags = [], []
        for r in range(8):
            upper = jnp.broadcast_to(uppers[r : r + 1, :], (8, LANES))
            bits = [(upper & bit) != 0 for bit in (8, 16, 32)]
            mine = (upper & 7) == sublane
            for first, found in ((0, reals), (UPPER, imags)):
                eights = [
                    picked[first + 8 * n : first + 8 * n + 8, r * LANES : (r + 1) * LANES]
                    for n in range(UPPER // 8)
                ]
                for bit in bits:
                    eights = [jnp.where(bit, b, a) for a, b in zip(eights[::2], eights[1::2])]
                found.append(jnp.where(mine, eights[0], 0.0))
        found = jnp.concatenate(reals + imags, axis=0).astype(BF16)
        out_ref[k] = dot(summing, found, NN).astype(BF16)


def slab_sum_kernel(parts_ref, out_ref):
    z_count = parts_ref.shape[0]
    quarters = []
    for z_lo in range(2):
        total = parts_ref[z_lo].astype(F32)
        for z in range(z_lo + 2, z_count, 2):
            total = total + parts_ref[z].astype(F32)
        quarters += [total[:8], total[8:]]
    quarter = lax.broadcasted_iota(jnp.int32, (8, LANES), 1) // 32
    for y in range(4):
        row = jnp.zeros((8, LANES), F32)
        for n, values in enumerate(quarters):
            shift = (n - y) % 4 * 32
            row = jnp.where(quarter == n, pltpu.roll(values, shift, 1) if shift else values, row)
        out_ref[pl.ds(8 * y, 8), :] = row


def product_kernel(got_ref, side_ref, legendre_ref, out_ref):
    modes, cycles, width = legendre_ref.shape
    rows = 2 * modes
    turned = jnp.transpose(got_ref[...])
    turned = jnp.concatenate([turned[:rows], turned[rows:]], axis=1).astype(BF16)
    place = lax.broadcasted_iota(jnp.int32, (cycles, cycles), 0) == jnp.broadcast_to(
        side_ref[:1, :cycles], (cycles, cycles)
    )
    sky = lax.dot_general(
        turned, jnp.where(place, 1.0, 0.0).astype(BF16), NT, preferred_element_type=F32
    )
    sky = jnp.concatenate([sky, sky], axis=1)
    lane = lax.broadcasted_iota(jnp.int32, (rows, 2 * cycles), 1)
    mode = lax.broadcasted_iota(jnp.int32, (rows, 2 * cycles), 0) & (modes - 1)
    owner = jnp.where(lane < cycles, 0, 1)
    blocks = [
        jnp.where(mode == owner + 2 * t, sky, 0.0).astype(BF16) for t in range(modes // 2)
    ]
    table = legendre_ref[...].reshape(modes * cycles, width)
    product = lax.dot_general(
        jnp.concatenate(blocks, axis=1), table, NN, preferred_element_type=F32
    )
    row_mode = lax.broadcasted_iota(jnp.int32, (rows, LANES), 0) & (modes - 1)
    column = lax.broadcasted_iota(jnp.int32, (rows, LANES), 1) - cycles
    order = jnp.sum(
        jnp.where(row_mode == column, jnp.broadcast_to(side_ref[:1, :], (rows, LANES)), 0).astype(F32),
        axis=1,
        keepdims=True,
    )
    degree = (LMAX - LW + 1 + lax.broadcasted_iota(jnp.int32, (rows, width), 1)).astype(F32)
    product = jnp.where(degree >= order, product, 0.0)
    out_ref[pl.ds(0, modes, stride=2), :] = product[:modes]
    out_ref[pl.ds(1, modes, stride=2), :] = product[modes:]


def kernel_call(kernel, out_shape, dtype=F32, scratch=(), limit=32, **options):
    return pl.pallas_call(
        kernel,
        out_shape=jax.ShapeDtypeStruct(out_shape, dtype) if dtype else out_shape,
        scratch_shapes=list(scratch),
        compiler_params=pltpu.CompilerParams(vmem_limit_bytes=limit * 1024 * 1024),
        **options,
    )


def pack_call(owners, capacity, kernel=pack_kernel):
    outs = [
        jax.ShapeDtypeStruct((owners * 8, LANES), F32),
        jax.ShapeDtypeStruct((8, LANES), jnp.int32),
    ]
    return kernel_call(
        kernel,
        outs,
        None,
        scratch=[
            pltpu.VMEM((owners, capacity), F32),
            pltpu.VMEM((owners, capacity), BF16),
            pltpu.VMEM((1, owners), jnp.int32),
            pltpu.VMEM((1, owners), jnp.int32),
            pltpu.VMEM((8, LANES), jnp.int32),
            pltpu.SemaphoreType.DMA((5,)),
        ],
        limit=60,
        in_specs=[pl.BlockSpec(memory_space=pl.ANY)] * 5,
    )


def local(positions, masses, send_counts, legendre, cycle_order, m_order):
    cube = ("z_lo", "y", "pslab")
    plane = ("y", "pslab")
    cycles = cycle_order.shape[0]
    planes = 16
    capacity = positions.shape[-1]
    mode_count = legendre.shape[0]
    order_rows = m_order.reshape(M // LANES, LANES)
    packed, side = pack_call(cycles, capacity)(
        positions.reshape(cycles, capacity),
        masses.reshape(cycles, capacity),
        send_counts.reshape(1, cycles),
        cycle_order.reshape(1, cycles),
        order_rows,
    )
    got = lax.all_to_all(
        packed.reshape(cycles, 8, LANES), cube, split_axis=0, concat_axis=0, tiled=True
    )
    hits = kernel_call(
        hits_kernel,
        (planes, ROWS, M // planes),
        BF16,
        limit=16,
        cost_estimate=pl.CostEstimate(flops=0, transcendentals=0, bytes_accessed=2 * ROWS * M),
    )(order_rows)
    cycle = kernel_call(
        deposit_kernel,
        (ROWS, 2 * LANES),
        cost_estimate=pl.CostEstimate(
            flops=2 * cycles * capacity * ROWS * 2 * LANES, transcendentals=0, bytes_accessed=2**19
        ),
    )(got)
    parts = kernel_call(spectrum_kernel, (planes, 2 * M // planes // LANES, LANES), BF16)(
        cycle, order_rows, hits, *tables()
    )
    got_parts = lax.all_to_all(parts, ("z_hi", "z_lo"), split_axis=0, concat_axis=0, tiled=True)
    own = kernel_call(slab_sum_kernel, (cycles // 2, LANES), limit=4)(got_parts)
    spread = lax.all_to_all(
        own.reshape(cycles // 2, 1, LANES), plane, split_axis=0, concat_axis=0, tiled=True
    )
    alm = kernel_call(product_kernel, (2 * mode_count, LW), limit=8)(
        spread.reshape(cycles // 2, LANES), side, legendre
    )
    return alm.reshape(mode_count, 2, LW)


def solution(mesh):
    cut = jax.sharding.Mesh(mesh.devices.reshape(8, 2, 4, 8), ("z_hi", "z_lo", "y", "pslab"))
    blk = ("z_hi", "z_lo", "y")
    placed = (
        P(blk, "pslab", None, None),
        P(blk, "pslab", None, None),
        P(blk, "pslab", None),
        P(("pslab",) + blk, None, None),
        P(),
        P(),
    )
    return jax.shard_map(
        local,
        mesh=cut,
        in_specs=placed,
        out_specs=P(("pslab",) + blk, None, None),
        check_vma=False,
    )
```

```python
import math

import jax
import jax.numpy as jnp
import numpy as np
from jax import lax
from jax.experimental import pallas as pl
from jax.experimental.pallas import tpu as pltpu
from jax.sharding import PartitionSpec as P

CYCLE_LEN = 32768
M = 16384
LMAX = 16384
LW = 128

LANES = 128
ROWS = CYCLE_LEN // LANES
UPPER = M // ROWS
TILES = 8
SUB = LANES // TILES
COLUMNS = (TILES + 1) * SUB

F32 = jnp.float32
BF16 = jnp.bfloat16

NT = (((1,), (1,)), ((), ()))
NN = (((1,), (0,)), ((), ()))


def halves(table):
    high = table.astype(jnp.bfloat16)
    low = (table - high.astype(np.float64)).astype(jnp.bfloat16)
    return high, low


def split(values):
    high = values.astype(BF16)
    low = (values - high.astype(F32)).astype(BF16)
    return high, low


def tables():
    two_pi = 2.0 * math.pi
    rows = np.arange(ROWS)
    lanes = np.arange(LANES)
    lanes = TILES * (lanes % SUB) + lanes // SUB
    upper = np.arange(UPPER)
    angle_one = (rows[:, None] * rows[None, :] % ROWS) * (two_pi / ROWS)
    one = np.concatenate([np.cos(angle_one), -np.sin(angle_one)], axis=0)
    twist = (rows[:, None] * lanes[None, :] % CYCLE_LEN) * (two_pi / CYCLE_LEN)
    angle_two = (upper[:, None] * lanes[None, :] % LANES) * (two_pi / LANES)
    cos_two, sin_two = np.cos(angle_two), np.sin(angle_two)
    two = np.concatenate(
        [
            np.concatenate([cos_two, sin_two], axis=1),
            np.concatenate([-sin_two, cos_two], axis=1),
        ],
        axis=0,
    ) * (CYCLE_LEN ** -0.5)
    return (
        *halves(one),
        np.cos(twist).astype(np.float32),
        np.sin(twist).astype(np.float32),
        *halves(two),
    )


def spread_row(values, row, count):
    tile = jnp.broadcast_to(values[row : row + 1, :], (16, LANES)).astype(BF16)
    return jnp.concatenate([tile] * (count // 16), axis=0)


def row_ids(count):
    return lax.broadcasted_iota(jnp.int32, (count, LANES), 0).astype(F32).astype(BF16)


def pack_kernel(positions_hbm, masses_hbm, counts_hbm, out_ref, positions_ref, masses_ref, counts_ref, sems):
    owners = out_ref.shape[0] // 8
    capacity = positions_ref.shape[1]
    copies = [
        pltpu.make_async_copy(positions_hbm, positions_ref, sems.at[0]),
        pltpu.make_async_copy(masses_hbm, masses_ref, sems.at[1]),
        pltpu.make_async_copy(counts_hbm, counts_ref, sems.at[2]),
    ]
    for copy in copies:
        copy.start()
    for copy in copies:
        copy.wait()
    slots = lax.broadcasted_iota(jnp.int32, (owners, LANES), 1)
    row = lax.broadcasted_iota(jnp.int32, (owners, owners), 0)
    column = lax.broadcasted_iota(jnp.int32, (owners, owners), 1)
    turned = jnp.where(row == column, jnp.broadcast_to(counts_ref[...], (owners, owners)), 0)
    counts = jnp.sum(turned.astype(F32), axis=1, keepdims=True).astype(jnp.int32)
    for j in range(capacity // LANES):
        cols = slice(j * LANES, (j + 1) * LANES)
        out_ref[pl.ds(j, owners, stride=8), :] = positions_ref[:, cols]
        live = slots + j * LANES < counts
        out_ref[pl.ds(4 + j, owners, stride=8), :] = jnp.where(
            live, masses_ref[:, cols].astype(F32), 0.0
        )


def deposit_kernel(got_ref, acc_ref, group=64):
    sources = got_ref.shape[0]
    zero = jnp.zeros((), BF16)

    def deposit(first):
        row_id = row_ids(ROWS)
        sub_id = lax.broadcasted_iota(jnp.int32, (SUB, LANES), 0)
        lane_ids = [(TILES * sub_id + t).astype(F32).astype(BF16) for t in range(TILES)]
        highs, lows = [], []
        for s in range(group):
            tile = got_ref[first + s]
            places, mass = tile[0:4], tile[4:8]
            floored = jnp.floor(places)
            fraction = places - floored
            pixel = floored.astype(jnp.int32) & (CYCLE_LEN - 1)
            high = (pixel >> 7).astype(F32)
            low = (pixel & (LANES - 1)).astype(F32)
            near = 1.0 - fraction
            for r in range(4):
                highs.append(
                    jnp.where(spread_row(high, r, ROWS) == row_id, spread_row(mass, r, ROWS), zero)
                )
                low_r, near_r, far_r = (spread_row(v, r, SUB) for v in (low, near, fraction))
                hits = [low_r == lane_id for lane_id in lane_ids]
                tiles = [jnp.where(hits[0], near_r, zero)]
                for t in range(1, TILES):
                    tiles.append(jnp.where(hits[t], near_r, jnp.where(hits[t - 1], far_r, zero)))
                tiles.append(jnp.where(hits[-1], far_r, zero))
                lows.append(jnp.concatenate(tiles, axis=0))
        return lax.dot_general(
            jnp.concatenate(highs, axis=1),
            jnp.concatenate(lows, axis=1),
            NT,
            preferred_element_type=F32,
        )

    acc_ref[:, LANES:] = jnp.zeros((ROWS, LANES), F32)
    if group == sources:
        acc_ref[:, :COLUMNS] = deposit(0)
    else:
        acc_ref[:, :LANES] = jnp.zeros((ROWS, LANES), F32)

        def step(n, carry):
            acc_ref[:, :COLUMNS] += deposit(n * group)
            return carry

        lax.fori_loop(0, sources // group, step, 0)


def hits_kernel(order_ref, places_ref, out_ref, side_ref, block=None):
    if block is None:
        block = lax.axis_index(("x", "core", "z_hi", "z_lo", "y"))
    zero, one = jnp.zeros((), BF16), jnp.ones((), BF16)
    planes = order_ref.shape[0] // 8
    cycles = places_ref.shape[1]

    row = lax.broadcasted_iota(jnp.int32, (cycles, cycles), 0)
    column = lax.broadcasted_iota(jnp.int32, (cycles, cycles), 1)
    half = cycles // 2
    taken = jnp.where(row == 2 * (column % half) + column // half, 1.0, 0.0).astype(BF16)
    places = jnp.broadcast_to(places_ref[...], (16, cycles)).astype(F32).astype(BF16)
    places = lax.dot_general(places, taken, NN, preferred_element_type=F32)[:8].astype(jnp.int32)
    own = jnp.broadcast_to(order_ref[pl.ds(block // 4, 1), :], side_ref.shape)
    own = pltpu.roll(own, lax.rem(LANES + cycles - lax.rem(block, 4) * 32, LANES), 1)
    side_lane = lax.broadcasted_iota(jnp.int32, side_ref.shape, 1)
    side_ref[...] = jnp.where(side_lane < cycles, jnp.concatenate([places, places], axis=1), own)

    def step(k, carry):
        ids = row_ids(ROWS)
        lower = (order_ref[pl.ds(k, 8, stride=planes), :] & (ROWS - 1)).astype(F32)
        hits = [jnp.where(spread_row(lower, r, ROWS) == ids, one, zero) for r in range(8)]
        out_ref[k] = jnp.concatenate(hits, axis=1)
        return carry

    lax.fori_loop(0, planes, step, 0)


def spectrum_kernel(
    acc_ref, order_ref, hits_ref, one_h_ref, one_l_ref, cos_ref, sin_ref, two_h_ref, two_l_ref, out_ref
):
    beyond = acc_ref[:, LANES:]
    column = lax.broadcasted_iota(jnp.int32, (ROWS, LANES), 1)
    next_row = pltpu.roll(pltpu.roll(beyond, LANES - SUB + 1, 1), 1, 0)
    cycle = acc_ref[:, :LANES] + jnp.where(
        column == 0, next_row, jnp.where(column < SUB, pltpu.roll(beyond, 1, 1), 0.0)
    )

    def dot(a, b, dims):
        return lax.dot_general(a, b, dims, preferred_element_type=F32)

    cycle_h, cycle_l = split(cycle)
    first = (
        dot(one_h_ref[...], cycle_l, NN)
        + dot(one_l_ref[...], cycle_h, NN)
        + dot(one_h_ref[...], cycle_h, NN)
    )
    real, imag = first[:ROWS], first[ROWS:]
    cos, sin = cos_ref[...], sin_ref[...]
    twisted = jnp.concatenate([real * cos + imag * sin, imag * cos - real * sin], axis=1)
    twisted_h, twisted_l = split(twisted)
    spectrum = (
        dot(two_h_ref[...], twisted_l, NT)
        + dot(two_l_ref[...], twisted_h, NT)
        + dot(two_h_ref[...], twisted_h, NT)
    )
    spectrum = spectrum.astype(BF16)
    upper_ids = lax.broadcasted_iota(jnp.int32, (UPPER, LANES), 0)
    planes = out_ref.shape[0]
    for k in range(planes):
        upper = order_ref[pl.ds(k, 8, stride=planes), :] >> 8
        picked = dot(spectrum, hits_ref[k], NN)
        reals, imags = [], []
        for r in range(8):
            cols = slice(r * LANES, (r + 1) * LANES)
            mine = jnp.broadcast_to(upper[r : r + 1, :], (UPPER, LANES)) == upper_ids
            reals.append(jnp.sum(jnp.where(mine, picked[:UPPER, cols], 0.0), axis=0, keepdims=True))
            imags.append(jnp.sum(jnp.where(mine, picked[UPPER:, cols], 0.0), axis=0, keepdims=True))
        rows = reals[::2] + imags[::2] + reals[1::2] + imags[1::2]
        out_ref[k] = jnp.concatenate(rows, axis=0).astype(BF16)


def slab_sum_kernel(parts_ref, out_ref):
    z_count = parts_ref.shape[0]
    quarter = lax.broadcasted_iota(jnp.int32, (4, LANES), 1) // 32
    for z_lo in range(2):
        total = parts_ref[z_lo].astype(F32)
        for z in range(z_lo + 2, z_count, 2):
            total = total + parts_ref[z].astype(F32)
        for y in range(4):
            row = jnp.zeros((4, LANES), F32)
            for n in range(4):
                shift = (n - y) % 4 * 32
                values = pltpu.roll(total, shift, 1) if shift else total
                row = jnp.where(quarter == n, values[4 * n : 4 * n + 4], row)
            out_ref[pl.ds(8 * y + z_lo, 4, stride=2), :] = row


def product_kernel(got_ref, side_ref, legendre_ref, out_ref):
    modes, cycles, width = legendre_ref.shape
    rows = 2 * modes
    got = jnp.concatenate([got_ref[pl.ds(z_lo, 16, stride=2), :] for z_lo in range(2)], axis=0)
    turned = jnp.transpose(got)
    turned = jnp.concatenate([turned[:rows], turned[rows:]], axis=1).astype(BF16)
    place = lax.broadcasted_iota(jnp.int32, (cycles, cycles), 0) == jnp.broadcast_to(
        side_ref[:1, :cycles], (cycles, cycles)
    )
    sky = lax.dot_general(
        turned, jnp.where(place, 1.0, 0.0).astype(BF16), NT, preferred_element_type=F32
    )
    sky = jnp.concatenate([sky, sky], axis=1)
    lane = lax.broadcasted_iota(jnp.int32, (rows, 2 * cycles), 1)
    mode = lax.broadcasted_iota(jnp.int32, (rows, 2 * cycles), 0) & (modes - 1)
    owner = jnp.where(lane < cycles, 0, 1)
    blocks = [
        jnp.where(mode == owner + 2 * t, sky, 0.0).astype(BF16) for t in range(modes // 2)
    ]
    table = legendre_ref[...].reshape(modes * cycles, width)
    product = lax.dot_general(
        jnp.concatenate(blocks, axis=1), table, NN, preferred_element_type=F32
    )
    row_mode = lax.broadcasted_iota(jnp.int32, (rows, LANES), 0) & (modes - 1)
    column = lax.broadcasted_iota(jnp.int32, (rows, LANES), 1) - cycles
    order = jnp.sum(
        jnp.where(row_mode == column, jnp.broadcast_to(side_ref[:1, :], (rows, LANES)), 0).astype(F32),
        axis=1,
        keepdims=True,
    )
    degree = (LMAX - LW + 1 + lax.broadcasted_iota(jnp.int32, (rows, width), 1)).astype(F32)
    product = jnp.where(degree >= order, product, 0.0)
    out_ref[pl.ds(0, modes, stride=2), :] = product[:modes]
    out_ref[pl.ds(1, modes, stride=2), :] = product[modes:]


def kernel_call(kernel, out_shape, dtype=F32, scratch=(), limit=32, **options):
    return pl.pallas_call(
        kernel,
        out_shape=jax.ShapeDtypeStruct(out_shape, dtype) if dtype else out_shape,
        scratch_shapes=list(scratch),
        compiler_params=pltpu.CompilerParams(vmem_limit_bytes=limit * 1024 * 1024),
        **options,
    )


def pack_call(owners, capacity):
    return kernel_call(
        pack_kernel,
        (owners * 8, LANES),
        scratch=[
            pltpu.VMEM((owners, capacity), F32),
            pltpu.VMEM((owners, capacity), BF16),
            pltpu.VMEM((1, owners), jnp.int32),
            pltpu.SemaphoreType.DMA((3,)),
        ],
        limit=60,
        in_specs=[pl.BlockSpec(memory_space=pl.ANY)] * 3,
    )


def hits_call(planes, kernel=hits_kernel):
    outs = [
        jax.ShapeDtypeStruct((planes, ROWS, M // planes), BF16),
        jax.ShapeDtypeStruct((8, LANES), jnp.int32),
    ]
    cost = pl.CostEstimate(flops=0, transcendentals=0, bytes_accessed=2 * ROWS * M)
    return kernel_call(kernel, outs, None, limit=16, cost_estimate=cost)


def local(positions, masses, send_counts, legendre, cycle_order, m_order):
    z = ("z_hi", "z_lo")
    cycles = cycle_order.shape[0]
    planes = lax.axis_size(z)
    capacity = positions.shape[-1]
    mode_count = legendre.shape[0]
    order_rows = m_order.reshape(M // LANES, LANES)
    packed = pack_call(cycles, capacity)(
        positions.reshape(cycles, capacity),
        masses.reshape(cycles, capacity),
        send_counts.reshape(1, cycles),
    )
    got = lax.all_to_all(
        packed.reshape(cycles, 8, LANES),
        ("z_lo", "y", "x", "core"),
        split_axis=0,
        concat_axis=0,
        tiled=True,
    )
    hits, side = hits_call(planes)(order_rows, cycle_order.reshape(1, cycles))
    cycle = kernel_call(
        deposit_kernel,
        (ROWS, 2 * LANES),
        cost_estimate=pl.CostEstimate(
            flops=2 * cycles * capacity * ROWS * 2 * LANES, transcendentals=0, bytes_accessed=2**19
        ),
    )(got)
    parts = kernel_call(spectrum_kernel, (planes, 2 * M // planes // LANES, LANES), BF16)(
        cycle, order_rows, hits, *tables()
    )
    got_parts = lax.all_to_all(
        parts.reshape(2 * planes, M // planes // LANES, LANES),
        z + ("core",),
        split_axis=0,
        concat_axis=0,
        tiled=True,
    )
    own = kernel_call(slab_sum_kernel, (cycles // 2, LANES), limit=4)(got_parts.reshape(parts.shape))
    spread = lax.all_to_all(
        own.reshape(cycles // 4, 2, LANES), ("y", "x"), split_axis=0, concat_axis=0, tiled=True
    )
    alm = kernel_call(product_kernel, (2 * mode_count, LW), limit=8)(
        spread.reshape(cycles // 2, LANES), side, legendre
    )
    return alm.reshape(mode_count, 2, LW)


def solution(mesh):
    cut = jax.sharding.Mesh(
        mesh.devices.reshape(8, 2, 4, 4, 2), ("z_hi", "z_lo", "y", "x", "core")
    )
    blk, pslab = ("z_hi", "z_lo", "y"), ("x", "core")
    placed = (
        P(blk, pslab, None, None),
        P(blk, pslab, None, None),
        P(blk, pslab, None),
        P(pslab + blk, None, None),
        P(),
        P(),
    )
    return jax.shard_map(
        local,
        mesh=cut,
        in_specs=placed,
        out_specs=P(pslab + blk, None, None),
        check_vma=False,
    )
```

```python
import math

import jax
import jax.numpy as jnp
import numpy as np
from jax import lax
from jax.experimental import pallas as pl
from jax.experimental.pallas import tpu as pltpu
from jax.sharding import PartitionSpec as P

CYCLE_LEN = 32768
M = 16384
LMAX = 16384
LW = 128

LANES = 128
ROWS = CYCLE_LEN // LANES
UPPER = M // ROWS
TILES = 8
SUB = LANES // TILES
COLUMNS = (TILES + 1) * SUB

F32 = jnp.float32
BF16 = jnp.bfloat16

NT = (((1,), (1,)), ((), ()))
NN = (((1,), (0,)), ((), ()))


def halves(table):
    high = table.astype(jnp.bfloat16)
    low = (table - high.astype(np.float64)).astype(jnp.bfloat16)
    return high, low


def split(values):
    high = values.astype(BF16)
    low = (values - high.astype(F32)).astype(BF16)
    return high, low


def tables():
    two_pi = 2.0 * math.pi
    rows = np.arange(ROWS)
    lanes = np.arange(LANES)
    lanes = TILES * (lanes % SUB) + lanes // SUB
    upper = np.arange(UPPER)
    angle_one = (rows[:, None] * rows[None, :] % ROWS) * (two_pi / ROWS)
    one = np.concatenate([np.cos(angle_one), -np.sin(angle_one)], axis=0)
    twist = (rows[:, None] * lanes[None, :] % CYCLE_LEN) * (two_pi / CYCLE_LEN)
    angle_two = (upper[:, None] * lanes[None, :] % LANES) * (two_pi / LANES)
    cos_two, sin_two = np.cos(angle_two), np.sin(angle_two)
    two = np.concatenate(
        [
            np.concatenate([cos_two, sin_two], axis=1),
            np.concatenate([-sin_two, cos_two], axis=1),
        ],
        axis=0,
    ) * (CYCLE_LEN ** -0.5)
    return (
        *halves(one),
        np.cos(twist).astype(np.float32),
        np.sin(twist).astype(np.float32),
        *halves(two),
    )


def spread_row(values, row, count):
    tile = jnp.broadcast_to(values[row : row + 1, :], (16, LANES)).astype(BF16)
    return jnp.concatenate([tile] * (count // 16), axis=0)


def row_ids(count):
    return lax.broadcasted_iota(jnp.int32, (count, LANES), 0).astype(F32).astype(BF16)


def pack_kernel(positions_hbm, masses_hbm, counts_hbm, out_hbm, positions_ref, masses_ref, counts_ref, out_ref, sems):
    owners, capacity = positions_ref.shape
    chunks = sems.shape[0] - 1
    rows = owners // chunks
    copies = []
    for n in range(chunks):
        part = pl.ds(n * rows, rows)
        copies.append(
            (
                pltpu.make_async_copy(positions_hbm.at[part, :], positions_ref.at[part, :], sems.at[n, 0]),
                pltpu.make_async_copy(masses_hbm.at[part, :], masses_ref.at[part, :], sems.at[n, 1]),
                pltpu.make_async_copy(
                    out_ref.at[pl.ds(n * rows * 8, rows * 8), :],
                    out_hbm.at[pl.ds(n * rows * 8, rows * 8), :],
                    sems.at[n, 2],
                ),
            )
        )
    counts_copy = pltpu.make_async_copy(counts_hbm, counts_ref, sems.at[chunks, 0])
    counts_copy.start()
    for positions_copy, masses_copy, _ in copies:
        positions_copy.start()
        masses_copy.start()
    counts_copy.wait()
    row = lax.broadcasted_iota(jnp.int32, (owners, owners), 0)
    column = lax.broadcasted_iota(jnp.int32, (owners, owners), 1)
    turned = jnp.where(row == column, jnp.broadcast_to(counts_ref[...], (owners, owners)), 0)
    counts = jnp.sum(turned.astype(F32), axis=1, keepdims=True).astype(jnp.int32)
    slots = lax.broadcasted_iota(jnp.int32, (rows, LANES), 1)
    for n, (positions_copy, masses_copy, out_copy) in enumerate(copies):
        first = n * rows
        positions_copy.wait()
        masses_copy.wait()
        for j in range(capacity // LANES):
            cols = slice(j * LANES, (j + 1) * LANES)
            out_ref[pl.ds(first * 8 + j, rows, stride=8), :] = positions_ref[first : first + rows, cols]
            live = slots + j * LANES < counts[first : first + rows]
            out_ref[pl.ds(first * 8 + 4 + j, rows, stride=8), :] = jnp.where(
                live, masses_ref[first : first + rows, cols].astype(F32), 0.0
            )
        out_copy.start()
    for _, _, out_copy in copies:
        out_copy.wait()


def deposit_kernel(got_ref, acc_ref, group=4):
    sources = got_ref.shape[0]
    zero = jnp.zeros((), BF16)

    def deposit(first):
        row_id = row_ids(ROWS)
        sub_id = lax.broadcasted_iota(jnp.int32, (SUB, LANES), 0)
        lane_ids = [(TILES * sub_id + t).astype(F32).astype(BF16) for t in range(TILES)]
        highs, lows = [], []
        for s in range(group):
            tile = got_ref[first + s]
            places, mass = tile[0:4], tile[4:8]
            floored = jnp.floor(places)
            fraction = places - floored
            pixel = floored.astype(jnp.int32) & (CYCLE_LEN - 1)
            high = (pixel >> 7).astype(F32)
            low = (pixel & (LANES - 1)).astype(F32)
            near = 1.0 - fraction
            for r in range(4):
                highs.append(
                    jnp.where(spread_row(high, r, ROWS) == row_id, spread_row(mass, r, ROWS), zero)
                )
                low_r, near_r, far_r = (spread_row(v, r, SUB) for v in (low, near, fraction))
                hits = [low_r == lane_id for lane_id in lane_ids]
                tiles = [jnp.where(hits[0], near_r, zero)]
                for t in range(1, TILES):
                    tiles.append(jnp.where(hits[t], near_r, jnp.where(hits[t - 1], far_r, zero)))
                tiles.append(jnp.where(hits[-1], far_r, zero))
                lows.append(jnp.concatenate(tiles, axis=0))
        return lax.dot_general(
            jnp.concatenate(highs, axis=1),
            jnp.concatenate(lows, axis=1),
            NT,
            preferred_element_type=F32,
        )

    acc_ref[:, LANES:] = jnp.zeros((ROWS, LANES), F32)
    acc_ref[:, :COLUMNS] = deposit(0)
    for first in range(group, sources, group):
        acc_ref[:, :COLUMNS] += deposit(first)


def hits_kernel(order_ref, places_ref, out_ref, side_ref, block=None):
    if block is None:
        block = lax.axis_index(("x", "core", "z_hi", "z_lo", "y"))
    zero, one = jnp.zeros((), BF16), jnp.ones((), BF16)
    planes = order_ref.shape[0] // 8
    cycles = places_ref.shape[1]

    row = lax.broadcasted_iota(jnp.int32, (cycles, cycles), 0)
    column = lax.broadcasted_iota(jnp.int32, (cycles, cycles), 1)
    half = cycles // 2
    taken = jnp.where(row == 2 * (column % half) + column // half, 1.0, 0.0).astype(BF16)
    places = jnp.broadcast_to(places_ref[...], (16, cycles)).astype(F32).astype(BF16)
    places = lax.dot_general(places, taken, NN, preferred_element_type=F32)[:8].astype(jnp.int32)
    own = jnp.broadcast_to(order_ref[pl.ds(block // 4, 1), :], side_ref.shape)
    own = pltpu.roll(own, lax.rem(LANES + cycles - lax.rem(block, 4) * 32, LANES), 1)
    side_lane = lax.broadcasted_iota(jnp.int32, side_ref.shape, 1)
    side_ref[...] = jnp.where(side_lane < cycles, jnp.concatenate([places, places], axis=1), own)

    def step(k, carry):
        ids = row_ids(ROWS)
        lower = (order_ref[pl.ds(k, 8, stride=planes), :] & (ROWS - 1)).astype(F32)
        hits = [jnp.where(spread_row(lower, r, ROWS) == ids, one, zero) for r in range(8)]
        out_ref[k] = jnp.concatenate(hits, axis=1)
        return carry

    lax.fori_loop(0, planes, step, 0)


def spectrum_kernel(
    acc_ref, order_ref, hits_ref, one_h_ref, one_l_ref, cos_ref, sin_ref, two_h_ref, two_l_ref, out_ref
):
    beyond = acc_ref[:, LANES:]
    column = lax.broadcasted_iota(jnp.int32, (ROWS, LANES), 1)
    next_row = pltpu.roll(pltpu.roll(beyond, LANES - SUB + 1, 1), 1, 0)
    cycle = acc_ref[:, :LANES] + jnp.where(
        column == 0, next_row, jnp.where(column < SUB, pltpu.roll(beyond, 1, 1), 0.0)
    )

    def dot(a, b, dims):
        return lax.dot_general(a, b, dims, preferred_element_type=F32)

    cycle_h, cycle_l = split(cycle)
    both = dot(one_h_ref[...], jnp.concatenate([cycle_h, cycle_l], axis=1), NN)
    first = both[:, :LANES] + (both[:, LANES:] + dot(one_l_ref[...], cycle_h, NN))
    real, imag = first[:ROWS], first[ROWS:]
    cos, sin = cos_ref[...], sin_ref[...]
    twisted = jnp.concatenate([real * cos + imag * sin, imag * cos - real * sin], axis=1)
    twisted_h, twisted_l = split(twisted)
    spectrum = (
        dot(two_h_ref[...], twisted_l, NT)
        + dot(two_l_ref[...], twisted_h, NT)
        + dot(two_h_ref[...], twisted_h, NT)
    )
    spectrum = spectrum.astype(BF16)
    upper_ids = lax.broadcasted_iota(jnp.int32, (UPPER, LANES), 0)
    planes = out_ref.shape[0]
    for k in range(planes):
        upper = order_ref[pl.ds(k, 8, stride=planes), :] >> 8
        picked = dot(spectrum, hits_ref[k], NN)
        reals, imags = [], []
        for r in range(8):
            cols = slice(r * LANES, (r + 1) * LANES)
            mine = jnp.broadcast_to(upper[r : r + 1, :], (UPPER, LANES)) == upper_ids
            reals.append(jnp.sum(jnp.where(mine, picked[:UPPER, cols], 0.0), axis=0, keepdims=True))
            imags.append(jnp.sum(jnp.where(mine, picked[UPPER:, cols], 0.0), axis=0, keepdims=True))
        rows = reals[::2] + imags[::2] + reals[1::2] + imags[1::2]
        out_ref[k] = jnp.concatenate(rows, axis=0).astype(BF16)


def slab_sum_kernel(parts_ref, out_ref):
    z_count = parts_ref.shape[0]
    quarter = lax.broadcasted_iota(jnp.int32, (4, LANES), 1) // 32
    for z_lo in range(2):
        total = parts_ref[z_lo].astype(F32)
        for z in range(z_lo + 2, z_count, 2):
            total = total + parts_ref[z].astype(F32)
        for y in range(4):
            row = jnp.zeros((4, LANES), F32)
            for n in range(4):
                shift = (n - y) % 4 * 32
                values = pltpu.roll(total, shift, 1) if shift else total
                row = jnp.where(quarter == n, values[4 * n : 4 * n + 4], row)
            out_ref[pl.ds(8 * y + z_lo, 4, stride=2), :] = row


def product_kernel(got_ref, side_ref, legendre_ref, out_ref):
    modes, cycles, width = legendre_ref.shape
    rows = 2 * modes
    got = jnp.concatenate([got_ref[pl.ds(z_lo, 16, stride=2), :] for z_lo in range(2)], axis=0)
    turned = jnp.transpose(got)
    turned = jnp.concatenate([turned[:rows], turned[rows:]], axis=1).astype(BF16)
    place = lax.broadcasted_iota(jnp.int32, (cycles, cycles), 0) == jnp.broadcast_to(
        side_ref[:1, :cycles], (cycles, cycles)
    )
    sky = lax.dot_general(
        turned, jnp.where(place, 1.0, 0.0).astype(BF16), NT, preferred_element_type=F32
    )
    sky = jnp.concatenate([sky, sky], axis=1)
    lane = lax.broadcasted_iota(jnp.int32, (rows, 2 * cycles), 1)
    mode = lax.broadcasted_iota(jnp.int32, (rows, 2 * cycles), 0) & (modes - 1)
    owner = jnp.where(lane < cycles, 0, 1)
    blocks = [
        jnp.where(mode == owner + 2 * t, sky, 0.0).astype(BF16) for t in range(modes // 2)
    ]
    table = legendre_ref[...].reshape(modes * cycles, width)
    product = lax.dot_general(
        jnp.concatenate(blocks, axis=1), table, NN, preferred_element_type=F32
    )
    row_mode = lax.broadcasted_iota(jnp.int32, (rows, LANES), 0) & (modes - 1)
    column = lax.broadcasted_iota(jnp.int32, (rows, LANES), 1) - cycles
    order = jnp.sum(
        jnp.where(row_mode == column, jnp.broadcast_to(side_ref[:1, :], (rows, LANES)), 0).astype(F32),
        axis=1,
        keepdims=True,
    )
    degree = (LMAX - LW + 1 + lax.broadcasted_iota(jnp.int32, (rows, width), 1)).astype(F32)
    product = jnp.where(degree >= order, product, 0.0)
    out_ref[pl.ds(0, modes, stride=2), :] = product[:modes]
    out_ref[pl.ds(1, modes, stride=2), :] = product[modes:]


def kernel_call(kernel, out_shape, dtype=F32, scratch=(), limit=32, **options):
    return pl.pallas_call(
        kernel,
        out_shape=jax.ShapeDtypeStruct(out_shape, dtype) if dtype else out_shape,
        scratch_shapes=list(scratch),
        compiler_params=pltpu.CompilerParams(vmem_limit_bytes=limit * 1024 * 1024),
        **options,
    )


def pack_call(owners, capacity):
    return kernel_call(
        pack_kernel,
        (owners * 8, LANES),
        scratch=[
            pltpu.VMEM((owners, capacity), F32),
            pltpu.VMEM((owners, capacity), BF16),
            pltpu.VMEM((1, owners), jnp.int32),
            pltpu.VMEM((owners * 8, LANES), F32),
            pltpu.SemaphoreType.DMA((5, 3)),
        ],
        limit=60,
        in_specs=[pl.BlockSpec(memory_space=pl.ANY)] * 3,
        out_specs=pl.BlockSpec(memory_space=pl.ANY),
    )


def hits_call(planes, kernel=hits_kernel):
    outs = [
        jax.ShapeDtypeStruct((planes, ROWS, M // planes), BF16),
        jax.ShapeDtypeStruct((8, LANES), jnp.int32),
    ]
    cost = pl.CostEstimate(flops=0, transcendentals=0, bytes_accessed=2 * ROWS * M)
    return kernel_call(kernel, outs, None, limit=16, cost_estimate=cost)


def local(positions, masses, send_counts, legendre, cycle_order, m_order):
    z = ("z_hi", "z_lo")
    cycles = cycle_order.shape[0]
    planes = lax.axis_size(z)
    capacity = positions.shape[-1]
    mode_count = legendre.shape[0]
    order_rows = m_order.reshape(M // LANES, LANES)
    packed = pack_call(cycles, capacity)(
        positions.reshape(cycles, capacity),
        masses.reshape(cycles, capacity),
        send_counts.reshape(1, cycles),
    )
    got = lax.all_to_all(
        packed.reshape(cycles, 8, LANES),
        ("z_lo", "y", "x", "core"),
        split_axis=0,
        concat_axis=0,
        tiled=True,
    )
    hits, side = hits_call(planes)(order_rows, cycle_order.reshape(1, cycles))
    cycle = kernel_call(
        deposit_kernel,
        (ROWS, 2 * LANES),
        cost_estimate=pl.CostEstimate(
            flops=2 * cycles * capacity * ROWS * 2 * LANES, transcendentals=0, bytes_accessed=2**19
        ),
    )(got)
    parts = kernel_call(spectrum_kernel, (planes, 2 * M // planes // LANES, LANES), BF16)(
        cycle, order_rows, hits, *tables()
    )
    got_parts = lax.all_to_all(
        parts.reshape(2 * planes, M // planes // LANES, LANES),
        z + ("core",),
        split_axis=0,
        concat_axis=0,
        tiled=True,
    )
    own = kernel_call(slab_sum_kernel, (cycles // 2, LANES), limit=4)(got_parts.reshape(parts.shape))
    spread = lax.all_to_all(
        own.reshape(cycles // 4, 2, LANES), ("y", "x"), split_axis=0, concat_axis=0, tiled=True
    )
    alm = kernel_call(product_kernel, (2 * mode_count, LW), limit=8)(
        spread.reshape(cycles // 2, LANES), side, legendre
    )
    return alm.reshape(mode_count, 2, LW)


def solution(mesh):
    cut = jax.sharding.Mesh(
        mesh.devices.reshape(8, 2, 4, 4, 2), ("z_hi", "z_lo", "y", "x", "core")
    )
    blk, pslab = ("z_hi", "z_lo", "y"), ("x", "core")
    placed = (
        P(blk, pslab, None, None),
        P(blk, pslab, None, None),
        P(blk, pslab, None),
        P(pslab + blk, None, None),
        P(),
        P(),
    )
    return jax.shard_map(
        local,
        mesh=cut,
        in_specs=placed,
        out_specs=P(pslab + blk, None, None),
        check_vma=False,
    )
```

```python
import math

import jax
import jax.numpy as jnp
import numpy as np
from jax import lax
from jax.experimental import pallas as pl
from jax.experimental.pallas import tpu as pltpu
from jax.sharding import PartitionSpec as P

CYCLE_LEN = 32768
M = 16384
LMAX = 16384
LW = 128

LANES = 128
ROWS = CYCLE_LEN // LANES
UPPER = M // ROWS
TILES = 8
SUB = LANES // TILES
COLUMNS = (TILES + 1) * SUB

F32 = jnp.float32
BF16 = jnp.bfloat16

NT = (((1,), (1,)), ((), ()))
NN = (((1,), (0,)), ((), ()))


def halves(table):
    high = table.astype(jnp.bfloat16)
    low = (table - high.astype(np.float64)).astype(jnp.bfloat16)
    return high, low


def split(values):
    high = values.astype(BF16)
    low = (values - high.astype(F32)).astype(BF16)
    return high, low


def tables():
    two_pi = 2.0 * math.pi
    rows = np.arange(ROWS)
    lanes = np.arange(LANES)
    lanes = TILES * (lanes % SUB) + lanes // SUB
    upper = np.arange(UPPER)
    angle_one = (rows[:, None] * rows[None, :] % ROWS) * (two_pi / ROWS)
    one = np.concatenate([np.cos(angle_one), -np.sin(angle_one)], axis=0)
    twist = (rows[:, None] * lanes[None, :] % CYCLE_LEN) * (two_pi / CYCLE_LEN)
    angle_two = (upper[:, None] * lanes[None, :] % LANES) * (two_pi / LANES)
    cos_two, sin_two = np.cos(angle_two), np.sin(angle_two)
    two = np.concatenate(
        [
            np.concatenate([cos_two, sin_two], axis=1),
            np.concatenate([-sin_two, cos_two], axis=1),
        ],
        axis=0,
    ) * (CYCLE_LEN ** -0.5)
    return (
        *halves(one),
        np.cos(twist).astype(np.float32),
        np.sin(twist).astype(np.float32),
        *halves(two),
    )


def spread_row(values, row, count):
    tile = jnp.broadcast_to(values[row : row + 1, :], (16, LANES)).astype(BF16)
    return jnp.concatenate([tile] * (count // 16), axis=0)


def row_ids(count):
    return lax.broadcasted_iota(jnp.int32, (count, LANES), 0).astype(F32).astype(BF16)


def pack_kernel(positions_hbm, masses_hbm, counts_hbm, out_hbm, positions_ref, masses_ref, counts_ref, out_ref, sems):
    owners, capacity = positions_ref.shape
    chunks = sems.shape[0] - 1
    rows = owners // chunks
    copies = []
    for n in range(chunks):
        part = pl.ds(n * rows, rows)
        copies.append(
            (
                pltpu.make_async_copy(positions_hbm.at[part, :], positions_ref.at[part, :], sems.at[n, 0]),
                pltpu.make_async_copy(masses_hbm.at[part, :], masses_ref.at[part, :], sems.at[n, 1]),
                pltpu.make_async_copy(
                    out_ref.at[pl.ds(n * rows * 8, rows * 8), :],
                    out_hbm.at[pl.ds(n * rows * 8, rows * 8), :],
                    sems.at[n, 2],
                ),
            )
        )
    counts_copy = pltpu.make_async_copy(counts_hbm, counts_ref, sems.at[chunks, 0])
    counts_copy.start()
    for positions_copy, masses_copy, _ in copies:
        positions_copy.start()
        masses_copy.start()
    counts_copy.wait()
    row = lax.broadcasted_iota(jnp.int32, (owners, owners), 0)
    column = lax.broadcasted_iota(jnp.int32, (owners, owners), 1)
    turned = jnp.where(row == column, jnp.broadcast_to(counts_ref[...], (owners, owners)), 0)
    counts = jnp.sum(turned.astype(F32), axis=1, keepdims=True).astype(jnp.int32)
    slots = lax.broadcasted_iota(jnp.int32, (rows, LANES), 1)
    for n, (positions_copy, masses_copy, out_copy) in enumerate(copies):
        first = n * rows
        positions_copy.wait()
        masses_copy.wait()
        for j in range(capacity // LANES):
            cols = slice(j * LANES, (j + 1) * LANES)
            out_ref[pl.ds(first * 8 + j, rows, stride=8), :] = positions_ref[first : first + rows, cols]
            live = slots + j * LANES < counts[first : first + rows]
            out_ref[pl.ds(first * 8 + 4 + j, rows, stride=8), :] = jnp.where(
                live, masses_ref[first : first + rows, cols].astype(F32), 0.0
            )
        out_copy.start()
    for _, _, out_copy in copies:
        out_copy.wait()


def deposit_kernel(got_ref, acc_ref):
    zero = jnp.zeros((), BF16)
    row_id = lax.broadcasted_iota(jnp.int32, (LANES, ROWS), 1).astype(F32).astype(BF16)
    sub_id = lax.broadcasted_iota(jnp.int32, (SUB, LANES), 0)
    lane_ids = [(TILES * sub_id + t).astype(F32).astype(BF16) for t in range(TILES)]
    highs, lows = [], []
    for s in range(got_ref.shape[0]):
        tile = got_ref[s]
        places, mass = tile[0:4], tile[4:8]
        floored = jnp.floor(places)
        fraction = places - floored
        pixel = floored.astype(jnp.int32) & (CYCLE_LEN - 1)
        high = (pixel >> 7).astype(F32)
        low = (pixel & (LANES - 1)).astype(F32)
        near = 1.0 - fraction
        turned = jnp.transpose(jnp.concatenate([high, mass], axis=0))
        for r in range(4):
            high_r, mass_r = (
                jnp.broadcast_to(turned[:, c : c + 1], (LANES, LANES)).astype(BF16) for c in (r, 4 + r)
            )
            highs.append(
                jnp.concatenate(
                    [
                        jnp.where(high_r == row_id[:, :LANES], mass_r, zero),
                        jnp.where(high_r == row_id[:, LANES:], mass_r, zero),
                    ],
                    axis=1,
                )
            )
            low_r, near_r, far_r = (spread_row(v, r, SUB) for v in (low, near, fraction))
            hits = [low_r == lane_id for lane_id in lane_ids]
            tiles = [jnp.where(hits[0], near_r, zero)]
            for t in range(1, TILES):
                tiles.append(jnp.where(hits[t], near_r, jnp.where(hits[t - 1], far_r, zero)))
            tiles.append(jnp.where(hits[-1], far_r, zero))
            lows.append(jnp.concatenate(tiles, axis=0))
    acc_ref[...] = lax.dot_general(
        jnp.concatenate(lows, axis=1),
        jnp.concatenate(highs, axis=0),
        NN,
        preferred_element_type=F32,
    )


def hits_kernel(order_ref, places_ref, out_ref, side_ref, block=None):
    if block is None:
        block = lax.axis_index(("x", "core", "z_hi", "z_lo", "y"))
    zero, one = jnp.zeros((), BF16), jnp.ones((), BF16)
    planes = order_ref.shape[0] // 8
    cycles = places_ref.shape[1]

    row = lax.broadcasted_iota(jnp.int32, (cycles, cycles), 0)
    column = lax.broadcasted_iota(jnp.int32, (cycles, cycles), 1)
    half = cycles // 2
    taken = jnp.where(row == 2 * (column % half) + column // half, 1.0, 0.0).astype(BF16)
    places = jnp.broadcast_to(places_ref[...], (16, cycles)).astype(F32).astype(BF16)
    places = lax.dot_general(places, taken, NN, preferred_element_type=F32)[:8].astype(jnp.int32)
    own = jnp.broadcast_to(order_ref[pl.ds(block // 4, 1), :], side_ref.shape)
    own = pltpu.roll(own, lax.rem(LANES + cycles - lax.rem(block, 4) * 32, LANES), 1)
    side_lane = lax.broadcasted_iota(jnp.int32, side_ref.shape, 1)
    side_ref[...] = jnp.where(side_lane < cycles, jnp.concatenate([places, places], axis=1), own)

    def step(k, carry):
        ids = row_ids(ROWS)
        lower = (order_ref[pl.ds(k, 8, stride=planes), :] & (ROWS - 1)).astype(F32)
        hits = [jnp.where(spread_row(lower, r, ROWS) == ids, one, zero) for r in range(8)]
        out_ref[k] = jnp.concatenate(hits, axis=1)
        return carry

    lax.fori_loop(0, planes, step, 0)


def spectrum_kernel(
    acc_ref, order_ref, hits_ref, one_h_ref, one_l_ref, cos_ref, sin_ref, two_h_ref, two_l_ref, out_ref
):
    beyond = pltpu.roll(acc_ref[LANES:, :], 1, 0)
    column = lax.broadcasted_iota(jnp.int32, (SUB, ROWS), 0)
    beyond = jnp.where(column == 0, pltpu.roll(beyond, 1, 1), beyond)
    cycle = jnp.concatenate([acc_ref[:SUB, :] + beyond, acc_ref[SUB:LANES, :]], axis=0)

    def dot(a, b, dims):
        return lax.dot_general(a, b, dims, preferred_element_type=F32)

    cycle_h, cycle_l = split(cycle)
    both = dot(one_h_ref[...], jnp.concatenate([cycle_h, cycle_l], axis=0), NT)
    first = both[:, :LANES] + (both[:, LANES:] + dot(one_l_ref[...], cycle_h, NT))
    real, imag = first[:ROWS], first[ROWS:]
    cos, sin = cos_ref[...], sin_ref[...]
    twisted = jnp.concatenate([real * cos + imag * sin, imag * cos - real * sin], axis=1)
    twisted_h, twisted_l = split(twisted)
    spectrum = (
        dot(two_h_ref[...], twisted_l, NT)
        + dot(two_l_ref[...], twisted_h, NT)
        + dot(two_h_ref[...], twisted_h, NT)
    )
    spectrum = spectrum.astype(BF16)
    upper_ids = lax.broadcasted_iota(jnp.int32, (UPPER, LANES), 0)
    planes = out_ref.shape[0]
    for k in range(planes):
        upper = order_ref[pl.ds(k, 8, stride=planes), :] >> 8
        picked = dot(spectrum, hits_ref[k], NN)
        reals, imags = [], []
        for r in range(8):
            cols = slice(r * LANES, (r + 1) * LANES)
            mine = jnp.broadcast_to(upper[r : r + 1, :], (UPPER, LANES)) == upper_ids
            reals.append(jnp.sum(jnp.where(mine, picked[:UPPER, cols], 0.0), axis=0, keepdims=True))
            imags.append(jnp.sum(jnp.where(mine, picked[UPPER:, cols], 0.0), axis=0, keepdims=True))
        rows = reals[::2] + imags[::2] + reals[1::2] + imags[1::2]
        out_ref[k] = jnp.concatenate(rows, axis=0).astype(BF16)


def slab_sum_kernel(parts_ref, out_ref):
    z_count = parts_ref.shape[0]
    quarter = lax.broadcasted_iota(jnp.int32, (4, LANES), 1) // 32
    for z_lo in range(2):
        total = parts_ref[z_lo].astype(F32)
        for z in range(z_lo + 2, z_count, 2):
            total = total + parts_ref[z].astype(F32)
        for y in range(4):
            row = jnp.zeros((4, LANES), F32)
            for n in range(4):
                shift = (n - y) % 4 * 32
                values = pltpu.roll(total, shift, 1) if shift else total
                row = jnp.where(quarter == n, values[4 * n : 4 * n + 4], row)
            out_ref[pl.ds(8 * y + z_lo, 4, stride=2), :] = row


def product_kernel(got_ref, side_ref, legendre_ref, out_ref):
    modes, cycles, width = legendre_ref.shape
    rows = 2 * modes
    got = jnp.concatenate([got_ref[pl.ds(z_lo, 16, stride=2), :] for z_lo in range(2)], axis=0)
    turned = jnp.transpose(got)
    turned = jnp.concatenate([turned[:rows], turned[rows:]], axis=1).astype(BF16)
    place = lax.broadcasted_iota(jnp.int32, (cycles, cycles), 0) == jnp.broadcast_to(
        side_ref[:1, :cycles], (cycles, cycles)
    )
    sky = lax.dot_general(
        turned, jnp.where(place, 1.0, 0.0).astype(BF16), NT, preferred_element_type=F32
    )
    sky = jnp.concatenate([sky, sky], axis=1)
    lane = lax.broadcasted_iota(jnp.int32, (rows, 2 * cycles), 1)
    mode = lax.broadcasted_iota(jnp.int32, (rows, 2 * cycles), 0) & (modes - 1)
    owner = jnp.where(lane < cycles, 0, 1)
    blocks = [
        jnp.where(mode == owner + 2 * t, sky, 0.0).astype(BF16) for t in range(modes // 2)
    ]
    table = legendre_ref[...].reshape(modes * cycles, width)
    product = lax.dot_general(
        jnp.concatenate(blocks, axis=1), table, NN, preferred_element_type=F32
    )
    row_mode = lax.broadcasted_iota(jnp.int32, (rows, LANES), 0) & (modes - 1)
    column = lax.broadcasted_iota(jnp.int32, (rows, LANES), 1) - cycles
    order = jnp.sum(
        jnp.where(row_mode == column, jnp.broadcast_to(side_ref[:1, :], (rows, LANES)), 0).astype(F32),
        axis=1,
        keepdims=True,
    )
    degree = (LMAX - LW + 1 + lax.broadcasted_iota(jnp.int32, (rows, width), 1)).astype(F32)
    product = jnp.where(degree >= order, product, 0.0)
    out_ref[pl.ds(0, modes, stride=2), :] = product[:modes]
    out_ref[pl.ds(1, modes, stride=2), :] = product[modes:]


def kernel_call(kernel, out_shape, dtype=F32, scratch=(), limit=32, **options):
    return pl.pallas_call(
        kernel,
        out_shape=jax.ShapeDtypeStruct(out_shape, dtype) if dtype else out_shape,
        scratch_shapes=list(scratch),
        compiler_params=pltpu.CompilerParams(vmem_limit_bytes=limit * 1024 * 1024),
        **options,
    )


def pack_call(owners, capacity):
    return kernel_call(
        pack_kernel,
        (owners * 8, LANES),
        scratch=[
            pltpu.VMEM((owners, capacity), F32),
            pltpu.VMEM((owners, capacity), BF16),
            pltpu.VMEM((1, owners), jnp.int32),
            pltpu.VMEM((owners * 8, LANES), F32),
            pltpu.SemaphoreType.DMA((5, 3)),
        ],
        limit=60,
        in_specs=[pl.BlockSpec(memory_space=pl.ANY)] * 3,
        out_specs=pl.BlockSpec(memory_space=pl.ANY),
    )


def hits_call(planes, kernel=hits_kernel):
    outs = [
        jax.ShapeDtypeStruct((planes, ROWS, M // planes), BF16),
        jax.ShapeDtypeStruct((8, LANES), jnp.int32),
    ]
    cost = pl.CostEstimate(flops=0, transcendentals=0, bytes_accessed=2 * ROWS * M)
    return kernel_call(kernel, outs, None, limit=16, cost_estimate=cost)


def local(positions, masses, send_counts, legendre, cycle_order, m_order):
    z = ("z_hi", "z_lo")
    cycles = cycle_order.shape[0]
    planes = lax.axis_size(z)
    capacity = positions.shape[-1]
    mode_count = legendre.shape[0]
    order_rows = m_order.reshape(M // LANES, LANES)
    packed = pack_call(cycles, capacity)(
        positions.reshape(cycles, capacity),
        masses.reshape(cycles, capacity),
        send_counts.reshape(1, cycles),
    )
    got = lax.all_to_all(
        packed.reshape(cycles, 8, LANES),
        ("z_lo", "y", "x", "core"),
        split_axis=0,
        concat_axis=0,
        tiled=True,
    )
    hits, side = hits_call(planes)(order_rows, cycle_order.reshape(1, cycles))
    cycle = kernel_call(
        deposit_kernel,
        (COLUMNS, ROWS),
        cost_estimate=pl.CostEstimate(
            flops=2 * cycles * capacity * ROWS * 2 * LANES, transcendentals=0, bytes_accessed=2**19
        ),
    )(got)
    parts = kernel_call(spectrum_kernel, (planes, 2 * M // planes // LANES, LANES), BF16)(
        cycle, order_rows, hits, *tables()
    )
    got_parts = lax.all_to_all(
        parts.reshape(2 * planes, M // planes // LANES, LANES),
        z + ("core",),
        split_axis=0,
        concat_axis=0,
        tiled=True,
    )
    own = kernel_call(slab_sum_kernel, (cycles // 2, LANES), limit=4)(got_parts.reshape(parts.shape))
    spread = lax.all_to_all(
        own.reshape(cycles // 4, 2, LANES), ("y", "x"), split_axis=0, concat_axis=0, tiled=True
    )
    alm = kernel_call(product_kernel, (2 * mode_count, LW), limit=8)(
        spread.reshape(cycles // 2, LANES), side, legendre
    )
    return alm.reshape(mode_count, 2, LW)


def solution(mesh):
    cut = jax.sharding.Mesh(
        mesh.devices.reshape(8, 2, 4, 4, 2), ("z_hi", "z_lo", "y", "x", "core")
    )
    blk, pslab = ("z_hi", "z_lo", "y"), ("x", "core")
    placed = (
        P(blk, pslab, None, None),
        P(blk, pslab, None, None),
        P(blk, pslab, None),
        P(pslab + blk, None, None),
        P(),
        P(),
    )
    return jax.shard_map(
        local,
        mesh=cut,
        in_specs=placed,
        out_specs=P(pslab + blk, None, None),
        check_vma=False,
    )
```

```python
import math

import jax
import jax.numpy as jnp
import numpy as np
from jax import lax
from jax.experimental import pallas as pl
from jax.experimental.pallas import tpu as pltpu
from jax.sharding import PartitionSpec as P

CYCLE_LEN = 32768
M = 16384
LMAX = 16384
LW = 128

LANES = 128
ROWS = CYCLE_LEN // LANES
UPPER = M // ROWS
TILES = 8
SUB = LANES // TILES
COLUMNS = (TILES + 1) * SUB

F32 = jnp.float32
BF16 = jnp.bfloat16

NT = (((1,), (1,)), ((), ()))
NN = (((1,), (0,)), ((), ()))


def halves(table):
    high = table.astype(jnp.bfloat16)
    low = (table - high.astype(np.float64)).astype(jnp.bfloat16)
    return high, low


def split(values):
    high = values.astype(BF16)
    low = (values - high.astype(F32)).astype(BF16)
    return high, low


def tables():
    two_pi = 2.0 * math.pi
    rows = np.arange(ROWS)
    lanes = np.arange(LANES)
    lanes = TILES * (lanes % SUB) + lanes // SUB
    upper = np.arange(UPPER)
    angle_one = (rows[:, None] * rows[None, :] % ROWS) * (two_pi / ROWS)
    one = np.concatenate([np.cos(angle_one), -np.sin(angle_one)], axis=0)
    twist = (rows[:, None] * lanes[None, :] % CYCLE_LEN) * (two_pi / CYCLE_LEN)
    angle_two = (upper[:, None] * lanes[None, :] % LANES) * (two_pi / LANES)
    cos_two, sin_two = np.cos(angle_two), np.sin(angle_two)
    two = np.concatenate(
        [
            np.concatenate([cos_two, sin_two], axis=1),
            np.concatenate([-sin_two, cos_two], axis=1),
        ],
        axis=0,
    ) * (CYCLE_LEN ** -0.5)
    return (
        *halves(one),
        np.cos(twist).astype(np.float32),
        np.sin(twist).astype(np.float32),
        *halves(two),
    )


def spread_row(values, row, count):
    tile = jnp.broadcast_to(values[row : row + 1, :], (16, LANES)).astype(BF16)
    return jnp.concatenate([tile] * (count // 16), axis=0)


def row_ids(count):
    return lax.broadcasted_iota(jnp.int32, (count, LANES), 0).astype(F32).astype(BF16)


def pack_kernel(positions_hbm, masses_hbm, counts_hbm, out_hbm, positions_ref, masses_ref, counts_ref, out_ref, sems):
    owners, capacity = positions_ref.shape
    chunks = sems.shape[0] - 1
    rows = owners // chunks
    copies = []
    for n in range(chunks):
        part = pl.ds(n * rows, rows)
        copies.append(
            (
                pltpu.make_async_copy(positions_hbm.at[part, :], positions_ref.at[part, :], sems.at[n, 0]),
                pltpu.make_async_copy(masses_hbm.at[part, :], masses_ref.at[part, :], sems.at[n, 1]),
                pltpu.make_async_copy(
                    out_ref.at[pl.ds(n * rows * 8, rows * 8), :],
                    out_hbm.at[pl.ds(n * rows * 8, rows * 8), :],
                    sems.at[n, 2],
                ),
            )
        )
    counts_copy = pltpu.make_async_copy(counts_hbm, counts_ref, sems.at[chunks, 0])
    counts_copy.start()
    for positions_copy, masses_copy, _ in copies:
        positions_copy.start()
        masses_copy.start()
    counts_copy.wait()
    row = lax.broadcasted_iota(jnp.int32, (owners, owners), 0)
    column = lax.broadcasted_iota(jnp.int32, (owners, owners), 1)
    turned = jnp.where(row == column, jnp.broadcast_to(counts_ref[...], (owners, owners)), 0)
    counts = jnp.sum(turned.astype(F32), axis=1, keepdims=True).astype(jnp.int32)
    slots = lax.broadcasted_iota(jnp.int32, (rows, LANES), 1)
    for n, (positions_copy, masses_copy, out_copy) in enumerate(copies):
        first = n * rows
        positions_copy.wait()
        masses_copy.wait()
        for j in range(capacity // LANES):
            cols = slice(j * LANES, (j + 1) * LANES)
            out_ref[pl.ds(first * 8 + j, rows, stride=8), :] = positions_ref[first : first + rows, cols]
            live = slots + j * LANES < counts[first : first + rows]
            out_ref[pl.ds(first * 8 + 4 + j, rows, stride=8), :] = jnp.where(
                live, masses_ref[first : first + rows, cols].astype(F32), 0.0
            )
        out_copy.start()
    for _, _, out_copy in copies:
        out_copy.wait()


def deposit_kernel(got_ref, acc_ref):
    sources, cycles = got_ref.shape[:2]
    zero = jnp.zeros((), BF16)

    def deposit(cycle):
        row_id = row_ids(ROWS)
        sub_id = lax.broadcasted_iota(jnp.int32, (SUB, LANES), 0)
        lane_ids = [(TILES * sub_id + t).astype(F32).astype(BF16) for t in range(TILES)]
        highs, lows = [], []
        for s in range(sources):
            tile = got_ref[s, cycle]
            places, mass = tile[0:4], tile[4:8]
            floored = jnp.floor(places)
            fraction = places - floored
            pixel = floored.astype(jnp.int32) & (CYCLE_LEN - 1)
            high = (pixel >> 7).astype(F32)
            low = (pixel & (LANES - 1)).astype(F32)
            near = 1.0 - fraction
            for r in range(4):
                highs.append(
                    jnp.where(spread_row(high, r, ROWS) == row_id, spread_row(mass, r, ROWS), zero)
                )
                low_r, near_r, far_r = (spread_row(v, r, SUB) for v in (low, near, fraction))
                hits = [low_r == lane_id for lane_id in lane_ids]
                tiles = [jnp.where(hits[0], near_r, zero)]
                for t in range(1, TILES):
                    tiles.append(jnp.where(hits[t], near_r, jnp.where(hits[t - 1], far_r, zero)))
                tiles.append(jnp.where(hits[-1], far_r, zero))
                lows.append(jnp.concatenate(tiles, axis=0))
        return lax.dot_general(
            jnp.concatenate(highs, axis=1),
            jnp.concatenate(lows, axis=1),
            NT,
            preferred_element_type=F32,
        )

    for cycle in range(cycles):
        acc_ref[cycle, :, LANES:] = jnp.zeros((ROWS, LANES), F32)
        acc_ref[cycle, :, :COLUMNS] = deposit(cycle)


def hits_kernel(order_ref, places_ref, out_ref, side_ref, block=None):
    if block is None:
        block = lax.axis_index(("x", "core", "z", "y"))
    zero, one = jnp.zeros((), BF16), jnp.ones((), BF16)
    planes = order_ref.shape[0] // 8
    cycles = places_ref.shape[1]

    row = lax.broadcasted_iota(jnp.int32, (cycles, cycles), 0)
    column = lax.broadcasted_iota(jnp.int32, (cycles, cycles), 1)
    half = cycles // 2
    taken = jnp.where(row == 2 * (column % half) + column // half, 1.0, 0.0).astype(BF16)
    places = jnp.broadcast_to(places_ref[...], (16, cycles)).astype(F32).astype(BF16)
    places = lax.dot_general(places, taken, NN, preferred_element_type=F32)[:8].astype(jnp.int32)
    own = jnp.broadcast_to(order_ref[pl.ds(block // 4, 1), :], side_ref.shape)
    own = pltpu.roll(own, lax.rem(LANES + cycles - lax.rem(block, 4) * 32, LANES), 1)
    side_lane = lax.broadcasted_iota(jnp.int32, side_ref.shape, 1)
    side_ref[...] = jnp.where(side_lane < cycles, jnp.concatenate([places, places], axis=1), own)

    def step(k, carry):
        ids = row_ids(ROWS)
        lower = (order_ref[pl.ds(k, 8, stride=planes), :] & (ROWS - 1)).astype(F32)
        hits = [jnp.where(spread_row(lower, r, ROWS) == ids, one, zero) for r in range(8)]
        out_ref[k] = jnp.concatenate(hits, axis=1)
        return carry

    lax.fori_loop(0, planes, step, 0)


def spectrum_kernel(
    acc_ref, order_ref, hits_ref, one_h_ref, one_l_ref, cos_ref, sin_ref, two_h_ref, two_l_ref, out_ref
):
    def dot(a, b, dims):
        return lax.dot_general(a, b, dims, preferred_element_type=F32)

    highs, lows = [], []
    column = lax.broadcasted_iota(jnp.int32, (ROWS, LANES), 1)
    for n in range(acc_ref.shape[0]):
        beyond = acc_ref[n, :, LANES:]
        next_row = pltpu.roll(pltpu.roll(beyond, LANES - SUB + 1, 1), 1, 0)
        moved = jnp.where(column < SUB, pltpu.roll(beyond, 1, 1), 0.0)
        high, low = split(acc_ref[n, :, :LANES] + jnp.where(column == 0, next_row, moved))
        highs.append(high)
        lows.append(low)
    first = dot(one_h_ref[...], jnp.concatenate(highs, axis=1), NN) + (
        dot(one_h_ref[...], jnp.concatenate(lows, axis=1), NN)
        + dot(one_l_ref[...], jnp.concatenate(highs, axis=1), NN)
    )
    cos, sin = cos_ref[...], sin_ref[...]
    highs, lows = [], []
    for n in range(acc_ref.shape[0]):
        cols = slice(n * LANES, (n + 1) * LANES)
        real, imag = first[:ROWS, cols], first[ROWS:, cols]
        twisted = jnp.concatenate([real * cos + imag * sin, imag * cos - real * sin], axis=1)
        high, low = split(twisted)
        highs.append(high)
        lows.append(low)
    spectrum = dot(two_h_ref[...], jnp.concatenate(highs, axis=0), NT) + (
        dot(two_h_ref[...], jnp.concatenate(lows, axis=0), NT)
        + dot(two_l_ref[...], jnp.concatenate(highs, axis=0), NT)
    )
    spectrum = spectrum.astype(BF16)
    spectrum = jnp.concatenate([spectrum[:, :ROWS], spectrum[:, ROWS:]], axis=0)
    upper_ids = lax.broadcasted_iota(jnp.int32, (UPPER, LANES), 0)
    planes = out_ref.shape[0]
    for k in range(planes):
        upper = order_ref[pl.ds(k, 8, stride=planes), :] >> 8
        picked = dot(spectrum, hits_ref[k], NN)
        found = []
        for r in range(8):
            cols = slice(r * LANES, (r + 1) * LANES)
            mine = jnp.broadcast_to(upper[r : r + 1, :], (UPPER, LANES)) == upper_ids
            found.append(
                [
                    jnp.sum(
                        jnp.where(mine, picked[UPPER * n : UPPER * (n + 1), cols], 0.0),
                        axis=0,
                        keepdims=True,
                    )
                    for n in range(4)
                ]
            )
        rows = [found[2 * x + core][n] for core in range(2) for n in range(4) for x in range(4)]
        out_ref[k] = jnp.concatenate(rows, axis=0).astype(BF16)


def slab_sum_kernel(parts_ref, out_ref):
    count = parts_ref.shape[0]
    quarter = lax.broadcasted_iota(jnp.int32, (4, LANES), 1) // 32
    for core in range(2):
        total = parts_ref[core].astype(F32)
        for n in range(core + 2, count, 2):
            total = total + parts_ref[n].astype(F32)
        for y in range(4):
            row = jnp.zeros((4, LANES), F32)
            for n in range(4):
                shift = (n - y) % 4 * 32
                values = pltpu.roll(total, shift, 1) if shift else total
                row = jnp.where(quarter == n, values[4 * n : 4 * n + 4], row)
            out_ref[pl.ds(8 * y + core, 4, stride=2), :] = row


def product_kernel(got_ref, side_ref, legendre_ref, out_ref):
    modes, cycles, width = legendre_ref.shape
    rows = 2 * modes
    turned = jnp.transpose(got_ref[...])
    turned = jnp.concatenate([turned[:rows], turned[rows:]], axis=1).astype(BF16)
    place = lax.broadcasted_iota(jnp.int32, (cycles, cycles), 0) == jnp.broadcast_to(
        side_ref[:1, :cycles], (cycles, cycles)
    )
    sky = lax.dot_general(
        turned, jnp.where(place, 1.0, 0.0).astype(BF16), NT, preferred_element_type=F32
    )
    sky = jnp.concatenate([sky, sky], axis=1)
    lane = lax.broadcasted_iota(jnp.int32, (rows, 2 * cycles), 1)
    mode = lax.broadcasted_iota(jnp.int32, (rows, 2 * cycles), 0) & (modes - 1)
    owner = jnp.where(lane < cycles, 0, 1)
    blocks = [
        jnp.where(mode == owner + 2 * t, sky, 0.0).astype(BF16) for t in range(modes // 2)
    ]
    table = legendre_ref[...].reshape(modes * cycles, width)
    product = lax.dot_general(
        jnp.concatenate(blocks, axis=1), table, NN, preferred_element_type=F32
    )
    row_mode = lax.broadcasted_iota(jnp.int32, (rows, LANES), 0) & (modes - 1)
    column = lax.broadcasted_iota(jnp.int32, (rows, LANES), 1) - cycles
    order = jnp.sum(
        jnp.where(row_mode == column, jnp.broadcast_to(side_ref[:1, :], (rows, LANES)), 0).astype(F32),
        axis=1,
        keepdims=True,
    )
    degree = (LMAX - LW + 1 + lax.broadcasted_iota(jnp.int32, (rows, width), 1)).astype(F32)
    product = jnp.where(degree >= order, product, 0.0)
    out_ref[pl.ds(0, modes, stride=2), :] = product[:modes]
    out_ref[pl.ds(1, modes, stride=2), :] = product[modes:]


def kernel_call(kernel, out_shape, dtype=F32, scratch=(), limit=32, **options):
    return pl.pallas_call(
        kernel,
        out_shape=jax.ShapeDtypeStruct(out_shape, dtype) if dtype else out_shape,
        scratch_shapes=list(scratch),
        compiler_params=pltpu.CompilerParams(vmem_limit_bytes=limit * 1024 * 1024),
        **options,
    )


def pack_call(owners, capacity):
    return kernel_call(
        pack_kernel,
        (owners * 8, LANES),
        scratch=[
            pltpu.VMEM((owners, capacity), F32),
            pltpu.VMEM((owners, capacity), BF16),
            pltpu.VMEM((1, owners), jnp.int32),
            pltpu.VMEM((owners * 8, LANES), F32),
            pltpu.SemaphoreType.DMA((5, 3)),
        ],
        limit=60,
        in_specs=[pl.BlockSpec(memory_space=pl.ANY)] * 3,
        out_specs=pl.BlockSpec(memory_space=pl.ANY),
    )


def hits_call(planes, kernel=hits_kernel):
    outs = [
        jax.ShapeDtypeStruct((planes, ROWS, M // planes), BF16),
        jax.ShapeDtypeStruct((8, LANES), jnp.int32),
    ]
    cost = pl.CostEstimate(flops=0, transcendentals=0, bytes_accessed=2 * ROWS * M)
    return kernel_call(kernel, outs, None, limit=16, cost_estimate=cost)


def local(positions, masses, send_counts, legendre, cycle_order, m_order):
    cycles = cycle_order.shape[0]
    planes = lax.axis_size("z")
    capacity = positions.shape[-1]
    mode_count = legendre.shape[0]
    order_rows = m_order.reshape(M // LANES, LANES)
    packed = pack_call(cycles, capacity)(
        positions.reshape(cycles, capacity),
        masses.reshape(cycles, capacity),
        send_counts.reshape(1, cycles),
    )
    got = lax.all_to_all(
        packed.reshape(cycles // 2, 2, 8, LANES),
        ("y", "x", "core"),
        split_axis=0,
        concat_axis=0,
        tiled=True,
    )
    hits, side = hits_call(planes)(order_rows, cycle_order.reshape(1, cycles))
    cycle = kernel_call(
        deposit_kernel,
        (2, ROWS, 2 * LANES),
        cost_estimate=pl.CostEstimate(
            flops=2 * cycles * capacity * ROWS * 2 * LANES, transcendentals=0, bytes_accessed=2**19
        ),
    )(got)
    parts = kernel_call(spectrum_kernel, (planes, 4 * M // planes // LANES, LANES), BF16)(
        cycle, order_rows, hits, *tables()
    )
    got_parts = lax.all_to_all(
        parts.reshape(2 * planes, 2 * M // planes // LANES, LANES),
        ("z", "core"),
        split_axis=0,
        concat_axis=0,
        tiled=True,
    )
    own = kernel_call(slab_sum_kernel, (cycles // 2, LANES), limit=4)(got_parts)
    spread = lax.all_to_all(
        own.reshape(cycles // 4, 2, LANES), ("y", "x"), split_axis=0, concat_axis=0, tiled=True
    )
    alm = kernel_call(product_kernel, (2 * mode_count, LW), limit=8)(
        spread.reshape(cycles // 2, LANES), side, legendre
    )
    return alm.reshape(mode_count, 2, LW)


def solution(mesh):
    cut = jax.sharding.Mesh(mesh.devices.reshape(16, 4, 4, 2), ("z", "y", "x", "core"))
    blk, pslab = ("z", "y"), ("x", "core")
    placed = (
        P(blk, pslab, None, None),
        P(blk, pslab, None, None),
        P(blk, pslab, None),
        P(pslab + blk, None, None),
        P(),
        P(),
    )
    return jax.shard_map(
        local,
        mesh=cut,
        in_specs=placed,
        out_specs=P(pslab + blk, None, None),
        check_vma=False,
    )
```

```python
import math

import jax
import jax.numpy as jnp
import numpy as np
from jax import lax
from jax.experimental import pallas as pl
from jax.experimental.pallas import tpu as pltpu
from jax.sharding import PartitionSpec as P

CYCLE_LEN = 32768
M = 16384
LMAX = 16384
LW = 128

LANES = 128
ROWS = CYCLE_LEN // LANES
UPPER = M // ROWS
TILES = 8
SUB = LANES // TILES
COLUMNS = (TILES + 1) * SUB

FIRST_IN_BLOCK = 18
FIRST_ON_LINE = 16
FIRST_IN_PLANE = 9

F32 = jnp.float32
BF16 = jnp.bfloat16

NT = (((1,), (1,)), ((), ()))
NN = (((1,), (0,)), ((), ()))


def halves(table):
    high = table.astype(jnp.bfloat16)
    low = (table - high.astype(np.float64)).astype(jnp.bfloat16)
    return high, low


def split(values):
    high = values.astype(BF16)
    low = (values - high.astype(F32)).astype(BF16)
    return high, low


def tables():
    two_pi = 2.0 * math.pi
    rows = np.arange(ROWS)
    lanes = np.arange(LANES)
    lanes = TILES * (lanes % SUB) + lanes // SUB
    upper = np.arange(UPPER)
    angle_one = (rows[:, None] * rows[None, :] % ROWS) * (two_pi / ROWS)
    one = np.concatenate([np.cos(angle_one), -np.sin(angle_one)], axis=0)
    twist = (rows[:, None] * lanes[None, :] % CYCLE_LEN) * (two_pi / CYCLE_LEN)
    angle_two = (upper[:, None] * lanes[None, :] % LANES) * (two_pi / LANES)
    cos_two, sin_two = np.cos(angle_two), np.sin(angle_two)
    two = np.concatenate(
        [
            np.concatenate([cos_two, sin_two], axis=1),
            np.concatenate([-sin_two, cos_two], axis=1),
        ],
        axis=0,
    ) * (CYCLE_LEN ** -0.5)
    return (
        *halves(one),
        np.cos(twist).astype(np.float32),
        np.sin(twist).astype(np.float32),
        *halves(two),
    )


def spread_row(values, row, count):
    tile = jnp.broadcast_to(values[row : row + 1, :], (16, LANES)).astype(BF16)
    return jnp.concatenate([tile] * (count // 16), axis=0)


def row_ids(count):
    return lax.broadcasted_iota(jnp.int32, (count, LANES), 0).astype(F32).astype(BF16)


def pack_kernel(positions_hbm, masses_hbm, counts_hbm, out_hbm, positions_ref, masses_ref, counts_ref, out_ref, sems):
    owners, capacity = positions_ref.shape
    rows = 16
    chunks = owners // rows
    in_copies, out_copies = [], []
    for n in range(chunks):
        part = pl.ds(n * rows, rows)
        in_copies.append(
            (
                pltpu.make_async_copy(positions_hbm.at[part, :], positions_ref.at[part, :], sems.at[n, 0]),
                pltpu.make_async_copy(masses_hbm.at[part, :], masses_ref.at[part, :], sems.at[n, 1]),
            )
        )
        cuts = sorted({n * rows, min(max(FIRST_IN_BLOCK, n * rows), (n + 1) * rows), (n + 1) * rows})
        out_copies.append(
            [
                pltpu.make_async_copy(
                    out_ref.at[pl.ds(8 * a, 8 * (b - a)), :],
                    out_hbm.at[pl.ds(8 * ((a - FIRST_IN_BLOCK) % owners), 8 * (b - a)), :],
                    sems.at[n, 2 + m],
                )
                for m, (a, b) in enumerate(zip(cuts, cuts[1:]))
            ]
        )
    counts_copy = pltpu.make_async_copy(counts_hbm, counts_ref, sems.at[chunks, 0])
    counts_copy.start()
    for copies in in_copies:
        for copy in copies:
            copy.start()
    counts_copy.wait()
    row = lax.broadcasted_iota(jnp.int32, (owners, owners), 0)
    column = lax.broadcasted_iota(jnp.int32, (owners, owners), 1)
    turned = jnp.where(row == column, jnp.broadcast_to(counts_ref[...], (owners, owners)), 0)
    counts = jnp.sum(turned.astype(F32), axis=1, keepdims=True).astype(jnp.int32)
    slots = lax.broadcasted_iota(jnp.int32, (rows, LANES), 1)
    for n in range(chunks):
        first = n * rows
        for copy in in_copies[n]:
            copy.wait()
        for j in range(capacity // LANES):
            cols = slice(j * LANES, (j + 1) * LANES)
            out_ref[pl.ds(first * 8 + j, rows, stride=8), :] = positions_ref[first : first + rows, cols]
            live = slots + j * LANES < counts[first : first + rows]
            out_ref[pl.ds(first * 8 + 4 + j, rows, stride=8), :] = jnp.where(
                live, masses_ref[first : first + rows, cols].astype(F32), 0.0
            )
        for copy in out_copies[n]:
            copy.start()
    for copies in out_copies:
        for copy in copies:
            copy.wait()


def deposit_kernel(got_ref, acc_ref):
    sources = got_ref.shape[0]
    zero = jnp.zeros((), BF16)

    def deposit():
        row_id = row_ids(ROWS)
        sub_id = lax.broadcasted_iota(jnp.int32, (SUB, LANES), 0)
        lane_ids = [(TILES * sub_id + t).astype(F32).astype(BF16) for t in range(TILES)]
        highs, lows = [], []
        for s in range(sources):
            tile = got_ref[s]
            places, mass = tile[0:4], tile[4:8]
            floored = jnp.floor(places)
            fraction = places - floored
            pixel = floored.astype(jnp.int32) & (CYCLE_LEN - 1)
            high = (pixel >> 7).astype(F32)
            low = (pixel & (LANES - 1)).astype(F32)
            near = 1.0 - fraction
            for r in range(4):
                highs.append(
                    jnp.where(spread_row(high, r, ROWS) == row_id, spread_row(mass, r, ROWS), zero)
                )
                low_r, near_r, far_r = (spread_row(v, r, SUB) for v in (low, near, fraction))
                hits = [low_r == lane_id for lane_id in lane_ids]
                tiles = [jnp.where(hits[0], near_r, zero)]
                for t in range(1, TILES):
                    tiles.append(jnp.where(hits[t], near_r, jnp.where(hits[t - 1], far_r, zero)))
                tiles.append(jnp.where(hits[-1], far_r, zero))
                lows.append(jnp.concatenate(tiles, axis=0))
        return lax.dot_general(
            jnp.concatenate(highs, axis=1),
            jnp.concatenate(lows, axis=1),
            NT,
            preferred_element_type=F32,
        )

    acc_ref[:, LANES:] = jnp.zeros((ROWS, LANES), F32)
    acc_ref[:, :COLUMNS] = deposit()


def hits_kernel(order_ref, places_ref, out_ref, side_ref, block=None):
    if block is None:
        block = lax.axis_index(("x", "core", "z_hi", "z_lo", "y"))
    zero, one = jnp.zeros((), BF16), jnp.ones((), BF16)
    planes = order_ref.shape[0] // 8
    cycles = places_ref.shape[1]

    row = lax.broadcasted_iota(jnp.int32, (cycles, cycles), 0)
    column = lax.broadcasted_iota(jnp.int32, (cycles, cycles), 1)
    half = cycles // 2
    taken = jnp.where(row == 2 * (column % half) + column // half, 1.0, 0.0).astype(BF16)
    places = jnp.broadcast_to(places_ref[...], (16, cycles)).astype(F32).astype(BF16)
    places = lax.dot_general(places, taken, NN, preferred_element_type=F32)[:8].astype(jnp.int32)
    own = jnp.broadcast_to(order_ref[pl.ds(block // 4, 1), :], side_ref.shape)
    own = pltpu.roll(own, lax.rem(LANES + cycles - lax.rem(block, 4) * 32, LANES), 1)
    side_lane = lax.broadcasted_iota(jnp.int32, side_ref.shape, 1)
    side_ref[...] = jnp.where(side_lane < cycles, jnp.concatenate([places, places], axis=1), own)

    def step(k, carry):
        ids = row_ids(ROWS)
        lower = (order_ref[pl.ds(k, 8, stride=planes), :] & (ROWS - 1)).astype(F32)
        hits = [jnp.where(spread_row(lower, r, ROWS) == ids, one, zero) for r in range(8)]
        out_ref[k] = jnp.concatenate(hits, axis=1)
        return carry

    lax.fori_loop(0, planes, step, 0)


def spectrum_kernel(
    acc_ref, order_ref, hits_ref, one_h_ref, one_l_ref, cos_ref, sin_ref, two_h_ref, two_l_ref, out_ref
):
    beyond = acc_ref[:, LANES:]
    column = lax.broadcasted_iota(jnp.int32, (ROWS, LANES), 1)
    next_row = pltpu.roll(pltpu.roll(beyond, LANES - SUB + 1, 1), 1, 0)
    cycle = acc_ref[:, :LANES] + jnp.where(
        column == 0, next_row, jnp.where(column < SUB, pltpu.roll(beyond, 1, 1), 0.0)
    )

    def dot(a, b, dims):
        return lax.dot_general(a, b, dims, preferred_element_type=F32)

    cycle_h, cycle_l = split(cycle)
    both = dot(one_h_ref[...], jnp.concatenate([cycle_h, cycle_l], axis=1), NN)
    first = both[:, :LANES] + (both[:, LANES:] + dot(one_l_ref[...], cycle_h, NN))
    real, imag = first[:ROWS], first[ROWS:]
    cos, sin = cos_ref[...], sin_ref[...]
    twisted = jnp.concatenate([real * cos + imag * sin, imag * cos - real * sin], axis=1)
    twisted_h, twisted_l = split(twisted)
    spectrum = (
        dot(two_h_ref[...], twisted_l, NT)
        + dot(two_l_ref[...], twisted_h, NT)
        + dot(two_h_ref[...], twisted_h, NT)
    )
    spectrum = spectrum.astype(BF16)
    upper_ids = lax.broadcasted_iota(jnp.int32, (UPPER, LANES), 0)
    planes = out_ref.shape[0]
    for k in range(planes):
        upper = order_ref[pl.ds(k, 8, stride=planes), :] >> 8
        picked = dot(spectrum, hits_ref[k], NN)
        reals, imags = [], []
        for r in range(8):
            cols = slice(r * LANES, (r + 1) * LANES)
            mine = jnp.broadcast_to(upper[r : r + 1, :], (UPPER, LANES)) == upper_ids
            reals.append(jnp.sum(jnp.where(mine, picked[:UPPER, cols], 0.0), axis=0, keepdims=True))
            imags.append(jnp.sum(jnp.where(mine, picked[UPPER:, cols], 0.0), axis=0, keepdims=True))
        rows = reals[::2] + imags[::2] + reals[1::2] + imags[1::2]
        out_ref[(k - FIRST_ON_LINE // 2) % planes] = jnp.concatenate(rows, axis=0).astype(BF16)


def slab_sum_kernel(parts_ref, out_ref):
    z_count = parts_ref.shape[0]
    quarter = lax.broadcasted_iota(jnp.int32, (4, LANES), 1) // 32
    for z_lo in range(2):
        total = parts_ref[z_lo].astype(F32)
        for z in range(z_lo + 2, z_count, 2):
            total = total + parts_ref[z].astype(F32)
        for y in range(4):
            row = jnp.zeros((4, LANES), F32)
            for n in range(4):
                shift = (n - y) % 4 * 32
                values = pltpu.roll(total, shift, 1) if shift else total
                row = jnp.where(quarter == n, values[4 * n : 4 * n + 4], row)
            for x in range(4):
                chip = (4 * y + x - FIRST_IN_PLANE) % 16
                out_ref[pl.ds(2 * chip + z_lo, 1), :] = row[x : x + 1]


def product_kernel(got_ref, side_ref, legendre_ref, out_ref):
    modes, cycles, width = legendre_ref.shape
    rows = 2 * modes
    before = FIRST_IN_PLANE
    got = []
    for z_lo in range(2):
        got.append(got_ref[pl.ds(2 * (16 - before) + z_lo, before, stride=2), :])
        got.append(got_ref[pl.ds(z_lo, 16 - before, stride=2), :])
    got = jnp.concatenate(got, axis=0)
    turned = jnp.transpose(got)
    turned = jnp.concatenate([turned[:rows], turned[rows:]], axis=1).astype(BF16)
    place = lax.broadcasted_iota(jnp.int32, (cycles, cycles), 0) == jnp.broadcast_to(
        side_ref[:1, :cycles], (cycles, cycles)
    )
    sky = lax.dot_general(
        turned, jnp.where(place, 1.0, 0.0).astype(BF16), NT, preferred_element_type=F32
    )
    sky = jnp.concatenate([sky, sky], axis=1)
    lane = lax.broadcasted_iota(jnp.int32, (rows, 2 * cycles), 1)
    mode = lax.broadcasted_iota(jnp.int32, (rows, 2 * cycles), 0) & (modes - 1)
    owner = jnp.where(lane < cycles, 0, 1)
    blocks = [
        jnp.where(mode == owner + 2 * t, sky, 0.0).astype(BF16) for t in range(modes // 2)
    ]
    table = legendre_ref[...].reshape(modes * cycles, width)
    product = lax.dot_general(
        jnp.concatenate(blocks, axis=1), table, NN, preferred_element_type=F32
    )
    row_mode = lax.broadcasted_iota(jnp.int32, (rows, LANES), 0) & (modes - 1)
    column = lax.broadcasted_iota(jnp.int32, (rows, LANES), 1) - cycles
    order = jnp.sum(
        jnp.where(row_mode == column, jnp.broadcast_to(side_ref[:1, :], (rows, LANES)), 0).astype(F32),
        axis=1,
        keepdims=True,
    )
    degree = (LMAX - LW + 1 + lax.broadcasted_iota(jnp.int32, (rows, width), 1)).astype(F32)
    product = jnp.where(degree >= order, product, 0.0)
    out_ref[pl.ds(0, modes, stride=2), :] = product[:modes]
    out_ref[pl.ds(1, modes, stride=2), :] = product[modes:]


def kernel_call(kernel, out_shape, dtype=F32, scratch=(), limit=32, **options):
    return pl.pallas_call(
        kernel,
        out_shape=jax.ShapeDtypeStruct(out_shape, dtype) if dtype else out_shape,
        scratch_shapes=list(scratch),
        compiler_params=pltpu.CompilerParams(vmem_limit_bytes=limit * 1024 * 1024),
        **options,
    )


def pack_call(owners, capacity):
    return kernel_call(
        pack_kernel,
        (owners * 8, LANES),
        scratch=[
            pltpu.VMEM((owners, capacity), F32),
            pltpu.VMEM((owners, capacity), BF16),
            pltpu.VMEM((1, owners), jnp.int32),
            pltpu.VMEM((owners * 8, LANES), F32),
            pltpu.SemaphoreType.DMA((5, 4)),
        ],
        limit=60,
        in_specs=[pl.BlockSpec(memory_space=pl.ANY)] * 3,
        out_specs=pl.BlockSpec(memory_space=pl.ANY),
    )


def hits_call(planes, kernel=hits_kernel):
    outs = [
        jax.ShapeDtypeStruct((planes, ROWS, M // planes), BF16),
        jax.ShapeDtypeStruct((8, LANES), jnp.int32),
    ]
    cost = pl.CostEstimate(flops=0, transcendentals=0, bytes_accessed=2 * ROWS * M)
    return kernel_call(kernel, outs, None, limit=16, cost_estimate=cost)


def exchange(values, axes, first):
    count = lax.axis_size(axes)
    members = [(first + n) % count for n in range(count)]
    return lax.all_to_all(
        values, axes, split_axis=0, concat_axis=0, axis_index_groups=[members], tiled=True
    )


def local(positions, masses, send_counts, legendre, cycle_order, m_order):
    z = ("z_hi", "z_lo")
    cycles = cycle_order.shape[0]
    planes = lax.axis_size(z)
    capacity = positions.shape[-1]
    mode_count = legendre.shape[0]
    order_rows = m_order.reshape(M // LANES, LANES)
    packed = pack_call(cycles, capacity)(
        positions.reshape(cycles, capacity),
        masses.reshape(cycles, capacity),
        send_counts.reshape(1, cycles),
    )
    got = exchange(packed.reshape(cycles, 8, LANES), ("z_lo", "y", "x", "core"), FIRST_IN_BLOCK)
    hits, side = hits_call(planes)(order_rows, cycle_order.reshape(1, cycles))
    cycle = kernel_call(
        deposit_kernel,
        (ROWS, 2 * LANES),
        cost_estimate=pl.CostEstimate(
            flops=2 * cycles * capacity * ROWS * 2 * LANES, transcendentals=0, bytes_accessed=2**19
        ),
    )(got)
    parts = kernel_call(spectrum_kernel, (planes, 2 * M // planes // LANES, LANES), BF16)(
        cycle, order_rows, hits, *tables()
    )
    parts = parts.reshape(2 * planes, M // planes // LANES, LANES)
    got_parts = exchange(parts, z + ("core",), FIRST_ON_LINE)
    own = kernel_call(slab_sum_kernel, (cycles // 2, LANES), limit=4)(
        got_parts.reshape(planes, 2 * M // planes // LANES, LANES)
    )
    spread = exchange(own.reshape(cycles // 4, 2, LANES), ("y", "x"), FIRST_IN_PLANE)
    alm = kernel_call(product_kernel, (2 * mode_count, LW), limit=8)(
        spread.reshape(cycles // 2, LANES), side, legendre
    )
    return alm.reshape(mode_count, 2, LW)


def solution(mesh):
    cut = jax.sharding.Mesh(
        mesh.devices.reshape(8, 2, 4, 4, 2), ("z_hi", "z_lo", "y", "x", "core")
    )
    blk, pslab = ("z_hi", "z_lo", "y"), ("x", "core")
    placed = (
        P(blk, pslab, None, None),
        P(blk, pslab, None, None),
        P(blk, pslab, None),
        P(pslab + blk, None, None),
        P(),
        P(),
    )
    return jax.shard_map(
        local,
        mesh=cut,
        in_specs=placed,
        out_specs=P(pslab + blk, None, None),
        check_vma=False,
    )
```

```python
import math

import jax
import jax.numpy as jnp
import numpy as np
from jax import lax
from jax.experimental import pallas as pl
from jax.experimental.pallas import tpu as pltpu
from jax.sharding import PartitionSpec as P

CYCLE_LEN = 32768
M = 16384
LMAX = 16384
LW = 128

LANES = 128
ROWS = CYCLE_LEN // LANES
UPPER = M // ROWS
TILES = 8
SUB = LANES // TILES
COLUMNS = (TILES + 1) * SUB

FIRST_IN_BLOCK = 20
FIRST_ON_LINE = 16
FIRST_IN_PLANE = 10

F32 = jnp.float32
BF16 = jnp.bfloat16

NT = (((1,), (1,)), ((), ()))
NN = (((1,), (0,)), ((), ()))


def halves(table):
    high = table.astype(jnp.bfloat16)
    low = (table - high.astype(np.float64)).astype(jnp.bfloat16)
    return high, low


def split(values):
    high = values.astype(BF16)
    low = (values - high.astype(F32)).astype(BF16)
    return high, low


def tables():
    two_pi = 2.0 * math.pi
    rows = np.arange(ROWS)
    lanes = np.arange(LANES)
    lanes = TILES * (lanes % SUB) + lanes // SUB
    upper = np.arange(UPPER)
    angle_one = (rows[:, None] * rows[None, :] % ROWS) * (two_pi / ROWS)
    one = np.concatenate([np.cos(angle_one), -np.sin(angle_one)], axis=0)
    twist = (rows[:, None] * lanes[None, :] % CYCLE_LEN) * (two_pi / CYCLE_LEN)
    angle_two = (upper[:, None] * lanes[None, :] % LANES) * (two_pi / LANES)
    cos_two, sin_two = np.cos(angle_two), np.sin(angle_two)
    two = np.concatenate(
        [
            np.concatenate([cos_two, sin_two], axis=1),
            np.concatenate([-sin_two, cos_two], axis=1),
        ],
        axis=0,
    ) * (CYCLE_LEN ** -0.5)
    return (
        *halves(one),
        np.cos(twist).astype(np.float32),
        np.sin(twist).astype(np.float32),
        *halves(two),
    )


def spread_row(values, row, count):
    tile = jnp.broadcast_to(values[row : row + 1, :], (16, LANES)).astype(BF16)
    return jnp.concatenate([tile] * (count // 16), axis=0)


def row_ids(count):
    return lax.broadcasted_iota(jnp.int32, (count, LANES), 0).astype(F32).astype(BF16)


def pack_kernel(positions_hbm, masses_hbm, counts_hbm, out_hbm, positions_ref, masses_ref, counts_ref, out_ref, sems):
    owners, capacity = positions_ref.shape
    rows = 16
    chunks = owners // rows
    in_copies, out_copies = [], []
    for n in range(chunks):
        part = pl.ds(n * rows, rows)
        in_copies.append(
            (
                pltpu.make_async_copy(positions_hbm.at[part, :], positions_ref.at[part, :], sems.at[n, 0]),
                pltpu.make_async_copy(masses_hbm.at[part, :], masses_ref.at[part, :], sems.at[n, 1]),
            )
        )
        cuts = sorted({n * rows, min(max(FIRST_IN_BLOCK, n * rows), (n + 1) * rows), (n + 1) * rows})
        out_copies.append(
            [
                pltpu.make_async_copy(
                    out_ref.at[pl.ds(8 * a, 8 * (b - a)), :],
                    out_hbm.at[pl.ds(8 * ((a - FIRST_IN_BLOCK) % owners), 8 * (b - a)), :],
                    sems.at[n, 2 + m],
                )
                for m, (a, b) in enumerate(zip(cuts, cuts[1:]))
            ]
        )
    counts_copy = pltpu.make_async_copy(counts_hbm, counts_ref, sems.at[chunks, 0])
    counts_copy.start()
    for copies in in_copies:
        for copy in copies:
            copy.start()
    counts_copy.wait()
    row = lax.broadcasted_iota(jnp.int32, (owners, owners), 0)
    column = lax.broadcasted_iota(jnp.int32, (owners, owners), 1)
    turned = jnp.where(row == column, jnp.broadcast_to(counts_ref[...], (owners, owners)), 0)
    counts = jnp.sum(turned.astype(F32), axis=1, keepdims=True).astype(jnp.int32)
    slots = lax.broadcasted_iota(jnp.int32, (rows, LANES), 1)
    for n in range(chunks):
        first = n * rows
        for copy in in_copies[n]:
            copy.wait()
        for j in range(capacity // LANES):
            cols = slice(j * LANES, (j + 1) * LANES)
            out_ref[pl.ds(first * 8 + j, rows, stride=8), :] = positions_ref[first : first + rows, cols]
            live = slots + j * LANES < counts[first : first + rows]
            out_ref[pl.ds(first * 8 + 4 + j, rows, stride=8), :] = jnp.where(
                live, masses_ref[first : first + rows, cols].astype(F32), 0.0
            )
        for copy in out_copies[n]:
            copy.start()
    for copies in out_copies:
        for copy in copies:
            copy.wait()


def deposit_kernel(got_ref, acc_ref):
    sources = got_ref.shape[0]
    zero = jnp.zeros((), BF16)

    def deposit():
        row_id = row_ids(ROWS)
        sub_id = lax.broadcasted_iota(jnp.int32, (SUB, LANES), 0)
        lane_ids = [(TILES * sub_id + t).astype(F32).astype(BF16) for t in range(TILES)]
        highs, lows = [], []
        for s in range(sources):
            tile = got_ref[s]
            places, mass = tile[0:4], tile[4:8]
            floored = jnp.floor(places)
            fraction = places - floored
            pixel = floored.astype(jnp.int32) & (CYCLE_LEN - 1)
            high = (pixel >> 7).astype(F32)
            low = (pixel & (LANES - 1)).astype(F32)
            near = 1.0 - fraction
            for r in range(4):
                highs.append(
                    jnp.where(spread_row(high, r, ROWS) == row_id, spread_row(mass, r, ROWS), zero)
                )
                low_r, near_r, far_r = (spread_row(v, r, SUB) for v in (low, near, fraction))
                hits = [low_r == lane_id for lane_id in lane_ids]
                tiles = [jnp.where(hits[0], near_r, zero)]
                for t in range(1, TILES):
                    tiles.append(jnp.where(hits[t], near_r, jnp.where(hits[t - 1], far_r, zero)))
                tiles.append(jnp.where(hits[-1], far_r, zero))
                lows.append(jnp.concatenate(tiles, axis=0))
        return lax.dot_general(
            jnp.concatenate(highs, axis=1),
            jnp.concatenate(lows, axis=1),
            NT,
            preferred_element_type=F32,
        )

    acc_ref[:, LANES:] = jnp.zeros((ROWS, LANES), F32)
    acc_ref[:, :COLUMNS] = deposit()


def hits_kernel(
    order_hbm, places_hbm, out_hbm, side_hbm, order_ref, places_ref, out_ref, side_ref, sems, block=None
):
    if block is None:
        block = lax.axis_index(("x", "core", "z_hi", "z_lo", "y"))
    zero, one = jnp.zeros((), BF16), jnp.ones((), BF16)
    planes = order_ref.shape[0] // 8
    cycles = places_ref.shape[1]
    order_copy = pltpu.make_async_copy(order_hbm, order_ref, sems.at[planes])
    places_copy = pltpu.make_async_copy(places_hbm, places_ref, sems.at[planes + 1])
    side_copy = pltpu.make_async_copy(side_ref, side_hbm, sems.at[planes + 2])
    out_copies = [
        pltpu.make_async_copy(out_ref.at[k], out_hbm.at[k], sems.at[k]) for k in range(planes)
    ]
    order_copy.start()
    places_copy.start()
    order_copy.wait()
    places_copy.wait()

    ids = row_ids(ROWS)
    for k in range(planes):
        lower = (order_ref[pl.ds(k, 8, stride=planes), :] & (ROWS - 1)).astype(F32)
        hits = [jnp.where(spread_row(lower, r, ROWS) == ids, one, zero) for r in range(8)]
        out_ref[k] = jnp.concatenate(hits, axis=1)
        out_copies[k].start()

    row = lax.broadcasted_iota(jnp.int32, (cycles, cycles), 0)
    column = lax.broadcasted_iota(jnp.int32, (cycles, cycles), 1)
    half = cycles // 2
    taken = jnp.where(row == 2 * (column % half) + column // half, 1.0, 0.0).astype(BF16)
    places = jnp.broadcast_to(places_ref[...], (16, cycles)).astype(F32).astype(BF16)
    places = lax.dot_general(places, taken, NN, preferred_element_type=F32)[:8].astype(jnp.int32)
    own = jnp.broadcast_to(order_ref[pl.ds(block // 4, 1), :], side_ref.shape)
    own = pltpu.roll(own, lax.rem(LANES + cycles - lax.rem(block, 4) * 32, LANES), 1)
    side_lane = lax.broadcasted_iota(jnp.int32, side_ref.shape, 1)
    side_ref[...] = jnp.where(side_lane < cycles, jnp.concatenate([places, places], axis=1), own)
    side_copy.start()
    for copy in out_copies:
        copy.wait()
    side_copy.wait()


def spectrum_kernel(
    acc_ref, order_ref, hits_ref, one_h_ref, one_l_ref, cos_ref, sin_ref, two_h_ref, two_l_ref, out_ref
):
    beyond = acc_ref[:, LANES:]
    column = lax.broadcasted_iota(jnp.int32, (ROWS, LANES), 1)
    next_row = pltpu.roll(pltpu.roll(beyond, LANES - SUB + 1, 1), 1, 0)
    cycle = acc_ref[:, :LANES] + jnp.where(
        column == 0, next_row, jnp.where(column < SUB, pltpu.roll(beyond, 1, 1), 0.0)
    )

    def dot(a, b, dims):
        return lax.dot_general(a, b, dims, preferred_element_type=F32)

    cycle_h, cycle_l = split(cycle)
    both = dot(one_h_ref[...], jnp.concatenate([cycle_h, cycle_l], axis=1), NN)
    first = both[:, :LANES] + (both[:, LANES:] + dot(one_l_ref[...], cycle_h, NN))
    real, imag = first[:ROWS], first[ROWS:]
    cos, sin = cos_ref[...], sin_ref[...]
    twisted = jnp.concatenate([real * cos + imag * sin, imag * cos - real * sin], axis=1)
    twisted_h, twisted_l = split(twisted)
    spectrum = (
        dot(two_h_ref[...], twisted_l, NT)
        + dot(two_l_ref[...], twisted_h, NT)
        + dot(two_h_ref[...], twisted_h, NT)
    )
    spectrum = spectrum.astype(BF16)
    upper_ids = lax.broadcasted_iota(jnp.int32, (UPPER, LANES), 0)
    planes = out_ref.shape[0]
    for k in range(planes):
        upper = order_ref[pl.ds(k, 8, stride=planes), :] >> 8
        picked = dot(spectrum, hits_ref[k], NN)
        reals, imags = [], []
        for r in range(8):
            cols = slice(r * LANES, (r + 1) * LANES)
            mine = jnp.broadcast_to(upper[r : r + 1, :], (UPPER, LANES)) == upper_ids
            reals.append(jnp.sum(jnp.where(mine, picked[:UPPER, cols], 0.0), axis=0, keepdims=True))
            imags.append(jnp.sum(jnp.where(mine, picked[UPPER:, cols], 0.0), axis=0, keepdims=True))
        rows = reals[::2] + imags[::2] + reals[1::2] + imags[1::2]
        out_ref[(k - FIRST_ON_LINE // 2) % planes] = jnp.concatenate(rows, axis=0).astype(BF16)


def slab_sum_kernel(parts_ref, out_ref):
    z_count = parts_ref.shape[0]
    quarter = lax.broadcasted_iota(jnp.int32, (4, LANES), 1) // 32
    for z_lo in range(2):
        total = parts_ref[z_lo].astype(F32)
        for z in range(z_lo + 2, z_count, 2):
            total = total + parts_ref[z].astype(F32)
        for y in range(4):
            row = jnp.zeros((4, LANES), F32)
            for n in range(4):
                shift = (n - y) % 4 * 32
                values = pltpu.roll(total, shift, 1) if shift else total
                row = jnp.where(quarter == n, values[4 * n : 4 * n + 4], row)
            for x in range(4):
                chip = (4 * y + x - FIRST_IN_PLANE) % 16
                out_ref[pl.ds(2 * chip + z_lo, 1), :] = row[x : x + 1]


def product_kernel(got_ref, side_ref, legendre_ref, out_ref):
    modes, cycles, width = legendre_ref.shape
    rows = 2 * modes
    before = FIRST_IN_PLANE
    got = []
    for z_lo in range(2):
        got.append(got_ref[pl.ds(2 * (16 - before) + z_lo, before, stride=2), :])
        got.append(got_ref[pl.ds(z_lo, 16 - before, stride=2), :])
    got = jnp.concatenate(got, axis=0)
    turned = jnp.transpose(got)
    turned = jnp.concatenate([turned[:rows], turned[rows:]], axis=1).astype(BF16)
    place = lax.broadcasted_iota(jnp.int32, (cycles, cycles), 0) == jnp.broadcast_to(
        side_ref[:1, :cycles], (cycles, cycles)
    )
    sky = lax.dot_general(
        turned, jnp.where(place, 1.0, 0.0).astype(BF16), NT, preferred_element_type=F32
    )
    sky = jnp.concatenate([sky, sky], axis=1)
    lane = lax.broadcasted_iota(jnp.int32, (rows, 2 * cycles), 1)
    mode = lax.broadcasted_iota(jnp.int32, (rows, 2 * cycles), 0) & (modes - 1)
    owner = jnp.where(lane < cycles, 0, 1)
    blocks = [
        jnp.where(mode == owner + 2 * t, sky, 0.0).astype(BF16) for t in range(modes // 2)
    ]
    table = legendre_ref[...].reshape(modes * cycles, width)
    product = lax.dot_general(
        jnp.concatenate(blocks, axis=1), table, NN, preferred_element_type=F32
    )
    row_mode = lax.broadcasted_iota(jnp.int32, (rows, LANES), 0) & (modes - 1)
    column = lax.broadcasted_iota(jnp.int32, (rows, LANES), 1) - cycles
    order = jnp.sum(
        jnp.where(row_mode == column, jnp.broadcast_to(side_ref[:1, :], (rows, LANES)), 0).astype(F32),
        axis=1,
        keepdims=True,
    )
    degree = (LMAX - LW + 1 + lax.broadcasted_iota(jnp.int32, (rows, width), 1)).astype(F32)
    product = jnp.where(degree >= order, product, 0.0)
    out_ref[pl.ds(0, modes, stride=2), :] = product[:modes]
    out_ref[pl.ds(1, modes, stride=2), :] = product[modes:]


def kernel_call(kernel, out_shape, dtype=F32, scratch=(), limit=32, **options):
    return pl.pallas_call(
        kernel,
        out_shape=jax.ShapeDtypeStruct(out_shape, dtype) if dtype else out_shape,
        scratch_shapes=list(scratch),
        compiler_params=pltpu.CompilerParams(vmem_limit_bytes=limit * 1024 * 1024),
        **options,
    )


def pack_call(owners, capacity):
    return kernel_call(
        pack_kernel,
        (owners * 8, LANES),
        scratch=[
            pltpu.VMEM((owners, capacity), F32),
            pltpu.VMEM((owners, capacity), BF16),
            pltpu.VMEM((1, owners), jnp.int32),
            pltpu.VMEM((owners * 8, LANES), F32),
            pltpu.SemaphoreType.DMA((5, 4)),
        ],
        limit=60,
        in_specs=[pl.BlockSpec(memory_space=pl.ANY)] * 3,
        out_specs=pl.BlockSpec(memory_space=pl.ANY),
    )


def hits_call(planes, kernel=hits_kernel):
    outs = [
        jax.ShapeDtypeStruct((planes, ROWS, M // planes), BF16),
        jax.ShapeDtypeStruct((8, LANES), jnp.int32),
    ]
    cost = pl.CostEstimate(flops=0, transcendentals=0, bytes_accessed=2 * ROWS * M)
    return kernel_call(
        kernel,
        outs,
        None,
        scratch=[
            pltpu.VMEM((M // LANES, LANES), jnp.int32),
            pltpu.VMEM((1, 64), jnp.int32),
            pltpu.VMEM((planes, ROWS, M // planes), BF16),
            pltpu.VMEM((8, LANES), jnp.int32),
            pltpu.SemaphoreType.DMA((planes + 3,)),
        ],
        limit=60,
        cost_estimate=cost,
        in_specs=[pl.BlockSpec(memory_space=pl.ANY)] * 2,
        out_specs=[pl.BlockSpec(memory_space=pl.ANY)] * 2,
    )


def exchange(values, axes, first):
    count = lax.axis_size(axes)
    members = [(first + n) % count for n in range(count)]
    return lax.all_to_all(
        values, axes, split_axis=0, concat_axis=0, axis_index_groups=[members], tiled=True
    )


def local(positions, masses, send_counts, legendre, cycle_order, m_order):
    z = ("z_hi", "z_lo")
    cycles = cycle_order.shape[0]
    planes = lax.axis_size(z)
    capacity = positions.shape[-1]
    mode_count = legendre.shape[0]
    order_rows = m_order.reshape(M // LANES, LANES)
    packed = pack_call(cycles, capacity)(
        positions.reshape(cycles, capacity),
        masses.reshape(cycles, capacity),
        send_counts.reshape(1, cycles),
    )
    got = exchange(packed.reshape(cycles, 8, LANES), ("z_lo", "y", "x", "core"), FIRST_IN_BLOCK)
    hits, side = hits_call(planes)(order_rows, cycle_order.reshape(1, cycles))
    cycle = kernel_call(
        deposit_kernel,
        (ROWS, 2 * LANES),
        cost_estimate=pl.CostEstimate(
            flops=2 * cycles * capacity * ROWS * 2 * LANES, transcendentals=0, bytes_accessed=2**19
        ),
    )(got)
    parts = kernel_call(spectrum_kernel, (planes, 2 * M // planes // LANES, LANES), BF16)(
        cycle, order_rows, hits, *tables()
    )
    parts = parts.reshape(2 * planes, M // planes // LANES, LANES)
    got_parts = exchange(parts, z + ("core",), FIRST_ON_LINE)
    own = kernel_call(slab_sum_kernel, (cycles // 2, LANES), limit=4)(
        got_parts.reshape(planes, 2 * M // planes // LANES, LANES)
    )
    spread = exchange(own.reshape(cycles // 4, 2, LANES), ("y", "x"), FIRST_IN_PLANE)
    alm = kernel_call(product_kernel, (2 * mode_count, LW), limit=8)(
        spread.reshape(cycles // 2, LANES), side, legendre
    )
    return alm.reshape(mode_count, 2, LW)


def solution(mesh):
    cut = jax.sharding.Mesh(
        mesh.devices.reshape(8, 2, 4, 4, 2), ("z_hi", "z_lo", "y", "x", "core")
    )
    blk, pslab = ("z_hi", "z_lo", "y"), ("x", "core")
    placed = (
        P(blk, pslab, None, None),
        P(blk, pslab, None, None),
        P(blk, pslab, None),
        P(pslab + blk, None, None),
        P(),
        P(),
    )
    return jax.shard_map(
        local,
        mesh=cut,
        in_specs=placed,
        out_specs=P(pslab + blk, None, None),
        check_vma=False,
    )
```

```python
import math

import jax
import jax.numpy as jnp
import numpy as np
from jax import lax
from jax.experimental import pallas as pl
from jax.experimental.pallas import tpu as pltpu
from jax.sharding import PartitionSpec as P

CYCLE_LEN = 32768
M = 16384
LMAX = 16384
LW = 128

LANES = 128
ROWS = CYCLE_LEN // LANES
UPPER = M // ROWS
TILES = 8
SUB = LANES // TILES
COLUMNS = (TILES + 1) * SUB

FIRST_IN_BLOCK = 20
FIRST_ON_LINE = 16
FIRST_IN_PLANE = 10

F32 = jnp.float32
BF16 = jnp.bfloat16

NT = (((1,), (1,)), ((), ()))
NN = (((1,), (0,)), ((), ()))


def halves(table):
    high = table.astype(jnp.bfloat16)
    low = (table - high.astype(np.float64)).astype(jnp.bfloat16)
    return high, low


def split(values):
    high = values.astype(BF16)
    low = (values - high.astype(F32)).astype(BF16)
    return high, low


def tables():
    two_pi = 2.0 * math.pi
    rows = np.arange(ROWS)
    lanes = np.arange(LANES)
    lanes = TILES * (lanes % SUB) + lanes // SUB
    upper = np.arange(UPPER)
    angle_one = (rows[:, None] * rows[None, :] % ROWS) * (two_pi / ROWS)
    one = np.concatenate([np.cos(angle_one), -np.sin(angle_one)], axis=0)
    twist = (rows[:, None] * lanes[None, :] % CYCLE_LEN) * (two_pi / CYCLE_LEN)
    angle_two = (upper[:, None] * lanes[None, :] % LANES) * (two_pi / LANES)
    cos_two, sin_two = np.cos(angle_two), np.sin(angle_two)
    two = np.concatenate(
        [
            np.concatenate([cos_two, sin_two], axis=1),
            np.concatenate([-sin_two, cos_two], axis=1),
        ],
        axis=0,
    ) * (CYCLE_LEN ** -0.5)
    return (
        *halves(one),
        np.cos(twist).astype(np.float32),
        np.sin(twist).astype(np.float32),
        *halves(two),
    )


def spread_row(values, row, count):
    tile = jnp.broadcast_to(values[row : row + 1, :], (16, LANES)).astype(BF16)
    return jnp.concatenate([tile] * (count // 16), axis=0)


def row_ids(count):
    return lax.broadcasted_iota(jnp.int32, (count, LANES), 0).astype(F32).astype(BF16)


def pack_kernel(positions_hbm, masses_hbm, counts_hbm, out_ref, positions_ref, masses_ref, counts_ref, sems):
    owners, capacity = positions_ref.shape
    rows = 16
    chunks = owners // rows
    copies = []
    for n in range(chunks):
        part = pl.ds(n * rows, rows)
        copies.append(
            (
                pltpu.make_async_copy(positions_hbm.at[part, :], positions_ref.at[part, :], sems.at[n, 0]),
                pltpu.make_async_copy(masses_hbm.at[part, :], masses_ref.at[part, :], sems.at[n, 1]),
            )
        )
    counts_copy = pltpu.make_async_copy(counts_hbm, counts_ref, sems.at[chunks, 0])
    counts_copy.start()
    for pair in copies:
        for copy in pair:
            copy.start()
    counts_copy.wait()
    row = lax.broadcasted_iota(jnp.int32, (owners, owners), 0)
    column = lax.broadcasted_iota(jnp.int32, (owners, owners), 1)
    turned = jnp.where(row == column, jnp.broadcast_to(counts_ref[...], (owners, owners)), 0)
    counts = jnp.sum(turned.astype(F32), axis=1, keepdims=True).astype(jnp.int32)
    slots = lax.broadcasted_iota(jnp.int32, (rows, LANES), 1)
    for n in range(chunks):
        first = n * rows
        cut = min(max(FIRST_IN_BLOCK - first, 0), rows)
        pieces = [(a, b) for a, b in ((0, cut), (cut, rows)) if b > a]
        for copy in copies[n]:
            copy.wait()
        for j in range(capacity // LANES):
            cols = slice(j * LANES, (j + 1) * LANES)
            places = positions_ref[first : first + rows, cols]
            live = slots + j * LANES < counts[first : first + rows]
            weights = jnp.where(live, masses_ref[first : first + rows, cols].astype(F32), 0.0)
            for a, b in pieces:
                base = 8 * ((first + a - FIRST_IN_BLOCK) % owners)
                out_ref[pl.ds(base + j, b - a, stride=8), :] = places[a:b]
                out_ref[pl.ds(base + 4 + j, b - a, stride=8), :] = weights[a:b]


def deposit_kernel(got_ref, acc_ref):
    sources = got_ref.shape[0]
    zero = jnp.zeros((), BF16)

    def deposit():
        row_id = row_ids(ROWS)
        sub_id = lax.broadcasted_iota(jnp.int32, (SUB, LANES), 0)
        lane_ids = [(TILES * sub_id + t).astype(F32).astype(BF16) for t in range(TILES)]
        highs, lows = [], []
        for s in range(sources):
            tile = got_ref[s]
            places, mass = tile[0:4], tile[4:8]
            floored = jnp.floor(places)
            fraction = places - floored
            pixel = floored.astype(jnp.int32) & (CYCLE_LEN - 1)
            high = (pixel >> 7).astype(F32)
            low = (pixel & (LANES - 1)).astype(F32)
            near = 1.0 - fraction
            for r in range(4):
                highs.append(
                    jnp.where(spread_row(high, r, ROWS) == row_id, spread_row(mass, r, ROWS), zero)
                )
                low_r, near_r, far_r = (spread_row(v, r, SUB) for v in (low, near, fraction))
                hits = [low_r == lane_id for lane_id in lane_ids]
                tiles = [jnp.where(hits[0], near_r, zero)]
                for t in range(1, TILES):
                    tiles.append(jnp.where(hits[t], near_r, jnp.where(hits[t - 1], far_r, zero)))
                tiles.append(jnp.where(hits[-1], far_r, zero))
                lows.append(jnp.concatenate(tiles, axis=0))
        return lax.dot_general(
            jnp.concatenate(highs, axis=1),
            jnp.concatenate(lows, axis=1),
            NT,
            preferred_element_type=F32,
        )

    acc_ref[:, LANES:] = jnp.zeros((ROWS, LANES), F32)
    acc_ref[:, :COLUMNS] = deposit()


def hits_kernel(
    order_hbm, places_hbm, out_hbm, side_hbm, order_ref, places_ref, out_ref, side_ref, sems, block=None
):
    if block is None:
        block = lax.axis_index(("x", "core", "z_hi", "z_lo", "y"))
    zero, one = jnp.zeros((), BF16), jnp.ones((), BF16)
    planes = order_ref.shape[0] // 8
    cycles = places_ref.shape[1]
    order_copy = pltpu.make_async_copy(order_hbm, order_ref, sems.at[planes])
    places_copy = pltpu.make_async_copy(places_hbm, places_ref, sems.at[planes + 1])
    side_copy = pltpu.make_async_copy(side_ref, side_hbm, sems.at[planes + 2])
    out_copies = [
        pltpu.make_async_copy(out_ref.at[k], out_hbm.at[k], sems.at[k]) for k in range(planes)
    ]
    order_copy.start()
    places_copy.start()
    order_copy.wait()
    places_copy.wait()

    ids = row_ids(ROWS)
    for k in range(planes):
        lower = (order_ref[pl.ds(k, 8, stride=planes), :] & (ROWS - 1)).astype(F32)
        hits = [jnp.where(spread_row(lower, r, ROWS) == ids, one, zero) for r in range(8)]
        out_ref[k] = jnp.concatenate(hits, axis=1)
        out_copies[k].start()

    row = lax.broadcasted_iota(jnp.int32, (cycles, cycles), 0)
    column = lax.broadcasted_iota(jnp.int32, (cycles, cycles), 1)
    half = cycles // 2
    taken = jnp.where(row == 2 * (column % half) + column // half, 1.0, 0.0).astype(BF16)
    places = jnp.broadcast_to(places_ref[...], (16, cycles)).astype(F32).astype(BF16)
    places = lax.dot_general(places, taken, NN, preferred_element_type=F32)[:8].astype(jnp.int32)
    own = jnp.broadcast_to(order_ref[pl.ds(block // 4, 1), :], side_ref.shape)
    own = pltpu.roll(own, lax.rem(LANES + cycles - lax.rem(block, 4) * 32, LANES), 1)
    side_lane = lax.broadcasted_iota(jnp.int32, side_ref.shape, 1)
    side_ref[...] = jnp.where(side_lane < cycles, jnp.concatenate([places, places], axis=1), own)
    side_copy.start()
    for copy in out_copies:
        copy.wait()
    side_copy.wait()


def spectrum_kernel(
    acc_ref, order_ref, hits_ref, one_h_ref, one_l_ref, cos_ref, sin_ref, two_h_ref, two_l_ref, out_ref
):
    beyond = acc_ref[:, LANES:]
    column = lax.broadcasted_iota(jnp.int32, (ROWS, LANES), 1)
    next_row = pltpu.roll(pltpu.roll(beyond, LANES - SUB + 1, 1), 1, 0)
    cycle = acc_ref[:, :LANES] + jnp.where(
        column == 0, next_row, jnp.where(column < SUB, pltpu.roll(beyond, 1, 1), 0.0)
    )

    def dot(a, b, dims):
        return lax.dot_general(a, b, dims, preferred_element_type=F32)

    cycle_h, cycle_l = split(cycle)
    both = dot(one_h_ref[...], jnp.concatenate([cycle_h, cycle_l], axis=1), NN)
    first = both[:, :LANES] + (both[:, LANES:] + dot(one_l_ref[...], cycle_h, NN))
    real, imag = first[:ROWS], first[ROWS:]
    cos, sin = cos_ref[...], sin_ref[...]
    twisted = jnp.concatenate([real * cos + imag * sin, imag * cos - real * sin], axis=1)
    twisted_h, twisted_l = split(twisted)
    spectrum = (
        dot(two_h_ref[...], twisted_l, NT)
        + dot(two_l_ref[...], twisted_h, NT)
        + dot(two_h_ref[...], twisted_h, NT)
    )
    spectrum = spectrum.astype(BF16)
    upper_ids = lax.broadcasted_iota(jnp.int32, (UPPER, LANES), 0)
    planes = out_ref.shape[0]
    for k in range(planes):
        upper = order_ref[pl.ds(k, 8, stride=planes), :] >> 8
        picked = dot(spectrum, hits_ref[k], NN)
        reals, imags = [], []
        for r in range(8):
            cols = slice(r * LANES, (r + 1) * LANES)
            mine = jnp.broadcast_to(upper[r : r + 1, :], (UPPER, LANES)) == upper_ids
            reals.append(jnp.sum(jnp.where(mine, picked[:UPPER, cols], 0.0), axis=0, keepdims=True))
            imags.append(jnp.sum(jnp.where(mine, picked[UPPER:, cols], 0.0), axis=0, keepdims=True))
        rows = reals[::2] + imags[::2] + reals[1::2] + imags[1::2]
        out_ref[(k - FIRST_ON_LINE // 2) % planes] = jnp.concatenate(rows, axis=0).astype(BF16)


def slab_sum_kernel(parts_ref, out_ref):
    z_count = parts_ref.shape[0]
    quarter = lax.broadcasted_iota(jnp.int32, (4, LANES), 1) // 32
    for z_lo in range(2):
        total = parts_ref[z_lo].astype(F32)
        for z in range(z_lo + 2, z_count, 2):
            total = total + parts_ref[z].astype(F32)
        for y in range(4):
            row = jnp.zeros((4, LANES), F32)
            for n in range(4):
                shift = (n - y) % 4 * 32
                values = pltpu.roll(total, shift, 1) if shift else total
                row = jnp.where(quarter == n, values[4 * n : 4 * n + 4], row)
            for x in range(4):
                chip = (4 * y + x - FIRST_IN_PLANE) % 16
                out_ref[pl.ds(2 * chip + z_lo, 1), :] = row[x : x + 1]


def product_kernel(got_ref, side_ref, legendre_ref, out_ref):
    modes, cycles, width = legendre_ref.shape
    rows = 2 * modes
    before = FIRST_IN_PLANE
    got = []
    for z_lo in range(2):
        got.append(got_ref[pl.ds(2 * (16 - before) + z_lo, before, stride=2), :])
        got.append(got_ref[pl.ds(z_lo, 16 - before, stride=2), :])
    got = jnp.concatenate(got, axis=0)
    turned = jnp.transpose(got)
    turned = jnp.concatenate([turned[:rows], turned[rows:]], axis=1).astype(BF16)
    place = lax.broadcasted_iota(jnp.int32, (cycles, cycles), 0) == jnp.broadcast_to(
        side_ref[:1, :cycles], (cycles, cycles)
    )
    sky = lax.dot_general(
        turned, jnp.where(place, 1.0, 0.0).astype(BF16), NT, preferred_element_type=F32
    )
    sky = jnp.concatenate([sky, sky], axis=1)
    lane = lax.broadcasted_iota(jnp.int32, (rows, 2 * cycles), 1)
    mode = lax.broadcasted_iota(jnp.int32, (rows, 2 * cycles), 0) & (modes - 1)
    owner = jnp.where(lane < cycles, 0, 1)
    blocks = [
        jnp.where(mode == owner + 2 * t, sky, 0.0).astype(BF16) for t in range(modes // 2)
    ]
    table = legendre_ref[...].reshape(modes * cycles, width)
    product = lax.dot_general(
        jnp.concatenate(blocks, axis=1), table, NN, preferred_element_type=F32
    )
    row_mode = lax.broadcasted_iota(jnp.int32, (rows, LANES), 0) & (modes - 1)
    column = lax.broadcasted_iota(jnp.int32, (rows, LANES), 1) - cycles
    order = jnp.sum(
        jnp.where(row_mode == column, jnp.broadcast_to(side_ref[:1, :], (rows, LANES)), 0).astype(F32),
        axis=1,
        keepdims=True,
    )
    degree = (LMAX - LW + 1 + lax.broadcasted_iota(jnp.int32, (rows, width), 1)).astype(F32)
    product = jnp.where(degree >= order, product, 0.0)
    out_ref[pl.ds(0, modes, stride=2), :] = product[:modes]
    out_ref[pl.ds(1, modes, stride=2), :] = product[modes:]


def kernel_call(kernel, out_shape, dtype=F32, scratch=(), limit=32, **options):
    return pl.pallas_call(
        kernel,
        out_shape=jax.ShapeDtypeStruct(out_shape, dtype) if dtype else out_shape,
        scratch_shapes=list(scratch),
        compiler_params=pltpu.CompilerParams(vmem_limit_bytes=limit * 1024 * 1024),
        **options,
    )


def pack_call(owners, capacity):
    return kernel_call(
        pack_kernel,
        (owners * 8, LANES),
        scratch=[
            pltpu.VMEM((owners, capacity), F32),
            pltpu.VMEM((owners, capacity), BF16),
            pltpu.VMEM((1, owners), jnp.int32),
            pltpu.SemaphoreType.DMA((5, 2)),
        ],
        limit=4,
        in_specs=[pl.BlockSpec(memory_space=pl.ANY)] * 3,
    )


def hits_call(planes, kernel=hits_kernel):
    outs = [
        jax.ShapeDtypeStruct((planes, ROWS, M // planes), BF16),
        jax.ShapeDtypeStruct((8, LANES), jnp.int32),
    ]
    cost = pl.CostEstimate(flops=0, transcendentals=0, bytes_accessed=2 * ROWS * M)
    return kernel_call(
        kernel,
        outs,
        None,
        scratch=[
            pltpu.VMEM((M // LANES, LANES), jnp.int32),
            pltpu.VMEM((1, 64), jnp.int32),
            pltpu.VMEM((planes, ROWS, M // planes), BF16),
            pltpu.VMEM((8, LANES), jnp.int32),
            pltpu.SemaphoreType.DMA((planes + 3,)),
        ],
        limit=60,
        cost_estimate=cost,
        in_specs=[pl.BlockSpec(memory_space=pl.ANY)] * 2,
        out_specs=[pl.BlockSpec(memory_space=pl.ANY)] * 2,
    )


def exchange(values, axes, first):
    count = lax.axis_size(axes)
    members = [(first + n) % count for n in range(count)]
    return lax.all_to_all(
        values, axes, split_axis=0, concat_axis=0, axis_index_groups=[members], tiled=True
    )


def local(positions, masses, send_counts, legendre, cycle_order, m_order):
    z = ("z_hi", "z_lo")
    cycles = cycle_order.shape[0]
    planes = lax.axis_size(z)
    capacity = positions.shape[-1]
    mode_count = legendre.shape[0]
    order_rows = m_order.reshape(M // LANES, LANES)
    particles = (
        positions.reshape(cycles, capacity),
        masses.reshape(cycles, capacity),
        send_counts.reshape(1, cycles),
    )
    packed = pack_call(cycles, capacity)(
        *(pltpu.with_memory_space_constraint(value, pltpu.HBM) for value in particles)
    )
    got = exchange(packed.reshape(cycles, 8, LANES), ("z_lo", "y", "x", "core"), FIRST_IN_BLOCK)
    hits, side = hits_call(planes)(order_rows, cycle_order.reshape(1, cycles))
    cycle = kernel_call(
        deposit_kernel,
        (ROWS, 2 * LANES),
        cost_estimate=pl.CostEstimate(
            flops=2 * cycles * capacity * ROWS * 2 * LANES, transcendentals=0, bytes_accessed=2**19
        ),
    )(got)
    parts = kernel_call(spectrum_kernel, (planes, 2 * M // planes // LANES, LANES), BF16)(
        cycle, order_rows, hits, *tables()
    )
    parts = parts.reshape(2 * planes, M // planes // LANES, LANES)
    got_parts = exchange(parts, z + ("core",), FIRST_ON_LINE)
    own = kernel_call(slab_sum_kernel, (cycles // 2, LANES), limit=4)(
        got_parts.reshape(planes, 2 * M // planes // LANES, LANES)
    )
    spread = exchange(own.reshape(cycles // 4, 2, LANES), ("y", "x"), FIRST_IN_PLANE)
    alm = kernel_call(product_kernel, (2 * mode_count, LW), limit=8)(
        spread.reshape(cycles // 2, LANES), side, legendre
    )
    return alm.reshape(mode_count, 2, LW)


def solution(mesh):
    cut = jax.sharding.Mesh(
        mesh.devices.reshape(8, 2, 4, 4, 2), ("z_hi", "z_lo", "y", "x", "core")
    )
    blk, pslab = ("z_hi", "z_lo", "y"), ("x", "core")
    placed = (
        P(blk, pslab, None, None),
        P(blk, pslab, None, None),
        P(blk, pslab, None),
        P(pslab + blk, None, None),
        P(),
        P(),
    )
    return jax.shard_map(
        local,
        mesh=cut,
        in_specs=placed,
        out_specs=P(pslab + blk, None, None),
        check_vma=False,
    )
```

```python
import math

import jax
import jax.numpy as jnp
import numpy as np
from jax import lax
from jax.experimental import pallas as pl
from jax.experimental.pallas import tpu as pltpu
from jax.sharding import PartitionSpec as P

CYCLE_LEN = 32768
M = 16384
LMAX = 16384
LW = 128

LANES = 128
ROWS = CYCLE_LEN // LANES
UPPER = M // ROWS
TILES = 8
SUB = LANES // TILES
COLUMNS = (TILES + 1) * SUB

FIRST_IN_BLOCK = 20
FIRST_ON_LINE = 10
FIRST_IN_PLANE = 10

F32 = jnp.float32
BF16 = jnp.bfloat16

NT = (((1,), (1,)), ((), ()))
NN = (((1,), (0,)), ((), ()))


def halves(table):
    high = table.astype(jnp.bfloat16)
    low = (table - high.astype(np.float64)).astype(jnp.bfloat16)
    return high, low


def split(values):
    high = values.astype(BF16)
    low = (values - high.astype(F32)).astype(BF16)
    return high, low


def tables():
    two_pi = 2.0 * math.pi
    rows = np.arange(ROWS)
    lanes = np.arange(LANES)
    lanes = TILES * (lanes % SUB) + lanes // SUB
    upper = np.arange(UPPER)
    angle_one = (rows[:, None] * rows[None, :] % ROWS) * (two_pi / ROWS)
    one = np.concatenate([np.cos(angle_one), -np.sin(angle_one)], axis=0)
    twist = (rows[:, None] * lanes[None, :] % CYCLE_LEN) * (two_pi / CYCLE_LEN)
    angle_two = (upper[:, None] * lanes[None, :] % LANES) * (two_pi / LANES)
    cos_two, sin_two = np.cos(angle_two), np.sin(angle_two)
    two = np.concatenate(
        [
            np.concatenate([cos_two, sin_two], axis=1),
            np.concatenate([-sin_two, cos_two], axis=1),
        ],
        axis=0,
    ) * (CYCLE_LEN ** -0.5)
    return (
        *halves(one),
        np.cos(twist).astype(np.float32),
        np.sin(twist).astype(np.float32),
        *halves(two),
    )


def spread_row(values, row, count):
    tile = jnp.broadcast_to(values[row : row + 1, :], (16, LANES)).astype(BF16)
    return jnp.concatenate([tile] * (count // 16), axis=0)


def row_ids(count):
    return lax.broadcasted_iota(jnp.int32, (count, LANES), 0).astype(F32).astype(BF16)


def pack_kernel(positions_hbm, masses_hbm, counts_hbm, out_hbm, positions_ref, masses_ref, counts_ref, out_ref, sems):
    owners, capacity = positions_ref.shape
    rows = 16
    chunks = owners // rows
    in_copies, out_copies = [], []
    for n in range(chunks):
        part = pl.ds(n * rows, rows)
        in_copies.append(
            (
                pltpu.make_async_copy(positions_hbm.at[part, :], positions_ref.at[part, :], sems.at[n, 0]),
                pltpu.make_async_copy(masses_hbm.at[part, :], masses_ref.at[part, :], sems.at[n, 1]),
            )
        )
        cuts = sorted({n * rows, min(max(FIRST_IN_BLOCK, n * rows), (n + 1) * rows), (n + 1) * rows})
        out_copies.append(
            [
                pltpu.make_async_copy(
                    out_ref.at[pl.ds(8 * a, 8 * (b - a)), :],
                    out_hbm.at[pl.ds(8 * ((a - FIRST_IN_BLOCK) % owners), 8 * (b - a)), :],
                    sems.at[n, 2 + m],
                )
                for m, (a, b) in enumerate(zip(cuts, cuts[1:]))
            ]
        )
    counts_copy = pltpu.make_async_copy(counts_hbm, counts_ref, sems.at[chunks, 0])
    counts_copy.start()
    for copies in in_copies:
        for copy in copies:
            copy.start()
    counts_copy.wait()
    row = lax.broadcasted_iota(jnp.int32, (owners, owners), 0)
    column = lax.broadcasted_iota(jnp.int32, (owners, owners), 1)
    turned = jnp.where(row == column, jnp.broadcast_to(counts_ref[...], (owners, owners)), 0)
    counts = jnp.sum(turned.astype(F32), axis=1, keepdims=True).astype(jnp.int32)
    slots = lax.broadcasted_iota(jnp.int32, (rows, LANES), 1)
    for n in range(chunks):
        first = n * rows
        for copy in in_copies[n]:
            copy.wait()
        for j in range(capacity // LANES):
            cols = slice(j * LANES, (j + 1) * LANES)
            out_ref[pl.ds(first * 8 + j, rows, stride=8), :] = positions_ref[first : first + rows, cols]
            live = slots + j * LANES < counts[first : first + rows]
            out_ref[pl.ds(first * 8 + 4 + j, rows, stride=8), :] = jnp.where(
                live, masses_ref[first : first + rows, cols].astype(F32), 0.0
            )
        for copy in out_copies[n]:
            copy.start()
    for copies in out_copies:
        for copy in copies:
            copy.wait()


def deposit_kernel(got_ref, acc_ref):
    sources = got_ref.shape[0]
    zero = jnp.zeros((), BF16)

    def deposit():
        row_id = row_ids(ROWS)
        sub_id = lax.broadcasted_iota(jnp.int32, (SUB, LANES), 0)
        lane_ids = [(TILES * sub_id + t).astype(F32).astype(BF16) for t in range(TILES)]
        highs, lows = [], []
        for s in range(sources):
            tile = got_ref[s]
            places, mass = tile[0:4], tile[4:8]
            floored = jnp.floor(places)
            fraction = places - floored
            pixel = floored.astype(jnp.int32) & (CYCLE_LEN - 1)
            high = (pixel >> 7).astype(F32)
            low = (pixel & (LANES - 1)).astype(F32)
            near = 1.0 - fraction
            for r in range(4):
                highs.append(
                    jnp.where(spread_row(high, r, ROWS) == row_id, spread_row(mass, r, ROWS), zero)
                )
                low_r, near_r, far_r = (spread_row(v, r, SUB) for v in (low, near, fraction))
                hits = [low_r == lane_id for lane_id in lane_ids]
                tiles = [jnp.where(hits[0], near_r, zero)]
                for t in range(1, TILES):
                    tiles.append(jnp.where(hits[t], near_r, jnp.where(hits[t - 1], far_r, zero)))
                tiles.append(jnp.where(hits[-1], far_r, zero))
                lows.append(jnp.concatenate(tiles, axis=0))
        return lax.dot_general(
            jnp.concatenate(highs, axis=1),
            jnp.concatenate(lows, axis=1),
            NT,
            preferred_element_type=F32,
        )

    acc_ref[:, LANES:] = jnp.zeros((ROWS, LANES), F32)
    acc_ref[:, :COLUMNS] = deposit()


def hits_kernel(
    order_hbm, places_hbm, out_hbm, side_hbm, order_ref, places_ref, out_ref, side_ref, sems, block=None
):
    if block is None:
        block = lax.axis_index(("x", "core", "z_hi", "z_lo", "y"))
    zero, one = jnp.zeros((), BF16), jnp.ones((), BF16)
    planes = order_ref.shape[0] // 8
    cycles = places_ref.shape[1]
    order_copy = pltpu.make_async_copy(order_hbm, order_ref, sems.at[planes])
    places_copy = pltpu.make_async_copy(places_hbm, places_ref, sems.at[planes + 1])
    side_copy = pltpu.make_async_copy(side_ref, side_hbm, sems.at[planes + 2])
    out_copies = [
        pltpu.make_async_copy(out_ref.at[k], out_hbm.at[k], sems.at[k]) for k in range(planes)
    ]
    order_copy.start()
    places_copy.start()
    order_copy.wait()
    places_copy.wait()

    ids = row_ids(ROWS)
    for k in range(planes):
        lower = (order_ref[pl.ds(k, 8, stride=planes), :] & (ROWS - 1)).astype(F32)
        hits = [jnp.where(spread_row(lower, r, ROWS) == ids, one, zero) for r in range(8)]
        out_ref[k] = jnp.concatenate(hits, axis=1)
        out_copies[k].start()

    row = lax.broadcasted_iota(jnp.int32, (cycles, cycles), 0)
    column = lax.broadcasted_iota(jnp.int32, (cycles, cycles), 1)
    half = cycles // 2
    taken = jnp.where(row == 2 * (column % half) + column // half, 1.0, 0.0).astype(BF16)
    places = jnp.broadcast_to(places_ref[...], (16, cycles)).astype(F32).astype(BF16)
    places = lax.dot_general(places, taken, NN, preferred_element_type=F32)[:8].astype(jnp.int32)
    own = jnp.broadcast_to(order_ref[pl.ds(block // 4, 1), :], side_ref.shape)
    own = pltpu.roll(own, lax.rem(LANES + cycles - lax.rem(block, 4) * 32, LANES), 1)
    side_lane = lax.broadcasted_iota(jnp.int32, side_ref.shape, 1)
    side_ref[...] = jnp.where(side_lane < cycles, jnp.concatenate([places, places], axis=1), own)
    side_copy.start()
    for copy in out_copies:
        copy.wait()
    side_copy.wait()


def spectrum_kernel(
    acc_ref, order_ref, hits_ref, one_h_ref, one_l_ref, cos_ref, sin_ref, two_h_ref, two_l_ref, out_ref
):
    beyond = acc_ref[:, LANES:]
    column = lax.broadcasted_iota(jnp.int32, (ROWS, LANES), 1)
    next_row = pltpu.roll(pltpu.roll(beyond, LANES - SUB + 1, 1), 1, 0)
    cycle = acc_ref[:, :LANES] + jnp.where(
        column == 0, next_row, jnp.where(column < SUB, pltpu.roll(beyond, 1, 1), 0.0)
    )

    def dot(a, b, dims):
        return lax.dot_general(a, b, dims, preferred_element_type=F32)

    cycle_h, cycle_l = split(cycle)
    both = dot(one_h_ref[...], jnp.concatenate([cycle_h, cycle_l], axis=1), NN)
    first = both[:, :LANES] + (both[:, LANES:] + dot(one_l_ref[...], cycle_h, NN))
    real, imag = first[:ROWS], first[ROWS:]
    cos, sin = cos_ref[...], sin_ref[...]
    twisted = jnp.concatenate([real * cos + imag * sin, imag * cos - real * sin], axis=1)
    twisted_h, twisted_l = split(twisted)
    spectrum = (
        dot(two_h_ref[...], twisted_l, NT)
        + dot(two_l_ref[...], twisted_h, NT)
        + dot(two_h_ref[...], twisted_h, NT)
    )
    spectrum = spectrum.astype(BF16)
    upper_ids = lax.broadcasted_iota(jnp.int32, (UPPER, LANES), 0)
    planes = out_ref.shape[0]
    for k in range(planes):
        upper = order_ref[pl.ds(k, 8, stride=planes), :] >> 8
        picked = dot(spectrum, hits_ref[k], NN)
        reals, imags = [], []
        for r in range(8):
            cols = slice(r * LANES, (r + 1) * LANES)
            mine = jnp.broadcast_to(upper[r : r + 1, :], (UPPER, LANES)) == upper_ids
            reals.append(jnp.sum(jnp.where(mine, picked[:UPPER, cols], 0.0), axis=0, keepdims=True))
            imags.append(jnp.sum(jnp.where(mine, picked[UPPER:, cols], 0.0), axis=0, keepdims=True))
        rows = reals[::2] + imags[::2] + reals[1::2] + imags[1::2]
        out_ref[(FIRST_ON_LINE - k) % planes] = jnp.concatenate(rows, axis=0).astype(BF16)


def slab_sum_kernel(parts_ref, out_ref):
    z_count = parts_ref.shape[0]
    quarter = lax.broadcasted_iota(jnp.int32, (4, LANES), 1) // 32
    for z_lo in range(2):
        total = parts_ref[z_lo].astype(F32)
        for z in range(z_lo + 2, z_count, 2):
            total = total + parts_ref[z].astype(F32)
        for y in range(4):
            row = jnp.zeros((4, LANES), F32)
            for n in range(4):
                shift = (n - y) % 4 * 32
                values = pltpu.roll(total, shift, 1) if shift else total
                row = jnp.where(quarter == n, values[4 * n : 4 * n + 4], row)
            for x in range(4):
                chip = (4 * y + x - FIRST_IN_PLANE) % 16
                out_ref[pl.ds(2 * chip + z_lo, 1), :] = row[x : x + 1]


def product_kernel(got_ref, side_ref, legendre_ref, out_ref):
    modes, cycles, width = legendre_ref.shape
    rows = 2 * modes
    before = FIRST_IN_PLANE
    got = []
    for z_lo in range(2):
        got.append(got_ref[pl.ds(2 * (16 - before) + z_lo, before, stride=2), :])
        got.append(got_ref[pl.ds(z_lo, 16 - before, stride=2), :])
    got = jnp.concatenate(got, axis=0)
    turned = jnp.transpose(got)
    turned = jnp.concatenate([turned[:rows], turned[rows:]], axis=1).astype(BF16)
    place = lax.broadcasted_iota(jnp.int32, (cycles, cycles), 0) == jnp.broadcast_to(
        side_ref[:1, :cycles], (cycles, cycles)
    )
    sky = lax.dot_general(
        turned, jnp.where(place, 1.0, 0.0).astype(BF16), NT, preferred_element_type=F32
    )
    sky = jnp.concatenate([sky, sky], axis=1)
    lane = lax.broadcasted_iota(jnp.int32, (rows, 2 * cycles), 1)
    mode = lax.broadcasted_iota(jnp.int32, (rows, 2 * cycles), 0) & (modes - 1)
    owner = jnp.where(lane < cycles, 0, 1)
    blocks = [
        jnp.where(mode == owner + 2 * t, sky, 0.0).astype(BF16) for t in range(modes // 2)
    ]
    table = legendre_ref[...].reshape(modes * cycles, width)
    product = lax.dot_general(
        jnp.concatenate(blocks, axis=1), table, NN, preferred_element_type=F32
    )
    row_mode = lax.broadcasted_iota(jnp.int32, (rows, LANES), 0) & (modes - 1)
    column = lax.broadcasted_iota(jnp.int32, (rows, LANES), 1) - cycles
    order = jnp.sum(
        jnp.where(row_mode == column, jnp.broadcast_to(side_ref[:1, :], (rows, LANES)), 0).astype(F32),
        axis=1,
        keepdims=True,
    )
    degree = (LMAX - LW + 1 + lax.broadcasted_iota(jnp.int32, (rows, width), 1)).astype(F32)
    product = jnp.where(degree >= order, product, 0.0)
    out_ref[pl.ds(0, modes, stride=2), :] = product[:modes]
    out_ref[pl.ds(1, modes, stride=2), :] = product[modes:]


def kernel_call(kernel, out_shape, dtype=F32, scratch=(), limit=32, **options):
    return pl.pallas_call(
        kernel,
        out_shape=jax.ShapeDtypeStruct(out_shape, dtype) if dtype else out_shape,
        scratch_shapes=list(scratch),
        compiler_params=pltpu.CompilerParams(vmem_limit_bytes=limit * 1024 * 1024),
        **options,
    )


def pack_call(owners, capacity):
    return kernel_call(
        pack_kernel,
        (owners * 8, LANES),
        scratch=[
            pltpu.VMEM((owners, capacity), F32),
            pltpu.VMEM((owners, capacity), BF16),
            pltpu.VMEM((1, owners), jnp.int32),
            pltpu.VMEM((owners * 8, LANES), F32),
            pltpu.SemaphoreType.DMA((5, 4)),
        ],
        limit=60,
        in_specs=[pl.BlockSpec(memory_space=pl.ANY)] * 3,
        out_specs=pl.BlockSpec(memory_space=pl.ANY),
    )


def hits_call(planes, kernel=hits_kernel):
    outs = [
        jax.ShapeDtypeStruct((planes, ROWS, M // planes), BF16),
        jax.ShapeDtypeStruct((8, LANES), jnp.int32),
    ]
    cost = pl.CostEstimate(flops=0, transcendentals=0, bytes_accessed=2 * ROWS * M)
    return kernel_call(
        kernel,
        outs,
        None,
        scratch=[
            pltpu.VMEM((M // LANES, LANES), jnp.int32),
            pltpu.VMEM((1, 64), jnp.int32),
            pltpu.VMEM((planes, ROWS, M // planes), BF16),
            pltpu.VMEM((8, LANES), jnp.int32),
            pltpu.SemaphoreType.DMA((planes + 3,)),
        ],
        limit=60,
        cost_estimate=cost,
        in_specs=[pl.BlockSpec(memory_space=pl.ANY)] * 2,
        out_specs=[pl.BlockSpec(memory_space=pl.ANY)] * 2,
    )


def members_from(first, count):
    return [(first + n) % count for n in range(count)]


def exchange(values, axes, members):
    return lax.all_to_all(
        values, axes, split_axis=0, concat_axis=0, axis_index_groups=[members], tiled=True
    )


def local(positions, masses, send_counts, legendre, cycle_order, m_order):
    z = ("z_hi", "z_lo")
    cycles = cycle_order.shape[0]
    planes = lax.axis_size(z)
    capacity = positions.shape[-1]
    mode_count = legendre.shape[0]
    order_rows = m_order.reshape(M // LANES, LANES)
    packed = pack_call(cycles, capacity)(
        positions.reshape(cycles, capacity),
        masses.reshape(cycles, capacity),
        send_counts.reshape(1, cycles),
    )
    got = exchange(packed.reshape(cycles, 8, LANES), ("z_lo", "y", "x", "core"), members_from(FIRST_IN_BLOCK, cycles))
    hits, side = hits_call(planes)(order_rows, cycle_order.reshape(1, cycles))
    cycle = kernel_call(
        deposit_kernel,
        (ROWS, 2 * LANES),
        cost_estimate=pl.CostEstimate(
            flops=2 * cycles * capacity * ROWS * 2 * LANES, transcendentals=0, bytes_accessed=2**19
        ),
    )(got)
    parts = kernel_call(spectrum_kernel, (planes, 2 * M // planes // LANES, LANES), BF16)(
        cycle, order_rows, hits, *tables()
    )
    parts = parts.reshape(2 * planes, M // planes // LANES, LANES)
    line = [(FIRST_ON_LINE - n) % planes * 2 + core for n in range(planes) for core in range(2)]
    got_parts = exchange(parts, z + ("core",), line)
    own = kernel_call(slab_sum_kernel, (cycles // 2, LANES), limit=4)(
        got_parts.reshape(planes, 2 * M // planes // LANES, LANES)
    )
    spread = exchange(own.reshape(cycles // 4, 2, LANES), ("y", "x"), members_from(FIRST_IN_PLANE, cycles // 4))
    alm = kernel_call(product_kernel, (2 * mode_count, LW), limit=8)(
        spread.reshape(cycles // 2, LANES), side, legendre
    )
    return alm.reshape(mode_count, 2, LW)


def solution(mesh):
    cut = jax.sharding.Mesh(
        mesh.devices.reshape(8, 2, 4, 4, 2), ("z_hi", "z_lo", "y", "x", "core")
    )
    blk, pslab = ("z_hi", "z_lo", "y"), ("x", "core")
    placed = (
        P(blk, pslab, None, None),
        P(blk, pslab, None, None),
        P(blk, pslab, None),
        P(pslab + blk, None, None),
        P(),
        P(),
    )
    return jax.shard_map(
        local,
        mesh=cut,
        in_specs=placed,
        out_specs=P(pslab + blk, None, None),
        check_vma=False,
    )
```

```python
import math

import jax
import jax.numpy as jnp
import numpy as np
from jax import lax
from jax.experimental import pallas as pl
from jax.experimental.pallas import tpu as pltpu
from jax.sharding import PartitionSpec as P

CYCLE_LEN = 32768
M = 16384
LMAX = 16384
LW = 128

LANES = 128
ROWS = CYCLE_LEN // LANES
UPPER = M // ROWS
TILES = 8
SUB = LANES // TILES
COLUMNS = (TILES + 1) * SUB

FIRST_IN_BLOCK = 20
FIRST_ON_LINE = 10
FIRST_IN_PLANE = 10

F32 = jnp.float32
BF16 = jnp.bfloat16

NT = (((1,), (1,)), ((), ()))
NN = (((1,), (0,)), ((), ()))


def halves(table):
    high = table.astype(jnp.bfloat16)
    low = (table - high.astype(np.float64)).astype(jnp.bfloat16)
    return high, low


def split(values):
    high = values.astype(BF16)
    low = (values - high.astype(F32)).astype(BF16)
    return high, low


def tables():
    two_pi = 2.0 * math.pi
    rows = np.arange(ROWS)
    lanes = np.arange(LANES)
    lanes = TILES * (lanes % SUB) + lanes // SUB
    upper = np.arange(UPPER)
    angle_one = (rows[:, None] * rows[None, :] % ROWS) * (two_pi / ROWS)
    one = np.concatenate([np.cos(angle_one), -np.sin(angle_one)], axis=0)
    twist = (rows[:, None] * lanes[None, :] % CYCLE_LEN) * (two_pi / CYCLE_LEN)
    angle_two = (upper[:, None] * lanes[None, :] % LANES) * (two_pi / LANES)
    cos_two, sin_two = np.cos(angle_two), np.sin(angle_two)
    two = np.concatenate(
        [
            np.concatenate([cos_two, sin_two], axis=1),
            np.concatenate([-sin_two, cos_two], axis=1),
        ],
        axis=0,
    ) * (CYCLE_LEN ** -0.5)
    return (
        *halves(one),
        np.cos(twist).astype(np.float32),
        np.sin(twist).astype(np.float32),
        *halves(two),
    )


def spread_row(values, row, count):
    tile = jnp.broadcast_to(values[row : row + 1, :], (16, LANES)).astype(BF16)
    return jnp.concatenate([tile] * (count // 16), axis=0)


def row_ids(count):
    return lax.broadcasted_iota(jnp.int32, (count, LANES), 0).astype(F32).astype(BF16)


def pack_kernel(positions_hbm, masses_hbm, counts_hbm, out_ref, positions_ref, masses_ref, counts_ref, sems):
    owners, capacity = positions_ref.shape
    rows = 16
    chunks = owners // rows
    copies = []
    for n in range(chunks):
        part = pl.ds(n * rows, rows)
        copies.append(
            (
                pltpu.make_async_copy(positions_hbm.at[part, :], positions_ref.at[part, :], sems.at[n, 0]),
                pltpu.make_async_copy(masses_hbm.at[part, :], masses_ref.at[part, :], sems.at[n, 1]),
            )
        )
    counts_copy = pltpu.make_async_copy(counts_hbm, counts_ref, sems.at[chunks, 0])
    counts_copy.start()
    for pair in copies:
        for copy in pair:
            copy.start()
    counts_copy.wait()
    row = lax.broadcasted_iota(jnp.int32, (owners, owners), 0)
    column = lax.broadcasted_iota(jnp.int32, (owners, owners), 1)
    turned = jnp.where(row == column, jnp.broadcast_to(counts_ref[...], (owners, owners)), 0)
    counts = jnp.sum(turned.astype(F32), axis=1, keepdims=True).astype(jnp.int32)
    slots = lax.broadcasted_iota(jnp.int32, (rows, LANES), 1)
    for n in range(chunks):
        first = n * rows
        cut = min(max(FIRST_IN_BLOCK - first, 0), rows)
        pieces = [(a, b) for a, b in ((0, cut), (cut, rows)) if b > a]
        for copy in copies[n]:
            copy.wait()
        for j in range(capacity // LANES):
            cols = slice(j * LANES, (j + 1) * LANES)
            places = positions_ref[first : first + rows, cols]
            live = slots + j * LANES < counts[first : first + rows]
            weights = jnp.where(live, masses_ref[first : first + rows, cols].astype(F32), 0.0)
            for a, b in pieces:
                base = 8 * ((first + a - FIRST_IN_BLOCK) % owners)
                out_ref[pl.ds(base + j, b - a, stride=8), :] = places[a:b]
                out_ref[pl.ds(base + 4 + j, b - a, stride=8), :] = weights[a:b]


def deposit_kernel(got_ref, acc_ref):
    sources = got_ref.shape[0]
    zero = jnp.zeros((), BF16)

    def deposit():
        row_id = row_ids(ROWS)
        sub_id = lax.broadcasted_iota(jnp.int32, (SUB, LANES), 0)
        lane_ids = [(TILES * sub_id + t).astype(F32).astype(BF16) for t in range(TILES)]
        highs, lows = [], []
        for s in range(sources):
            tile = got_ref[s]
            places, mass = tile[0:4], tile[4:8]
            floored = jnp.floor(places)
            fraction = places - floored
            pixel = floored.astype(jnp.int32) & (CYCLE_LEN - 1)
            high = (pixel >> 7).astype(F32)
            low = (pixel & (LANES - 1)).astype(F32)
            near = 1.0 - fraction
            for r in range(4):
                highs.append(
                    jnp.where(spread_row(high, r, ROWS) == row_id, spread_row(mass, r, ROWS), zero)
                )
                low_r, near_r, far_r = (spread_row(v, r, SUB) for v in (low, near, fraction))
                hits = [low_r == lane_id for lane_id in lane_ids]
                tiles = [jnp.where(hits[0], near_r, zero)]
                for t in range(1, TILES):
                    tiles.append(jnp.where(hits[t], near_r, jnp.where(hits[t - 1], far_r, zero)))
                tiles.append(jnp.where(hits[-1], far_r, zero))
                lows.append(jnp.concatenate(tiles, axis=0))
        return lax.dot_general(
            jnp.concatenate(highs, axis=1),
            jnp.concatenate(lows, axis=1),
            NT,
            preferred_element_type=F32,
        )

    acc_ref[:, LANES:] = jnp.zeros((ROWS, LANES), F32)
    acc_ref[:, :COLUMNS] = deposit()


def spectrum_kernel(
    acc_ref,
    order_ref,
    places_ref,
    one_h_ref,
    one_l_ref,
    cos_ref,
    sin_ref,
    two_h_ref,
    two_l_ref,
    out_ref,
    side_ref,
    block=None,
):
    if block is None:
        block = lax.axis_index(("x", "core", "z_hi", "z_lo", "y"))
    cycles = places_ref.shape[1]
    row = lax.broadcasted_iota(jnp.int32, (cycles, cycles), 0)
    column = lax.broadcasted_iota(jnp.int32, (cycles, cycles), 1)
    half = cycles // 2
    taken = jnp.where(row == 2 * (column % half) + column // half, 1.0, 0.0).astype(BF16)
    places = jnp.broadcast_to(places_ref[...], (16, cycles)).astype(F32).astype(BF16)
    places = lax.dot_general(places, taken, NN, preferred_element_type=F32)[:8].astype(jnp.int32)
    own = jnp.broadcast_to(order_ref[pl.ds(block // 4, 1), :], side_ref.shape)
    own = pltpu.roll(own, lax.rem(LANES + cycles - lax.rem(block, 4) * 32, LANES), 1)
    side_lane = lax.broadcasted_iota(jnp.int32, side_ref.shape, 1)
    side_ref[...] = jnp.where(side_lane < cycles, jnp.concatenate([places, places], axis=1), own)

    beyond = acc_ref[:, LANES:]
    column = lax.broadcasted_iota(jnp.int32, (ROWS, LANES), 1)
    next_row = pltpu.roll(pltpu.roll(beyond, LANES - SUB + 1, 1), 1, 0)
    cycle = acc_ref[:, :LANES] + jnp.where(
        column == 0, next_row, jnp.where(column < SUB, pltpu.roll(beyond, 1, 1), 0.0)
    )

    def dot(a, b, dims):
        return lax.dot_general(a, b, dims, preferred_element_type=F32)

    cycle_h, cycle_l = split(cycle)
    both = dot(one_h_ref[...], jnp.concatenate([cycle_h, cycle_l], axis=1), NN)
    first = both[:, :LANES] + (both[:, LANES:] + dot(one_l_ref[...], cycle_h, NN))
    real, imag = first[:ROWS], first[ROWS:]
    cos, sin = cos_ref[...], sin_ref[...]
    twisted = jnp.concatenate([real * cos + imag * sin, imag * cos - real * sin], axis=1)
    twisted_h, twisted_l = split(twisted)
    spectrum = (
        dot(two_h_ref[...], twisted_l, NT)
        + dot(two_l_ref[...], twisted_h, NT)
        + dot(two_h_ref[...], twisted_h, NT)
    )
    spectrum = spectrum.astype(BF16)
    zero, one = jnp.zeros((), BF16), jnp.ones((), BF16)
    ids = row_ids(ROWS)
    upper_ids = lax.broadcasted_iota(jnp.int32, (UPPER, LANES), 0)
    planes = out_ref.shape[0]
    for k in range(planes):
        orders = order_ref[pl.ds(k, 8, stride=planes), :]
        lower = (orders & (ROWS - 1)).astype(F32)
        upper = orders >> 8
        hits = [jnp.where(spread_row(lower, r, ROWS) == ids, one, zero) for r in range(8)]
        picked = dot(spectrum, jnp.concatenate(hits, axis=1), NN)
        reals, imags = [], []
        for r in range(8):
            cols = slice(r * LANES, (r + 1) * LANES)
            mine = jnp.broadcast_to(upper[r : r + 1, :], (UPPER, LANES)) == upper_ids
            reals.append(jnp.sum(jnp.where(mine, picked[:UPPER, cols], 0.0), axis=0, keepdims=True))
            imags.append(jnp.sum(jnp.where(mine, picked[UPPER:, cols], 0.0), axis=0, keepdims=True))
        rows = reals[::2] + imags[::2] + reals[1::2] + imags[1::2]
        out_ref[(FIRST_ON_LINE - k) % planes] = jnp.concatenate(rows, axis=0).astype(BF16)


def slab_sum_kernel(parts_ref, out_ref):
    z_count = parts_ref.shape[0]
    quarter = lax.broadcasted_iota(jnp.int32, (4, LANES), 1) // 32
    for z_lo in range(2):
        total = parts_ref[z_lo].astype(F32)
        for z in range(z_lo + 2, z_count, 2):
            total = total + parts_ref[z].astype(F32)
        for y in range(4):
            row = jnp.zeros((4, LANES), F32)
            for n in range(4):
                shift = (n - y) % 4 * 32
                values = pltpu.roll(total, shift, 1) if shift else total
                row = jnp.where(quarter == n, values[4 * n : 4 * n + 4], row)
            for x in range(4):
                chip = (4 * y + x - FIRST_IN_PLANE) % 16
                out_ref[pl.ds(2 * chip + z_lo, 1), :] = row[x : x + 1]


def product_kernel(got_ref, side_ref, legendre_ref, out_ref):
    modes, cycles, width = legendre_ref.shape
    rows = 2 * modes
    before = FIRST_IN_PLANE
    got = []
    for z_lo in range(2):
        got.append(got_ref[pl.ds(2 * (16 - before) + z_lo, before, stride=2), :])
        got.append(got_ref[pl.ds(z_lo, 16 - before, stride=2), :])
    got = jnp.concatenate(got, axis=0)
    turned = jnp.transpose(got)
    turned = jnp.concatenate([turned[:rows], turned[rows:]], axis=1).astype(BF16)
    place = lax.broadcasted_iota(jnp.int32, (cycles, cycles), 0) == jnp.broadcast_to(
        side_ref[:1, :cycles], (cycles, cycles)
    )
    sky = lax.dot_general(
        turned, jnp.where(place, 1.0, 0.0).astype(BF16), NT, preferred_element_type=F32
    )
    sky = jnp.concatenate([sky, sky], axis=1)
    lane = lax.broadcasted_iota(jnp.int32, (rows, 2 * cycles), 1)
    mode = lax.broadcasted_iota(jnp.int32, (rows, 2 * cycles), 0) & (modes - 1)
    owner = jnp.where(lane < cycles, 0, 1)
    blocks = [
        jnp.where(mode == owner + 2 * t, sky, 0.0).astype(BF16) for t in range(modes // 2)
    ]
    table = legendre_ref[...].reshape(modes * cycles, width)
    product = lax.dot_general(
        jnp.concatenate(blocks, axis=1), table, NN, preferred_element_type=F32
    )
    row_mode = lax.broadcasted_iota(jnp.int32, (rows, LANES), 0) & (modes - 1)
    column = lax.broadcasted_iota(jnp.int32, (rows, LANES), 1) - cycles
    order = jnp.sum(
        jnp.where(row_mode == column, jnp.broadcast_to(side_ref[:1, :], (rows, LANES)), 0).astype(F32),
        axis=1,
        keepdims=True,
    )
    degree = (LMAX - LW + 1 + lax.broadcasted_iota(jnp.int32, (rows, width), 1)).astype(F32)
    product = jnp.where(degree >= order, product, 0.0)
    out_ref[pl.ds(0, modes, stride=2), :] = product[:modes]
    out_ref[pl.ds(1, modes, stride=2), :] = product[modes:]


def kernel_call(kernel, out_shape, dtype=F32, scratch=(), limit=32, **options):
    return pl.pallas_call(
        kernel,
        out_shape=jax.ShapeDtypeStruct(out_shape, dtype) if dtype else out_shape,
        scratch_shapes=list(scratch),
        compiler_params=pltpu.CompilerParams(vmem_limit_bytes=limit * 1024 * 1024),
        **options,
    )


def pack_call(owners, capacity):
    return kernel_call(
        pack_kernel,
        (owners * 8, LANES),
        scratch=[
            pltpu.VMEM((owners, capacity), F32),
            pltpu.VMEM((owners, capacity), BF16),
            pltpu.VMEM((1, owners), jnp.int32),
            pltpu.SemaphoreType.DMA((5, 2)),
        ],
        limit=4,
        in_specs=[pl.BlockSpec(memory_space=pl.ANY)] * 3,
    )


def spectrum_call(planes, kernel=spectrum_kernel):
    outs = [
        jax.ShapeDtypeStruct((planes, 2 * M // planes // LANES, LANES), BF16),
        jax.ShapeDtypeStruct((8, LANES), jnp.int32),
    ]
    return kernel_call(kernel, outs, None)


def members_from(first, count):
    return [(first + n) % count for n in range(count)]


def exchange(values, axes, members):
    return lax.all_to_all(
        values, axes, split_axis=0, concat_axis=0, axis_index_groups=[members], tiled=True
    )


def local(positions, masses, send_counts, legendre, cycle_order, m_order):
    z = ("z_hi", "z_lo")
    cycles = cycle_order.shape[0]
    planes = lax.axis_size(z)
    capacity = positions.shape[-1]
    mode_count = legendre.shape[0]
    order_rows = m_order.reshape(M // LANES, LANES)
    particles = (
        positions.reshape(cycles, capacity),
        masses.reshape(cycles, capacity),
        send_counts.reshape(1, cycles),
    )
    packed = pack_call(cycles, capacity)(
        *(pltpu.with_memory_space_constraint(value, pltpu.HBM) for value in particles)
    )
    got = exchange(packed.reshape(cycles, 8, LANES), ("z_lo", "y", "x", "core"), members_from(FIRST_IN_BLOCK, cycles))
    cycle = kernel_call(
        deposit_kernel,
        (ROWS, 2 * LANES),
        cost_estimate=pl.CostEstimate(
            flops=2 * cycles * capacity * ROWS * 2 * LANES, transcendentals=0, bytes_accessed=2**19
        ),
    )(got)
    parts, side = spectrum_call(planes)(
        cycle, order_rows, cycle_order.reshape(1, cycles), *tables()
    )
    parts = parts.reshape(2 * planes, M // planes // LANES, LANES)
    line = [(FIRST_ON_LINE - n) % planes * 2 + core for n in range(planes) for core in range(2)]
    got_parts = exchange(parts, z + ("core",), line)
    own = kernel_call(slab_sum_kernel, (cycles // 2, LANES), limit=4)(
        got_parts.reshape(planes, 2 * M // planes // LANES, LANES)
    )
    spread = exchange(own.reshape(cycles // 4, 2, LANES), ("y", "x"), members_from(FIRST_IN_PLANE, cycles // 4))
    alm = kernel_call(product_kernel, (2 * mode_count, LW), limit=8)(
        spread.reshape(cycles // 2, LANES), side, legendre
    )
    return alm.reshape(mode_count, 2, LW)


def solution(mesh):
    cut = jax.sharding.Mesh(
        mesh.devices.reshape(8, 2, 4, 4, 2), ("z_hi", "z_lo", "y", "x", "core")
    )
    blk, pslab = ("z_hi", "z_lo", "y"), ("x", "core")
    placed = (
        P(blk, pslab, None, None),
        P(blk, pslab, None, None),
        P(blk, pslab, None),
        P(pslab + blk, None, None),
        P(),
        P(),
    )
    return jax.shard_map(
        local,
        mesh=cut,
        in_specs=placed,
        out_specs=P(pslab + blk, None, None),
        check_vma=False,
    )
```

```python
import math

import jax
import jax.numpy as jnp
import numpy as np
from jax import lax
from jax.experimental import pallas as pl
from jax.experimental.pallas import tpu as pltpu
from jax.sharding import PartitionSpec as P

CYCLE_LEN = 32768
M = 16384
LMAX = 16384
LW = 128

LANES = 128
ROWS = CYCLE_LEN // LANES
UPPER = M // ROWS
TILES = 8
SUB = LANES // TILES
COLUMNS = (TILES + 1) * SUB

FIRST_IN_BLOCK = 20
FIRST_ON_LINE = 10
FIRST_IN_PLANE = 10

F32 = jnp.float32
BF16 = jnp.bfloat16

NT = (((1,), (1,)), ((), ()))
NN = (((1,), (0,)), ((), ()))


def halves(table):
    high = table.astype(jnp.bfloat16)
    low = (table - high.astype(np.float64)).astype(jnp.bfloat16)
    return high, low


def split(values):
    high = values.astype(BF16)
    low = (values - high.astype(F32)).astype(BF16)
    return high, low


def tables():
    two_pi = 2.0 * math.pi
    rows = np.arange(ROWS)
    lanes = np.arange(LANES)
    lanes = TILES * (lanes % SUB) + lanes // SUB
    upper = np.arange(UPPER)
    angle_one = (rows[:, None] * rows[None, :] % ROWS) * (two_pi / ROWS)
    one = np.concatenate([np.cos(angle_one), -np.sin(angle_one)], axis=0)
    twist = (rows[:, None] * lanes[None, :] % CYCLE_LEN) * (two_pi / CYCLE_LEN)
    angle_two = (upper[:, None] * lanes[None, :] % LANES) * (two_pi / LANES)
    cos_two, sin_two = np.cos(angle_two), np.sin(angle_two)
    two = np.concatenate(
        [
            np.concatenate([cos_two, sin_two], axis=1),
            np.concatenate([-sin_two, cos_two], axis=1),
        ],
        axis=0,
    ) * (CYCLE_LEN ** -0.5)
    return (
        *halves(one),
        np.cos(twist).astype(np.float32),
        np.sin(twist).astype(np.float32),
        *halves(two),
    )


def spread_row(values, row, count):
    tile = jnp.broadcast_to(values[row : row + 1, :], (16, LANES)).astype(BF16)
    return jnp.concatenate([tile] * (count // 16), axis=0)


def row_ids(count):
    return lax.broadcasted_iota(jnp.int32, (count, LANES), 0).astype(F32).astype(BF16)


def pack_kernel(positions_hbm, masses_hbm, counts_hbm, out_ref, positions_ref, masses_ref, counts_ref, sems):
    owners, capacity = positions_ref.shape
    rows = 16
    chunks = owners // rows
    copies = []
    for n in range(chunks):
        part = pl.ds(n * rows, rows)
        copies.append(
            (
                pltpu.make_async_copy(positions_hbm.at[part, :], positions_ref.at[part, :], sems.at[n, 0]),
                pltpu.make_async_copy(masses_hbm.at[part, :], masses_ref.at[part, :], sems.at[n, 1]),
            )
        )
    counts_copy = pltpu.make_async_copy(counts_hbm, counts_ref, sems.at[chunks, 0])
    counts_copy.start()
    for pair in copies:
        for copy in pair:
            copy.start()
    counts_copy.wait()
    row = lax.broadcasted_iota(jnp.int32, (owners, owners), 0)
    column = lax.broadcasted_iota(jnp.int32, (owners, owners), 1)
    turned = jnp.where(row == column, jnp.broadcast_to(counts_ref[...], (owners, owners)), 0)
    counts = jnp.sum(turned.astype(F32), axis=1, keepdims=True).astype(jnp.int32)
    slots = lax.broadcasted_iota(jnp.int32, (rows, LANES), 1)
    for n in range(chunks):
        first = n * rows
        cut = min(max(FIRST_IN_BLOCK - first, 0), rows)
        pieces = [(a, b) for a, b in ((0, cut), (cut, rows)) if b > a]
        for copy in copies[n]:
            copy.wait()
        for j in range(capacity // LANES):
            cols = slice(j * LANES, (j + 1) * LANES)
            places = positions_ref[first : first + rows, cols]
            live = slots + j * LANES < counts[first : first + rows]
            weights = jnp.where(live, masses_ref[first : first + rows, cols].astype(F32), 0.0)
            for a, b in pieces:
                base = 8 * ((first + a - FIRST_IN_BLOCK) % owners)
                out_ref[pl.ds(base + j, b - a, stride=8), :] = places[a:b]
                out_ref[pl.ds(base + 4 + j, b - a, stride=8), :] = weights[a:b]


def deposit_kernel(got_ref, acc_ref):
    sources = got_ref.shape[0]
    zero = jnp.zeros((), BF16)

    def deposit():
        row_id = row_ids(ROWS)
        sub_id = lax.broadcasted_iota(jnp.int32, (SUB, LANES), 0)
        lane_ids = [(TILES * sub_id + t).astype(F32).astype(BF16) for t in range(TILES)]
        highs, lows = [], []
        for s in range(sources):
            tile = got_ref[s]
            places, mass = tile[0:4], tile[4:8]
            floored = jnp.floor(places)
            fraction = places - floored
            pixel = floored.astype(jnp.int32) & (CYCLE_LEN - 1)
            high = (pixel >> 7).astype(F32)
            low = (pixel & (LANES - 1)).astype(F32)
            near = 1.0 - fraction
            for r in range(4):
                highs.append(
                    jnp.where(spread_row(high, r, ROWS) == row_id, spread_row(mass, r, ROWS), zero)
                )
                low_r, near_r, far_r = (spread_row(v, r, SUB) for v in (low, near, fraction))
                hits = [low_r == lane_id for lane_id in lane_ids]
                tiles = [jnp.where(hits[0], near_r, zero)]
                for t in range(1, TILES):
                    tiles.append(jnp.where(hits[t], near_r, jnp.where(hits[t - 1], far_r, zero)))
                tiles.append(jnp.where(hits[-1], far_r, zero))
                lows.append(jnp.concatenate(tiles, axis=0))
        return lax.dot_general(
            jnp.concatenate(highs, axis=1),
            jnp.concatenate(lows, axis=1),
            NT,
            preferred_element_type=F32,
        )

    acc_ref[:, LANES:] = jnp.zeros((ROWS, LANES), F32)
    acc_ref[:, :COLUMNS] = deposit()


def spectrum_kernel(
    acc_ref,
    order_ref,
    places_hbm,
    one_h_ref,
    one_l_ref,
    cos_ref,
    sin_ref,
    two_h_ref,
    two_l_ref,
    out_ref,
    side_ref,
    places_ref,
    sems,
    block=None,
):
    if block is None:
        block = lax.axis_index(("x", "core", "z_hi", "z_lo", "y"))
    places_copy = pltpu.make_async_copy(places_hbm, places_ref, sems.at[0])
    places_copy.start()

    beyond = acc_ref[:, LANES:]
    column = lax.broadcasted_iota(jnp.int32, (ROWS, LANES), 1)
    next_row = pltpu.roll(pltpu.roll(beyond, LANES - SUB + 1, 1), 1, 0)
    cycle = acc_ref[:, :LANES] + jnp.where(
        column == 0, next_row, jnp.where(column < SUB, pltpu.roll(beyond, 1, 1), 0.0)
    )

    def dot(a, b, dims):
        return lax.dot_general(a, b, dims, preferred_element_type=F32)

    cycle_h, cycle_l = split(cycle)
    both = dot(one_h_ref[...], jnp.concatenate([cycle_h, cycle_l], axis=1), NN)
    first = both[:, :LANES] + (both[:, LANES:] + dot(one_l_ref[...], cycle_h, NN))
    real, imag = first[:ROWS], first[ROWS:]
    cos, sin = cos_ref[...], sin_ref[...]
    twisted = jnp.concatenate([real * cos + imag * sin, imag * cos - real * sin], axis=1)
    twisted_h, twisted_l = split(twisted)
    spectrum = (
        dot(two_h_ref[...], twisted_l, NT)
        + dot(two_l_ref[...], twisted_h, NT)
        + dot(two_h_ref[...], twisted_h, NT)
    )
    spectrum = spectrum.astype(BF16)
    zero, one = jnp.zeros((), BF16), jnp.ones((), BF16)
    ids = row_ids(ROWS)
    upper_ids = lax.broadcasted_iota(jnp.int32, (UPPER, LANES), 0)
    planes = out_ref.shape[0]
    for k in range(planes):
        orders = order_ref[pl.ds(k, 8, stride=planes), :]
        lower = (orders & (ROWS - 1)).astype(F32)
        upper = orders >> 8
        hits = [jnp.where(spread_row(lower, r, ROWS) == ids, one, zero) for r in range(8)]
        picked = dot(spectrum, jnp.concatenate(hits, axis=1), NN)
        reals, imags = [], []
        for r in range(8):
            cols = slice(r * LANES, (r + 1) * LANES)
            mine = jnp.broadcast_to(upper[r : r + 1, :], (UPPER, LANES)) == upper_ids
            reals.append(jnp.sum(jnp.where(mine, picked[:UPPER, cols], 0.0), axis=0, keepdims=True))
            imags.append(jnp.sum(jnp.where(mine, picked[UPPER:, cols], 0.0), axis=0, keepdims=True))
        rows = reals[::2] + imags[::2] + reals[1::2] + imags[1::2]
        out_ref[(FIRST_ON_LINE - k) % planes] = jnp.concatenate(rows, axis=0).astype(BF16)

    places_copy.wait()
    cycles = places_ref.shape[1]
    row = lax.broadcasted_iota(jnp.int32, (cycles, cycles), 0)
    column = lax.broadcasted_iota(jnp.int32, (cycles, cycles), 1)
    half = cycles // 2
    taken = jnp.where(row == 2 * (column % half) + column // half, 1.0, 0.0).astype(BF16)
    places = jnp.broadcast_to(places_ref[...], (16, cycles)).astype(F32).astype(BF16)
    places = lax.dot_general(places, taken, NN, preferred_element_type=F32)[:8].astype(jnp.int32)
    own = jnp.broadcast_to(order_ref[pl.ds(block // 4, 1), :], side_ref.shape)
    own = pltpu.roll(own, lax.rem(LANES + cycles - lax.rem(block, 4) * 32, LANES), 1)
    side_lane = lax.broadcasted_iota(jnp.int32, side_ref.shape, 1)
    side_ref[...] = jnp.where(side_lane < cycles, jnp.concatenate([places, places], axis=1), own)


def slab_sum_kernel(parts_ref, out_ref):
    z_count = parts_ref.shape[0]
    quarter = lax.broadcasted_iota(jnp.int32, (4, LANES), 1) // 32
    for z_lo in range(2):
        total = parts_ref[z_lo].astype(F32)
        for z in range(z_lo + 2, z_count, 2):
            total = total + parts_ref[z].astype(F32)
        for y in range(4):
            row = jnp.zeros((4, LANES), F32)
            for n in range(4):
                shift = (n - y) % 4 * 32
                values = pltpu.roll(total, shift, 1) if shift else total
                row = jnp.where(quarter == n, values[4 * n : 4 * n + 4], row)
            for x in range(4):
                chip = (4 * y + x - FIRST_IN_PLANE) % 16
                out_ref[pl.ds(2 * chip + z_lo, 1), :] = row[x : x + 1]


def product_kernel(got_ref, side_ref, legendre_ref, out_ref):
    modes, cycles, width = legendre_ref.shape
    rows = 2 * modes
    before = FIRST_IN_PLANE
    got = []
    for z_lo in range(2):
        got.append(got_ref[pl.ds(2 * (16 - before) + z_lo, before, stride=2), :])
        got.append(got_ref[pl.ds(z_lo, 16 - before, stride=2), :])
    got = jnp.concatenate(got, axis=0)
    turned = jnp.transpose(got)
    turned = jnp.concatenate([turned[:rows], turned[rows:]], axis=1).astype(BF16)
    place = lax.broadcasted_iota(jnp.int32, (cycles, cycles), 0) == jnp.broadcast_to(
        side_ref[:1, :cycles], (cycles, cycles)
    )
    sky = lax.dot_general(
        turned, jnp.where(place, 1.0, 0.0).astype(BF16), NT, preferred_element_type=F32
    )
    sky = jnp.concatenate([sky, sky], axis=1)
    lane = lax.broadcasted_iota(jnp.int32, (rows, 2 * cycles), 1)
    mode = lax.broadcasted_iota(jnp.int32, (rows, 2 * cycles), 0) & (modes - 1)
    owner = jnp.where(lane < cycles, 0, 1)
    blocks = [
        jnp.where(mode == owner + 2 * t, sky, 0.0).astype(BF16) for t in range(modes // 2)
    ]
    table = legendre_ref[...].reshape(modes * cycles, width)
    product = lax.dot_general(
        jnp.concatenate(blocks, axis=1), table, NN, preferred_element_type=F32
    )
    row_mode = lax.broadcasted_iota(jnp.int32, (rows, LANES), 0) & (modes - 1)
    column = lax.broadcasted_iota(jnp.int32, (rows, LANES), 1) - cycles
    order = jnp.sum(
        jnp.where(row_mode == column, jnp.broadcast_to(side_ref[:1, :], (rows, LANES)), 0).astype(F32),
        axis=1,
        keepdims=True,
    )
    degree = (LMAX - LW + 1 + lax.broadcasted_iota(jnp.int32, (rows, width), 1)).astype(F32)
    product = jnp.where(degree >= order, product, 0.0)
    out_ref[pl.ds(0, modes, stride=2), :] = product[:modes]
    out_ref[pl.ds(1, modes, stride=2), :] = product[modes:]


def kernel_call(kernel, out_shape, dtype=F32, scratch=(), limit=32, **options):
    return pl.pallas_call(
        kernel,
        out_shape=jax.ShapeDtypeStruct(out_shape, dtype) if dtype else out_shape,
        scratch_shapes=list(scratch),
        compiler_params=pltpu.CompilerParams(vmem_limit_bytes=limit * 1024 * 1024),
        **options,
    )


def pack_call(owners, capacity):
    return kernel_call(
        pack_kernel,
        (owners * 8, LANES),
        scratch=[
            pltpu.VMEM((owners, capacity), F32),
            pltpu.VMEM((owners, capacity), BF16),
            pltpu.VMEM((1, owners), jnp.int32),
            pltpu.SemaphoreType.DMA((5, 2)),
        ],
        limit=4,
        in_specs=[pl.BlockSpec(memory_space=pl.ANY)] * 3,
    )


def spectrum_call(planes, kernel=spectrum_kernel):
    outs = [
        jax.ShapeDtypeStruct((planes, 2 * M // planes // LANES, LANES), BF16),
        jax.ShapeDtypeStruct((8, LANES), jnp.int32),
    ]
    whole, in_hbm = pl.BlockSpec(), pl.BlockSpec(memory_space=pl.ANY)
    return kernel_call(
        kernel,
        outs,
        None,
        scratch=[pltpu.VMEM((1, 64), jnp.int32), pltpu.SemaphoreType.DMA((1,))],
        in_specs=[whole, whole, in_hbm] + [whole] * 6,
    )


def members_from(first, count):
    return [(first + n) % count for n in range(count)]


def exchange(values, axes, members):
    return lax.all_to_all(
        values, axes, split_axis=0, concat_axis=0, axis_index_groups=[members], tiled=True
    )


def local(positions, masses, send_counts, legendre, cycle_order, m_order):
    z = ("z_hi", "z_lo")
    cycles = cycle_order.shape[0]
    planes = lax.axis_size(z)
    capacity = positions.shape[-1]
    mode_count = legendre.shape[0]
    order_rows = m_order.reshape(M // LANES, LANES)
    particles = (
        positions.reshape(cycles, capacity),
        masses.reshape(cycles, capacity),
        send_counts.reshape(1, cycles),
    )
    packed = pack_call(cycles, capacity)(
        *(pltpu.with_memory_space_constraint(value, pltpu.HBM) for value in particles)
    )
    got = exchange(packed.reshape(cycles, 8, LANES), ("z_lo", "y", "x", "core"), members_from(FIRST_IN_BLOCK, cycles))
    cycle = kernel_call(
        deposit_kernel,
        (ROWS, 2 * LANES),
        cost_estimate=pl.CostEstimate(
            flops=2 * cycles * capacity * ROWS * 2 * LANES, transcendentals=0, bytes_accessed=2**19
        ),
    )(got)
    parts, side = spectrum_call(planes)(
        cycle,
        order_rows,
        pltpu.with_memory_space_constraint(cycle_order.reshape(1, cycles), pltpu.HBM),
        *tables(),
    )
    parts = parts.reshape(2 * planes, M // planes // LANES, LANES)
    line = [(FIRST_ON_LINE - n) % planes * 2 + core for n in range(planes) for core in range(2)]
    got_parts = exchange(parts, z + ("core",), line)
    own = kernel_call(slab_sum_kernel, (cycles // 2, LANES), limit=4)(
        got_parts.reshape(planes, 2 * M // planes // LANES, LANES)
    )
    spread = exchange(own.reshape(cycles // 4, 2, LANES), ("y", "x"), members_from(FIRST_IN_PLANE, cycles // 4))
    alm = kernel_call(product_kernel, (2 * mode_count, LW), limit=8)(
        spread.reshape(cycles // 2, LANES), side, legendre
    )
    return alm.reshape(mode_count, 2, LW)


def solution(mesh):
    cut = jax.sharding.Mesh(
        mesh.devices.reshape(8, 2, 4, 4, 2), ("z_hi", "z_lo", "y", "x", "core")
    )
    blk, pslab = ("z_hi", "z_lo", "y"), ("x", "core")
    placed = (
        P(blk, pslab, None, None),
        P(blk, pslab, None, None),
        P(blk, pslab, None),
        P(pslab + blk, None, None),
        P(),
        P(),
    )
    return jax.shard_map(
        local,
        mesh=cut,
        in_specs=placed,
        out_specs=P(pslab + blk, None, None),
        check_vma=False,
    )
```
